32 devices in a mesh: rep: 8 (over z, y), shard: 4 (over x, core).
Axes of the slice: x: 2, y: 2, z: 4, core: 2. Of those that a mesh axis runs over, the one named last changes fastest.
Arguments:
- inputs: bfloat16 [65536, 768], P(('rep', 'shard')), may hold values from -6 to 6
- earlier: bfloat16 [4, 65536, 768], P(None, ('rep', 'shard')), may hold values from -6 to 6
- segments: int32 [64, 1024], P(('rep', 'shard')), may hold values from 0 to 31, never falling along the last dimension, each value on 1 to 512 neighbouring positions
- cotangent: bfloat16 [65536, 768], P(('rep', 'shard')), may hold values from -6 to 6
- mix_weights: float32 [5], replicated, may hold values from 0.2 to 1
- ln1_gain: bfloat16 [768], P('shard'), may hold values from 0.25 to 1.75
- ln1_bias: bfloat16 [768], P('shard'), may hold values from -1.75 to 1.75
- qkv_weight: bfloat16 [768, 2304], P('shard'), may hold values from -0.21875 to 0.21875
- qkv_bias: bfloat16 [2304], P('shard'), may hold values from -1.75 to 1.75
- out_weight: bfloat16 [768, 768], P('shard'), may hold values from -0.875 to 0.875
- out_bias: bfloat16 [768], P('shard'), may hold values from -1.75 to 1.75
- ln2_gain: bfloat16 [768], P('shard'), may hold values from 0.25 to 1.75
- ln2_bias: bfloat16 [768], P('shard'), may hold values from -1.75 to 1.75
- up_weight: bfloat16 [768, 3072], P('shard'), may hold values from -0.21875 to 0.21875
- up_bias: bfloat16 [3072], P('shard'), may hold values from -1.75 to 1.75
- down_weight: bfloat16 [3072, 768], P('shard'), may hold values from -0.109375 to 0.109375
- down_bias: bfloat16 [768], P('shard'), may hold values from -1.75 to 1.75
Outputs:
- output: bfloat16 [65536, 768], P(('rep', 'shard'))
- input_grad: float32 [65536, 768], P(('rep', 'shard'))
- earlier_grad: float32 [4, 65536, 768], P(None, ('rep', 'shard'))
- mix_grad: float32 [5], replicated
- grad_ln1_gain: float32 [768], P('shard')
- grad_ln1_bias: float32 [768], P('shard')
- grad_qkv_weight: float32 [768, 2304], P('shard')
- grad_qkv_bias: float32 [2304], P('shard')
- grad_out_weight: float32 [768, 768], P('shard')
- grad_out_bias: float32 [768], P('shard')
- grad_ln2_gain: float32 [768], P('shard')
- grad_ln2_bias: float32 [768], P('shard')
- grad_up_weight: float32 [768, 3072], P('shard')
- grad_up_bias: float32 [3072], P('shard')
- grad_down_weight: float32 [3072, 768], P('shard')
- grad_down_bias: float32 [768], P('shard')
The draws below stay inside these ranges and needn't reach their ends.
Inputs may be any that keep to these rules, and one draw needn't show every extreme that they name: `segments`: document numbers never fall along a sequence; each of the 32 documents of a sequence holds 1 to 512 tokens, and one of them exactly 512.
All inputs are finite; a program needn't handle non-finite values.
Results may differ from the reference program's by a relative error of at most 0.0092.
Values may be sent and summed in bfloat16 or wider, within the bound.
No kernel may reach another device: no remote copies, remote signals or barrier semaphores. Data moves between devices by JAX's collectives and lax.ppermute only.
A program may use at most 384 MiB of HBM per device.

```python
import math
import jax
import jax.numpy as jnp
import numpy as np
from jax import lax

D = 768
HEADS = 12
HEAD = 64
FF = 3072
SEQ_LEN = 1024
DOCS = 32
DOC_MOST = 512
SEQUENCES = 64
TOKENS = 65536


def levels(stream_key, extent, cuts, smallest, largest):
    level, own = 1.0, jax.random.fold_in(stream_key, 6)
    for dim, shards_of in cuts:
        draws = jnp.exp(jax.random.uniform(jax.random.fold_in(own, dim), (shards_of,), jnp.float32, smallest / len(cuts), largest / len(cuts)))
        level = level * jnp.repeat(draws, extent[dim] // shards_of).reshape([-1 if axis == dim else 1 for axis in range(len(extent))])
    return level


def profile(amount, total, most, skew):
    loads = [(1 << 20) // math.isqrt(standing ** skew) + 1 for standing in range(2, amount + 1)]
    rest, holding = total - most - (amount - 1), [1] * (amount - 1)
    while rest > 0:
        free = [i for i in range(amount - 1) if holding[i] < most]
        whole, budget = sum([loads[i] for i in free]), rest
        for i in free:
            extra = min(most - holding[i], max(1, budget * loads[i] // whole), rest)
            holding[i] = holding[i] + extra
            rest = rest - extra
    return np.array([most] + holding)


def uneven_parts(rng, amount, total, limit, skew):
    if amount == 2:
        one = jax.random.randint(rng, (), max(1, total - limit), min(limit, total - 1) + 1)
        return jnp.stack([one, total - one])
    lengths = jnp.asarray(profile(amount, total, limit, skew), jnp.int32)
    twos = (amount - 1) // 2
    source_of, receiver = lengths[1:1 + 2 * twos:2], lengths[2:2 + 2 * twos:2]
    slack = jnp.minimum(source_of - 1, limit - receiver)
    shifted = jax.random.randint(jax.random.fold_in(rng, 1), (twos,), 0, 1 << 20) % (slack + 1)
    lengths = lengths.at[1:1 + 2 * twos:2].set(source_of - shifted).at[2:2 + 2 * twos:2].set(receiver + shifted)
    return lengths[jax.random.permutation(jax.random.fold_in(rng, 2), amount)]


def normal_values(rng, dims, spread, most, split=(), held_as=jnp.bfloat16):
    loudness = levels(rng, dims, split, -0.22, 0.18) if split else 1.0
    entries = jax.random.normal(rng, dims, jnp.float32) * spread * loudness
    return jnp.minimum(jnp.maximum(entries, -most), most).astype(held_as)


def setup_inputs(seed: int = 0) -> dict:
    key_list = jax.random.split(jax.random.key(seed), 18)
    return {
        "inputs": normal_values(key_list[0], (TOKENS, D), 1.0, 6.0, ((0, 32),)),
        "earlier": normal_values(key_list[1], (4, TOKENS, D), 1.0, 6.0, ((1, 32),)),
        "segments": jax.vmap(lambda own: jnp.searchsorted(jnp.cumsum(uneven_parts(own, DOCS, SEQ_LEN, DOC_MOST, 2)), jnp.arange(SEQ_LEN), side="right"))(jax.random.split(key_list[2], SEQUENCES)).reshape((SEQUENCES, SEQ_LEN)).astype(jnp.int32),
        "cotangent": normal_values(key_list[3], (TOKENS, D), 1.0, 6.0, ((0, 32),)),
        "mix_weights": jnp.clip(jax.random.uniform(key_list[4], (5,), jnp.float32, 0.2, 1.0), 0.2, 1.0),
        "ln1_gain": jnp.clip(1.0 + 0.15 * jax.random.normal(key_list[5], (D,), jnp.float32), 0.25, 1.75).astype(jnp.bfloat16),
        "ln1_bias": normal_values(key_list[6], (D,), 0.3, 1.75, ((0, 4),)),
        "qkv_weight": normal_values(key_list[7], (D, 3 * D), D ** -0.5, 0.21875, ((0, 4),)),
        "qkv_bias": normal_values(key_list[8], (3 * D,), 0.3, 1.75, ((0, 4),)),
        "out_weight": normal_values(key_list[9], (D, D), (D // 16) ** -0.5, 0.875, ((0, 4),)),
        "out_bias": normal_values(key_list[10], (D,), 0.3, 1.75, ((0, 4),)),
        "ln2_gain": jnp.clip(1.0 + 0.15 * jax.random.normal(key_list[11], (D,), jnp.float32), 0.25, 1.75).astype(jnp.bfloat16),
        "ln2_bias": normal_values(key_list[12], (D,), 0.3, 1.75, ((0, 4),)),
        "up_weight": normal_values(key_list[13], (D, FF), D ** -0.5, 0.21875, ((0, 4),)),
        "up_bias": normal_values(key_list[14], (FF,), 0.3, 1.75, ((0, 4),)),
        "down_weight": normal_values(key_list[15], (FF, D), FF ** -0.5, 0.109375, ((0, 4),)),
        "down_bias": normal_values(key_list[16], (D,), 0.3, 1.75, ((0, 4),)),
    }


epsilon = 1e-05
highest = lax.Precision.HIGHEST

@jax.custom_vjp
def low(v):
    return lax.optimization_barrier(v.astype(jnp.bfloat16)).astype(jnp.float32)

@jax.custom_vjp
def low_back(v):
    return v

def low_keep(v):
    return (low(v), None)

def low_pass(kept, grad):
    return (grad,)

def back_keep(v):
    return (v, None)

def back_low(kept, grad):
    return (low(grad),)
low.defvjp(low_keep, low_pass)
low_back.defvjp(back_keep, back_low)

def rope_tables(length, half_size):
    inv_freq = jnp.exp(jnp.arange(half_size, dtype=jnp.float32) * (-math.log(10000.0) / half_size))
    angles = jnp.arange(length, dtype=jnp.float32)[:, None] * inv_freq[None, :]
    return (jnp.cos(angles), jnp.sin(angles))

def rotate(tensor, cosine_table, sine_table):
    half_size = tensor.shape[-1] // 2
    first_half = tensor[..., :half_size]
    second_half = tensor[..., half_size:]
    cos_part = cosine_table[:, None, :]
    sin_part = sine_table[:, None, :]
    return jnp.concatenate([first_half * cos_part - second_half * sin_part, second_half * cos_part + first_half * sin_part], axis=-1)

def layer_norm(values, gain, bias):
    row_mean = lax.optimization_barrier(jnp.mean(values, axis=-1, keepdims=True))
    centred = values - row_mean
    row_var = lax.optimization_barrier(jnp.mean(centred * centred, axis=-1, keepdims=True))
    return centred * lax.rsqrt(row_var + epsilon) * gain + bias

def attend(queries, key_rows, value_rows, doc_ids):
    raw_scores = low_back(jnp.einsum('qhd,khd->hqk', queries, key_rows, precision=highest))
    length = queries.shape[0]
    positions = jnp.arange(length)
    allowed = (positions[:, None] >= positions[None, :]) & (doc_ids[:, None] == doc_ids[None, :])
    scores = jnp.where(allowed[None], raw_scores * queries.shape[-1] ** (-0.5), -1e+30)
    attn_probs = low(jax.nn.softmax(scores, axis=-1))
    return low(low_back(jnp.einsum('hqk,khd->qhd', attn_probs, value_rows, precision=highest)))

def block_forward(params, block_in, states, mix_alpha, doc_ids):
    gain_one, bias_one, w_qkv, b_qkv, w_out, b_out, gain_two, bias_two, w_up, b_up, w_down, b_down = params
    group_size, length = doc_ids.shape
    model_width = block_in.shape[1]
    act_one = low(layer_norm(block_in, gain_one, bias_one))
    qkv_rows = low_back(jnp.dot(act_one, w_qkv, precision=highest)) + b_qkv
    qkv_rows = qkv_rows.reshape(group_size, length, 3, HEADS, HEAD)
    cosine_table, sine_table = rope_tables(length, HEAD // 2)
    queries = low(rotate(qkv_rows[:, :, 0], cosine_table, sine_table))
    key_rows = low(rotate(qkv_rows[:, :, 1], cosine_table, sine_table))
    value_rows = low(qkv_rows[:, :, 2])
    attended = lax.map(jax.checkpoint(lambda group_item: attend(*group_item)), (queries, key_rows, value_rows, doc_ids))
    attended = attended.reshape(group_size * length, model_width)
    hidden_one = block_in + low_back(jnp.dot(attended, w_out, precision=highest)) + b_out
    act_two = low(layer_norm(hidden_one, gain_two, bias_two))
    pre_act = low_back(jnp.dot(act_two, w_up, precision=highest)) + b_up
    act_three = low(jax.nn.gelu(pre_act, approximate=True))
    block_out = hidden_one + low_back(jnp.dot(act_three, w_down, precision=highest)) + b_down
    return mix_alpha[0] * states[0] + mix_alpha[1] * states[1] + mix_alpha[2] * states[2] + mix_alpha[3] * states[3] + mix_alpha[4] * block_out

def reference(inputs, earlier, segments, cotangent, mix_weights, ln1_gain, ln1_bias, qkv_weight, qkv_bias, out_weight, out_bias, ln2_gain, ln2_bias, up_weight, up_bias, down_weight, down_bias):
    params = (ln1_gain.astype(jnp.float32), ln1_bias.astype(jnp.float32), qkv_weight.astype(jnp.float32), qkv_bias.astype(jnp.float32), out_weight.astype(jnp.float32), out_bias.astype(jnp.float32), ln2_gain.astype(jnp.float32), ln2_bias.astype(jnp.float32), up_weight.astype(jnp.float32), up_bias.astype(jnp.float32), down_weight.astype(jnp.float32), down_bias.astype(jnp.float32))
    seq_total = segments.shape[0]
    group_size = math.gcd(max(1, 4096 // SEQ_LEN), seq_total)
    group_count = seq_total // group_size
    row_count = group_size * SEQ_LEN
    block_rows = inputs.astype(jnp.float32).reshape(group_count, row_count, D)
    state_rows = earlier.astype(jnp.float32).reshape(4, group_count, row_count, D).transpose(1, 0, 2, 3)
    cot_rows = cotangent.astype(jnp.float32).reshape(group_count, row_count, D)
    doc_rows = segments.reshape(group_count, group_size, SEQ_LEN)
    mix_alpha = mix_weights.astype(jnp.float32)

    def group_step(totals, group_item):
        rows_in, states_in, doc_group, cot_group = group_item
        mixed_rows, pull_back = jax.vjp(lambda params_in, rows_arg, states_arg, alpha_arg: block_forward(params_in, rows_arg, states_arg, alpha_arg, doc_group), params, rows_in, states_in, mix_alpha)
        grad_params, grad_rows, grad_states, grad_alpha = pull_back(cot_group)
        new_params = tuple((running + added for running, added in zip(totals[0], grad_params)))
        return ((new_params, totals[1] + grad_alpha), (mixed_rows.astype(jnp.bfloat16), grad_rows, grad_states))
    start = (tuple((jnp.zeros_like(piece_param) for piece_param in params)), jnp.zeros_like(mix_alpha))
    (param_grads, mix_grad), (mixed_all, grad_all, state_grads) = lax.scan(group_step, start, (block_rows, state_rows, doc_rows, cot_rows))
    output = mixed_all.reshape(TOKENS, D)
    input_grad = grad_all.reshape(TOKENS, D)
    earlier_grad = state_grads.transpose(1, 0, 2, 3).reshape(4, TOKENS, D)
    return (output, input_grad, earlier_grad, mix_grad, param_grads[0], param_grads[1], param_grads[2], param_grads[3], param_grads[4], param_grads[5], param_grads[6], param_grads[7], param_grads[8], param_grads[9], param_grads[10], param_grads[11])
```

```python
import math

import jax
import jax.numpy as jnp
from jax import lax
from jax.experimental import pallas as pl
from jax.experimental.pallas import tpu as pltpu
from jax.sharding import PartitionSpec as P

HEADS = 12
HEAD = 64
PAIR = 2 * HEAD
EPSILON = 1e-05
LOG2E = math.log2(math.e)
NEG = -1e30
GELU_A = math.sqrt(2.0 / math.pi)
GELU_B = GELU_A * 0.044715
BF = jnp.bfloat16
F32 = jnp.float32
MIB = 1 << 20
MLP_PARTS = 2


def dot_nn(a, b):
    return lax.dot_general(a, b, (((1,), (0,)), ((), ())), preferred_element_type=F32)


def dot_nt(a, b):
    return lax.dot_general(a, b, (((1,), (1,)), ((), ())), preferred_element_type=F32)


def dot_tn(a, b):
    return lax.dot_general(a, b, (((0,), (0,)), ((), ())), preferred_element_type=F32)


def dot_tt(a, b):
    return lax.dot_general(a, b, (((0,), (1,)), ((), ())), preferred_element_type=F32)


def params(vmem):
    return pltpu.CompilerParams(vmem_limit_bytes=vmem * MIB)


ANY = pl.BlockSpec(memory_space=pl.ANY)


def load_pieces(me, pieces, target, sems, start, cols=None):
    copies = []
    for j, piece in enumerate(pieces):
        rows = piece.shape[0]
        at = pl.multiple_of((me ^ j) * rows, rows)
        source = piece if cols is None else piece.at[:, cols]
        copies.append(pltpu.make_async_copy(source, target.at[pl.ds(at, rows), :], sems.at[j]))
    for copy in copies:
        if start:
            copy.start()
        else:
            copy.wait()


def load_some_pieces(me, pieces, target, sems, start, index, count):
    for j, piece in enumerate(pieces):
        rows = piece.shape[0]
        per = len(pieces) // count
        owner = me ^ j

        @pl.when(owner // per == index)
        def _(j=j, piece=piece, rows=rows, owner=owner):
            at = pl.multiple_of((owner - index * per) * rows, rows)
            copy = pltpu.make_async_copy(piece, target.at[pl.ds(at, rows), :], sems.at[j])
            if start:
                copy.start()
            else:
                copy.wait()


def whole(shape):
    zeros = (0,) * len(shape)
    return pl.BlockSpec(shape, lambda *_: zeros, pipeline_mode=pl.Buffered(1))


SMEM = pl.BlockSpec(memory_space=pltpu.SMEM)


def ring_shape(length, width):
    return pltpu.VMEM((width // 128, 2 * length, 128), F32)


def ring_put(ring, at, value):
    for j in range(ring.shape[0]):
        part = value[:, j * 128 : (j + 1) * 128]
        ring[j, at : at + value.shape[0]] = part
        twin = ring.shape[1] // 2 + at
        ring[j, twin : twin + value.shape[0]] = part


def ring_get(ring, start, rows):
    return jnp.concatenate([ring[j, pl.ds(start, rows), :] for j in range(ring.shape[0])], axis=1)


def norm_parts(v):
    mean = jnp.mean(v, axis=-1, keepdims=True)
    centred = v - mean
    var = jnp.mean(centred * centred, axis=-1, keepdims=True)
    r = lax.rsqrt(var + EPSILON)
    return centred * r, r


def qkv_kernel(
    me_ref, shift_ref, x_ref, cot_ref, gain_ref, bias_ref, wb_ref, cos_ref, sin_ref, *refs
):
    pieces, (xr_ref, cr_ref, act_ref, q_ref, k_ref, v_ref, ring, w_ref, sems) = refs[:-9], refs[-9:]
    length, width = x_ref.shape

    @pl.when(pl.program_id(0) == 0)
    def _():
        load_pieces(me_ref[0], pieces, w_ref, sems, True)

    shift = shift_ref[pl.program_id(0)]
    for source, target in ((cot_ref, cr_ref), (x_ref, xr_ref)):
        ring_put(ring, 0, source[...].astype(F32))
        target[...] = ring_get(ring, shift, length).astype(BF)
    n, _ = norm_parts(xr_ref[...].astype(F32))
    act_ref[...] = (n * gain_ref[...].astype(F32) + bias_ref[...].astype(F32)).astype(BF)
    half = HEAD // 2
    rows = 256

    @pl.when(pl.program_id(0) == 0)
    def _():
        load_pieces(me_ref[0], pieces, w_ref, sems, False)

    for part, out in enumerate((q_ref, k_ref, v_ref)):
        scale = LOG2E * HEAD**-0.5 if part == 0 else 1.0
        for base in range(0, width, rows):
            at = part * width + base
            cols = slice(at, at + rows)
            y = dot_tt(w_ref[:, cols], act_ref[...]) + wb_ref[cols, :]
            if part == 2:
                out[0, base : base + rows, :] = y.astype(BF)
                continue
            cos, sin = cos_ref[0], sin_ref[0]
            for h in range(0, rows, HEAD):
                u, w = y[h : h + half], y[h + half : h + HEAD]
                a, b = u * cos - w * sin, w * cos + u * sin
                if part == 0:
                    a, b = a * scale, b * scale
                out[0, base + h : base + h + half, :] = a.astype(BF)
                out[0, base + h + half : base + h + HEAD, :] = b.astype(BF)


def qkv_call(me, shift, x, cot, gain, bias, wb, cos, sin, pieces):
    tokens, width = x.shape
    nseq = shift.shape[0]
    length = tokens // nseq
    row = pl.BlockSpec((length, width), lambda s: (s, 0))
    col = pl.BlockSpec((1, width, length), lambda s: (s, 0, 0))
    tab = pl.BlockSpec((1, HEAD // 2, length), lambda s: (s, 0, 0))
    low = jax.ShapeDtypeStruct((tokens, width), BF)
    turned = jax.ShapeDtypeStruct((nseq, width, length), BF)
    return pl.pallas_call(
        qkv_kernel,
        grid=(nseq,),
        in_specs=[
            SMEM, SMEM, row, row, whole((1, width)), whole((1, width)), whole(wb.shape), tab, tab,
            *(ANY for _ in pieces),
        ],
        out_specs=[row, row, row, col, col, col],
        out_shape=[low, low, low, turned, turned, turned],
        scratch_shapes=[
            ring_shape(length, width),
            pltpu.VMEM((width, 3 * width), BF),
            pltpu.SemaphoreType.DMA((len(pieces),)),
        ],
        compiler_params=params(60),
        cost_estimate=pl.CostEstimate(
            flops=2 * tokens * width * 3 * width, bytes_accessed=20 * MIB, transcendentals=0
        ),
        name="qkv",
    )(me, shift, x, cot, gain, bias, wb, cos, sin, *pieces)


def fill_masks(segc_ref, segr_ref, mask, blk):
    kk = lax.broadcasted_iota(jnp.int32, (blk, blk), 0)
    qq = lax.broadcasted_iota(jnp.int32, (blk, blk), 1)
    causal = kk <= qq
    mask[0] = jnp.where(causal, 0.0, NEG)
    for i, (kb, qb) in enumerate(((0, 0), (0, 1), (1, 1))):
        same = segc_ref[0, pl.ds(kb * blk, blk), :] == segr_ref[0, :, pl.ds(qb * blk, blk)]
        keep = same if kb != qb else same & causal
        mask[1 + i] = jnp.where(keep, 0.0, NEG)


def scores_of(keys, query, mask, half, qb, blk):
    top = dot_nn(keys[: (qb + 1) * blk], query)
    if half == 0:
        diag = top[qb * blk :] + mask[0]
        return diag if qb == 0 else jnp.concatenate([top[:blk], diag], axis=0)
    if qb == 0:
        return top + mask[1]
    return jnp.concatenate([top[:blk] + mask[2], top[blk:] + mask[3]], axis=0)


def one_head(pair_rows, head):
    zero = jnp.zeros((HEAD, pair_rows.shape[1]), pair_rows.dtype)
    rows = pair_rows[head * HEAD : (head + 1) * HEAD]
    return jnp.concatenate([rows, zero] if head == 0 else [zero, rows], axis=0)


def attend_kernel(segc_ref, segr_ref, q_ref, k_ref, v_ref, o_ref, l_ref, mask):
    length = q_ref.shape[2]
    blk = length // 4

    @pl.when(pl.program_id(1) == 0)
    def _():
        fill_masks(segc_ref, segr_ref, mask, blk)

    for half in range(2):
        base = half * 2 * blk
        keys = k_ref[0, :, base : base + 2 * blk].T
        for head in range(2):
            hs = slice(head * HEAD, (head + 1) * HEAD)
            for qb in range(2):
                qs = slice(base + qb * blk, base + (qb + 1) * blk)
                s = scores_of(keys, one_head(q_ref[0, :, qs], head), mask, half, qb, blk)
                top = jnp.max(s, axis=0, keepdims=True)
                p = jnp.exp2(s - top)
                total = jnp.sum(p, axis=0, keepdims=True)
                o = dot_nn(v_ref[0, hs, base : base + (qb + 1) * blk], p.astype(BF))
                o_ref[0, hs, qs] = (o / total).astype(BF)
                l_ref[0, 0, head : head + 1, qs] = top + jnp.log2(total)


def attend_call(segc, segr, q, k, v):
    nseq, width, length = q.shape
    pairs = width // PAIR
    blk = length // 4
    blockspec = pl.BlockSpec((1, PAIR, length), lambda s, h: (s, h, 0))
    return pl.pallas_call(
        attend_kernel,
        grid=(nseq, pairs),
        in_specs=[
            pl.BlockSpec((1, 2 * blk, 1), lambda s, h: (s, 0, 0)),
            pl.BlockSpec((1, 1, 2 * blk), lambda s, h: (s, 0, 0)),
            blockspec, blockspec, blockspec,
        ],
        out_specs=[blockspec, pl.BlockSpec((1, 1, 2, length), lambda s, h: (s, h, 0, 0))],
        out_shape=[
            jax.ShapeDtypeStruct((nseq, width, length), BF),
            jax.ShapeDtypeStruct((nseq, pairs, 2, length), F32),
        ],
        scratch_shapes=[pltpu.VMEM((4, blk, blk), F32)],
        compiler_params=params(40),
        cost_estimate=pl.CostEstimate(
            flops=18 * nseq * 10**9, bytes_accessed=14 * MIB, transcendentals=0
        ),
        name="attend",
    )(segc, segr, q, k, v)


def attend_back_kernel(
    segc_ref, segr_ref, q_ref, k_ref, v_ref, o_ref, g_ref, l_ref, cos_ref, sin_ref,
    gq_ref, gk_ref, gv_ref, sum_ref, mask, turn,
):
    length = q_ref.shape[2]
    blk = length // 4
    hd = HEAD // 2

    @pl.when(pl.program_id(1) == 0)
    def _():
        fill_masks(segc_ref, segr_ref, mask, blk)

    for half in range(2):
        base = half * 2 * blk
        ks = slice(base, base + 2 * blk)
        keys = k_ref[0, :, ks].T
        values = v_ref[0, :, ks].T
        for head in range(2):
            hs = slice(head * HEAD, (head + 1) * HEAD)
            for qb in range(2):
                qs = slice(base + qb * blk, base + (qb + 1) * blk)
                span = slice(base, base + (qb + 1) * blk)
                g = g_ref[0, hs, qs]
                delta = jnp.sum(g.astype(F32) * o_ref[0, hs, qs].astype(F32), axis=0, keepdims=True)
                s = scores_of(keys, one_head(q_ref[0, :, qs], head), mask, half, qb, blk)
                p = jnp.exp2(s - l_ref[0, 0, head : head + 1, qs])
                gp = dot_nn(values[: (qb + 1) * blk], one_head(g_ref[0, :, qs], head))
                ds = (p * (gp - delta)).astype(BF)
                dv = dot_nt(g, p.astype(BF))
                dk = dot_nt(q_ref[0, hs, qs], ds)
                turn[0, hs, qs] = dot_nn(k_ref[0, hs, span], ds)
                if qb == 0:
                    held_k, held_v = dk, dv
                else:
                    turn[1, hs, base : base + blk] = dk[:, :blk] + held_k
                    turn[1, hs, base + blk : base + 2 * blk] = dk[:, blk:]
                    turn[2, hs, base : base + blk] = dv[:, :blk] + held_v
                    turn[2, hs, base + blk : base + 2 * blk] = dv[:, blk:]
    cos, sin = cos_ref[0], sin_ref[0]

    def lanes(v):
        total = v[:, :128]
        for at in range(128, length, 128):
            total = total + v[:, at : at + 128]
        return total

    for part, (out, scale) in enumerate(((gq_ref, HEAD**-0.5), (gk_ref, 1.0 / LOG2E), (gv_ref, 1.0))):
        for head in range(2):
            at = head * HEAD
            u = turn[part, at : at + hd]
            w = turn[part, at + hd : at + HEAD]
            if part < 2:
                u, w = (u * cos + w * sin) * scale, (w * cos - u * sin) * scale
            out[0, at : at + hd, :] = u.astype(BF)
            out[0, at + hd : at + HEAD, :] = w.astype(BF)
            sum_ref[0, part, at : at + hd] = lanes(u)
            sum_ref[0, part, at + hd : at + HEAD] = lanes(w)


def attend_back_call(segc, segr, q, k, v, o, g, lse, cos, sin):
    nseq, width, length = q.shape
    pairs = width // PAIR
    blk = length // 4
    blockspec = pl.BlockSpec((1, PAIR, length), lambda s, h: (s, h, 0))
    tab = pl.BlockSpec((1, HEAD // 2, length), lambda s, h: (s, 0, 0))
    turned = jax.ShapeDtypeStruct((nseq, width, length), BF)
    return pl.pallas_call(
        attend_back_kernel,
        grid=(nseq, pairs),
        in_specs=[
            pl.BlockSpec((1, 2 * blk, 1), lambda s, h: (s, 0, 0)),
            pl.BlockSpec((1, 1, 2 * blk), lambda s, h: (s, 0, 0)),
            blockspec, blockspec, blockspec, blockspec, blockspec,
            pl.BlockSpec((1, 1, 2, length), lambda s, h: (s, h, 0, 0)),
            tab, tab,
        ],
        out_specs=[
            blockspec, blockspec, blockspec,
            pl.BlockSpec((1, 3, PAIR, 128), lambda s, h: (s, 0, h, 0)),
        ],
        out_shape=[turned, turned, turned, jax.ShapeDtypeStruct((nseq, 3, width, 128), F32)],
        scratch_shapes=[pltpu.VMEM((4, blk, blk), F32), pltpu.VMEM((3, PAIR, length), F32)],
        compiler_params=params(48),
        cost_estimate=pl.CostEstimate(
            flops=30 * nseq * 10**9, bytes_accessed=30 * MIB, transcendentals=0
        ),
        name="attend_back",
    )(segc, segr, q, k, v, o, g, lse, cos, sin)


def mlp_kernel(index, count, names, members, *refs):
    ref = dict(zip(names, refs))
    first, last = index == 0, index == count - 1
    rows, width = ref["cot"].shape
    step = pl.program_id(0)
    span = ref["wu"].shape[1]

    def weights(start):
        me, sems = ref["me"][0], ref["sems"]
        if first or last:
            load_pieces(me, [ref["wo", j] for j in range(members)], ref["wo"], sems.at[0], start)
        cols = slice(index * span, (index + 1) * span)
        load_pieces(me, [ref["wu", j] for j in range(members)], ref["wu"], sems.at[1], start, cols)
        pieces = [ref["wd", j] for j in range(members)]
        load_some_pieces(me, pieces, ref["wd"], sems.at[2], start, index, count)

    @pl.when(step == 0)
    def _():
        weights(True)
        weights(False)

    final = pl.num_programs(0) - 1
    acc_u, acc_d, low = ref["acc_u"], ref["acc_d"], ref["low"]
    chunks, _, chunk = acc_u.shape
    alpha = ref["mix"][4]

    @pl.when(step == 0)
    def _():
        acc_u[...] = jnp.zeros_like(acc_u)
        acc_d[...] = jnp.zeros_like(acc_d)
        ref["dbu"][...] = jnp.zeros_like(ref["dbu"])

    cot = ref["cot"][...].astype(F32)
    g_out = cot * alpha
    low[...] = g_out.astype(BF)
    if first:
        hidden = ref["x"][...].astype(F32) + dot_tn(ref["a"][0], ref["wo"][...]) + ref["bo"][...].astype(F32)
        n, _ = norm_parts(hidden)
        ref["hid"][...] = hidden
        ref["act"][...] = (n * ref["gain"][...].astype(F32) + ref["bias"][...].astype(F32)).astype(BF)
        total_up = hidden + ref["bd"][...].astype(F32)
        total_back = None
    else:
        total_up, total_back = ref["up_in"][...], ref["back_in"][...]
    act2 = ref["act"]
    for f in range(chunks):
        cols = slice(f * chunk, (f + 1) * chunk)
        wu = ref["wu"][:, cols]
        wd = ref["wd"][cols, :]
        pre = dot_nn(act2[...], wu) + ref["bu"][:, cols].astype(F32)
        g_act = dot_nt(low[...], wd)
        square = pre * pre
        h = 0.5 + 0.5 * jnp.tanh(pre * (GELU_A + GELU_B * square))
        act = (pre * h).astype(BF)
        slope = h + (pre * (h * (1.0 - h))) * (2.0 * GELU_A + 6.0 * GELU_B * square)
        g_pre = g_act * slope
        ref["dbu"][:, cols] += jnp.sum(g_pre, axis=0, keepdims=True)
        g_low = g_pre.astype(BF)
        total_up = total_up + dot_nn(act, wd)
        more = dot_nt(g_low, wu)
        total_back = more if total_back is None else total_back + more
        acc_d[f] += dot_tn(act, low[...])
        acc_u[f] += dot_tn(act2[...], g_low)
    ref["up"][...] = total_up
    if not last:
        ref["back"][...] = total_back
    else:
        e = total_back
        gain = ref["gain"][...].astype(F32)
        n, r = norm_parts(ref["hid"][...])
        eg = e * gain
        part = r * (
            eg - jnp.mean(eg, axis=-1, keepdims=True) - n * jnp.mean(eg * n, axis=-1, keepdims=True)
        )
        g_hidden = g_out + part
        ref["gh"][...] = g_hidden
        g_low = g_hidden.astype(BF)

        @pl.when(step == 0)
        def _():
            ref["sum"][...] = jnp.zeros_like(ref["sum"])
            ref["acc_o"][...] = jnp.zeros_like(ref["acc_o"])

        for i, term in enumerate((e * n, e, g_hidden, g_out, total_up * cot)):
            ref["sum"][i : i + 1, :] += jnp.sum(term, axis=0, keepdims=True)
        ref["acc_o"][...] += dot_nn(ref["a"][0], g_low)
        ref["ga"][0] = dot_nt(ref["wo"][...], g_low).astype(BF)

    @pl.when(step == final)
    def _():
        for f in range(chunks):
            cols = slice(f * chunk, (f + 1) * chunk)
            for m in range(members):
                own = width // members
                at = f * own
                ref["dw"][m, at : at + own] = acc_u[f, m * own : (m + 1) * own].astype(BF)
            if not last:
                ref["dwd"][cols, :] = acc_d[f].astype(BF)
        if last:
            base, own = chunks * width // members, width // members
            deep = count * span // members
            for m in range(members):
                at = m * deep
                if at < index * span:
                    piece = ref["dwd_in"][at : at + deep]
                else:
                    at -= index * span
                    parts, here = [], at
                    while here < at + deep:
                        f, off = divmod(here, chunk)
                        size = min(chunk - off, at + deep - here)
                        parts.append(acc_d[f, off : off + size].astype(BF))
                        here += size
                    piece = parts[0] if len(parts) == 1 else jnp.concatenate(parts, axis=0)
                ref["dw"][m, base : base + deep] = piece
                rest = base + deep
                ref["dw"][m, rest : rest + own] = ref["acc_o"][m * own : (m + 1) * own].astype(BF)


def mlp_call(index, count, values, pieces):
    tokens, width = values["cot"].shape
    nseq, _, length = values["a"].shape
    members = len(pieces["wu"])
    ff = pieces["wu"][0].shape[1]
    span = ff // count
    rows = length // 2
    chunk = width
    first, last = index == 0, index == count - 1
    row = pl.BlockSpec((rows, width), lambda i: (i, 0))
    col = pl.BlockSpec((1, width, rows), lambda i: (i // 2, 0, i % 2))
    vec = whole((1, width))
    f32row = jax.ShapeDtypeStruct((tokens, width), F32)
    depth = span // chunk * (width // members)
    if last:
        depth += ff // members + width // members
    ins = {
        "me": SMEM,
        "mix": SMEM,
        "cot": row,
        "bu": pl.BlockSpec((1, span), lambda i: (0, index), pipeline_mode=pl.Buffered(1)),
    }
    outs = {
        "dw": (whole((members, depth, width)), jax.ShapeDtypeStruct((members, depth, width), BF)),
        "dbu": (whole((1, span)), jax.ShapeDtypeStruct((1, span), F32)),
        "up": (row, f32row),
    }
    scratch = {
        "acc_u": pltpu.VMEM((span // chunk, width, chunk), F32),
        "acc_d": pltpu.VMEM((span // chunk, chunk, width), F32),
        "low": pltpu.VMEM((rows, width), BF),
        "wu": pltpu.VMEM((width, span), BF),
        "wd": pltpu.VMEM((span, width), BF),
        "sems": pltpu.SemaphoreType.DMA((3, members)),
    }
    if first:
        ins |= {"x": row, "a": col, "bo": vec, "gain": vec, "bias": vec, "bd": vec}
        outs |= {"hid": (row, f32row), "act": (row, jax.ShapeDtypeStruct((tokens, width), BF))}
    else:
        ins |= {"act": row, "up_in": row, "back_in": row}
    if last:
        ins |= {"hid": row, "a": col, "gain": vec, "dwd_in": whole((index * span, width))}
        outs |= {
            "gh": (row, f32row),
            "ga": (col, jax.ShapeDtypeStruct(values["a"].shape, BF)),
            "sum": (whole((8, width)), jax.ShapeDtypeStruct((8, width), F32)),
        }
        scratch |= {"acc_o": pltpu.VMEM((width, width), F32)}
    else:
        outs |= {
            "back": (row, f32row),
            "dwd": (whole((span, width)), jax.ShapeDtypeStruct((span, width), BF)),
        }
    if first or last:
        scratch |= {"wo": pltpu.VMEM((width, width), BF)}
    parts = {
        (name, j): piece
        for name in (("wo", "wu", "wd") if first or last else ("wu", "wd"))
        for j, piece in enumerate(pieces[name])
    }
    names = [*ins, *parts, *outs, *scratch]
    result = pl.pallas_call(
        lambda *refs: mlp_kernel(index, count, names, members, *refs),
        grid=(tokens // rows,),
        in_specs=[*ins.values(), *(ANY for _ in parts)],
        out_specs=[spec for spec, _ in outs.values()],
        out_shape=[shape for _, shape in outs.values()],
        scratch_shapes=list(scratch.values()),
        compiler_params=params(60),
        cost_estimate=pl.CostEstimate(
            flops=6 * tokens * width * (2 * span + width // 2), bytes_accessed=40 * MIB, transcendentals=0
        ),
        name="mlp",
    )(*(values[name] for name in ins), *parts.values())
    return dict(zip(outs, result))


def qkv_grad_kernel(gq_ref, gk_ref, gv_ref, act_ref, dw_ref, acc):
    step = pl.program_id(0)
    last = pl.num_programs(0) - 1
    for part, g in enumerate((gq_ref, gk_ref, gv_ref)):
        term = dot_tt(act_ref[...], g[0])
        acc[part] = jnp.where(step == 0, term, acc[part] + term)

    @pl.when(step == last)
    def _():
        members = dw_ref.shape[0]
        own = acc.shape[1] // members
        for part in range(3):
            for m in range(members):
                dw_ref[m, part * own : (part + 1) * own] = acc[part, m * own : (m + 1) * own].astype(BF)


def qkv_grad_call(members, gq, gk, gv, act):
    tokens, width = act.shape
    nseq, _, length = gq.shape
    col = pl.BlockSpec((1, width, length), lambda s: (s, 0, 0))
    packed = (members, 3 * width // members, width)
    return pl.pallas_call(
        qkv_grad_kernel,
        grid=(nseq,),
        in_specs=[col, col, col, pl.BlockSpec((length, width), lambda s: (s, 0))],
        out_specs=whole(packed),
        out_shape=jax.ShapeDtypeStruct(packed, BF),
        scratch_shapes=[pltpu.VMEM((3, width, width), F32)],
        compiler_params=params(60),
        cost_estimate=pl.CostEstimate(
            flops=2 * tokens * width * 3 * width, bytes_accessed=16 * MIB, transcendentals=0
        ),
        name="qkv_grad",
    )(gq, gk, gv, act)


def first_back_kernel(
    me_ref, shift_ref, gq_ref, gk_ref, gv_ref, x_ref, gh_ref, gain_ref, *refs
):
    pieces, (gx_ref, sum_ref, ring, w_ref, sems) = refs[:-5], refs[-5:]
    length, width = x_ref.shape
    step = pl.program_id(0)
    shift = shift_ref[step]

    @pl.when(step == 0)
    def _():
        load_pieces(me_ref[0], pieces, w_ref, sems, True)
        sum_ref[...] = jnp.zeros_like(sum_ref)
        load_pieces(me_ref[0], pieces, w_ref, sems, False)

    rows = 256
    gain = gain_ref[...].astype(F32)
    sum_n = jnp.zeros((1, width), F32)
    sum_e = jnp.zeros((1, width), F32)
    for at in range(0, length, rows):
        rs = slice(at, at + rows)
        e = sum(
            dot_tt(g[0, :, rs], w_ref[:, i * width : (i + 1) * width])
            for i, g in enumerate((gq_ref, gk_ref, gv_ref))
        )
        n, r = norm_parts(x_ref[rs].astype(F32))
        eg = e * gain
        part = r * (
            eg - jnp.mean(eg, axis=-1, keepdims=True) - n * jnp.mean(eg * n, axis=-1, keepdims=True)
        )
        sum_n += jnp.sum(e * n, axis=0, keepdims=True)
        sum_e += jnp.sum(e, axis=0, keepdims=True)
        ring_put(ring, at, gh_ref[rs] + part)
    sum_ref[0:1] += sum_n
    sum_ref[1:2] += sum_e
    gx_ref[...] = ring_get(ring, length - shift, length)


def first_back_call(me, shift, gq, gk, gv, x, gh, gain, pieces):
    tokens, width = x.shape
    nseq, _, length = gq.shape
    row = pl.BlockSpec((length, width), lambda s: (s, 0))
    col = pl.BlockSpec((1, width, length), lambda s: (s, 0, 0))
    return pl.pallas_call(
        first_back_kernel,
        grid=(nseq,),
        in_specs=[SMEM, SMEM, col, col, col, row, row, whole((1, width)), *(ANY for _ in pieces)],
        out_specs=[row, whole((8, width))],
        out_shape=[
            jax.ShapeDtypeStruct((tokens, width), F32),
            jax.ShapeDtypeStruct((8, width), F32),
        ],
        scratch_shapes=[
            ring_shape(length, width),
            pltpu.VMEM((width, 3 * width), BF),
            pltpu.SemaphoreType.DMA((len(pieces),)),
        ],
        compiler_params=params(60),
        cost_estimate=pl.CostEstimate(
            flops=2 * tokens * width * 3 * width, bytes_accessed=30 * MIB, transcendentals=0
        ),
        name="first_back",
    )(me, shift, gq, gk, gv, x, gh, gain, *pieces)


def states_kernel(mix_ref, e_ref, c_ref, part_ref, ge_ref, sum_ref):
    @pl.when(pl.program_id(0) == 0)
    def _():
        sum_ref[...] = jnp.zeros_like(sum_ref)

    cot = c_ref[...].astype(F32)
    total = None
    for j in range(e_ref.shape[0]):
        e = e_ref[j].astype(F32)
        term = mix_ref[j] * e
        total = term if total is None else total + term
        ge_ref[j] = mix_ref[j] * cot
        sum_ref[j : j + 1] += jnp.sum(e * cot, axis=0, keepdims=True)
    part_ref[...] = total


def states_call(mix, earlier, cot):
    states, tokens, width = earlier.shape
    rows = 256
    row = pl.BlockSpec((rows, width), lambda i: (i, 0))
    stack = pl.BlockSpec((states, rows, width), lambda i: (0, i, 0))
    return pl.pallas_call(
        states_kernel,
        grid=(tokens // rows,),
        in_specs=[SMEM, stack, row],
        out_specs=[row, stack, whole((8, width))],
        out_shape=[
            jax.ShapeDtypeStruct((tokens, width), F32),
            jax.ShapeDtypeStruct(earlier.shape, F32),
            jax.ShapeDtypeStruct((8, width), F32),
        ],
        compiler_params=params(32),
        cost_estimate=pl.CostEstimate(
            flops=16 * tokens * width, bytes_accessed=48 * MIB, transcendentals=0
        ),
        name="states",
    )(mix, earlier, cot)


def mix_kernel(shift_ref, mix_ref, part_ref, b_ref, out_ref, ring):
    length = b_ref.shape[0]
    ring_put(ring, 0, b_ref[...])
    rolled = ring_get(ring, length - shift_ref[pl.program_id(0)], length)
    out_ref[...] = (part_ref[...] + mix_ref[4] * rolled).astype(BF)


def mix_call(shift, mix, part, block_out):
    tokens, width = part.shape
    nseq = shift.shape[0]
    length = tokens // nseq
    row = pl.BlockSpec((length, width), lambda s: (s, 0))
    return pl.pallas_call(
        mix_kernel,
        grid=(nseq,),
        in_specs=[SMEM, SMEM, row, row],
        out_specs=row,
        out_shape=jax.ShapeDtypeStruct((tokens, width), BF),
        scratch_shapes=[ring_shape(length, width)],
        compiler_params=params(48),
        cost_estimate=pl.CostEstimate(
            flops=2 * tokens * width, bytes_accessed=16 * MIB, transcendentals=0
        ),
        name="mix",
    )(shift, mix, part, block_out)


def swap(v, axis, bits):
    size = lax.axis_size(axis)
    return lax.ppermute(v, axis, [(i, i ^ bits) for i in range(size)])


def gather_pieces(v):
    pieces = []
    for k in range(lax.axis_size("shard") // 2):
        far = v if k == 0 else swap(v, "shard", 2 * k)
        pieces += [far, swap(far, "shard", 1)]
    return pieces


def in_order(pieces, mine):
    stack = jnp.stack(pieces)
    return [lax.dynamic_index_in_dim(stack, j ^ mine, 0, keepdims=False) for j in range(len(pieces))]


def total_of(terms):
    total = terms[0].astype(F32)
    for term in terms[1:]:
        total = total + term.astype(F32)
    return total


def reduce_packed(packed):
    members, rows, width = packed.shape
    me, rep = lax.axis_index("shard"), lax.axis_index("rep")
    core, chip = me % 2, me // 2
    groups = members // 2
    pairs = packed.reshape(groups, 2, rows, width)

    def pick(v, at):
        return lax.dynamic_index_in_dim(v, at, 0, keepdims=False)

    other = lax.dynamic_index_in_dim(pairs, 1 - core, 1, keepdims=False)
    near = swap(other, "shard", 1)
    own = lax.dynamic_index_in_dim(pairs, core, 1, keepdims=False)
    terms = [pick(own, chip), pick(near, chip)]
    for k in range(1, groups):
        send = total_of([pick(own, chip ^ k), pick(near, chip ^ k)]).astype(BF)
        terms.append(swap(send, "shard", 2 * k))
    side, group = rep % 2, rep // 2
    count = lax.axis_size("rep") // 2
    terms = [t.reshape(2, rows // 2, width) for t in terms]
    send = total_of([pick(t, 1 - side) for t in terms]).astype(BF)
    terms = [pick(t, side) for t in terms] + [swap(send, "rep", 1)]
    terms = [t.reshape(count, rows // 2 // count, width) for t in terms]
    got = []
    for k in range(1, count):
        send = total_of([pick(t, group ^ k) for t in terms]).astype(BF)
        got.append(swap(send, "rep", 2 * k))
    done = total_of([pick(t, group) for t in terms] + got).astype(BF)
    pieces = [done] + [swap(done, "rep", 2 * k) for k in range(1, count)]
    half = jnp.concatenate(in_order(pieces, group), axis=0)
    return jnp.concatenate(in_order([half, swap(half, "rep", 1)], side), axis=0).astype(F32)


def reduce_small(v):
    for axis in ("shard", "rep"):
        bits = 1
        while bits < lax.axis_size(axis):
            v = v + swap(v, axis, bits)
            bits *= 2
    return v


def shards(
    inputs, earlier, segments, cotangent, mix_weights,
    ln1_gain, ln1_bias, qkv_weight, qkv_bias, out_weight, out_bias,
    ln2_gain, ln2_bias, up_weight, up_bias, down_weight, down_bias,
):
    nseq, length = segments.shape
    width = inputs.shape[1]
    blk = length // 2

    members = lax.axis_size("shard")
    me = lax.axis_index("shard").astype(jnp.int32)
    me_ref = me[None]
    vectors = [ln1_gain, ln1_bias, qkv_bias, out_bias, ln2_gain, ln2_bias, up_bias, down_bias]
    sizes = [v.shape[0] for v in vectors]
    flat = jnp.concatenate(vectors)
    flat = jnp.concatenate([flat, jnp.zeros((-flat.shape[0] % 128,), BF)]).reshape(-1, 128)
    flat = jnp.stack(in_order(gather_pieces(flat), me)).reshape(members, -1)
    full, at = [], 0
    for size in sizes:
        full.append(flat[:, at : at + size].reshape(-1))
        at += size
    g1, b1, bqkv, bo, g2, b2, bu, bd = full
    wqkv, wo, wu, wd = [gather_pieces(v) for v in (qkv_weight, out_weight, up_weight, down_weight)]

    shift = jnp.argmax(segments[:, : length - blk + 1] == segments[:, blk - 1 :], axis=1).astype(jnp.int32)
    rolled = (jnp.arange(length, dtype=jnp.int32)[None] + shift[:, None]) % length
    twice = jnp.concatenate([segments, segments], axis=1)
    others = jnp.stack([lax.dynamic_slice(twice[i], (shift[i] + blk,), (length - blk,)) for i in range(nseq)])
    segc, segr = others[:, :, None], others[:, None, :]
    inv = jnp.exp(jnp.arange(HEAD // 2, dtype=F32) * (-math.log(10000.0) / (HEAD // 2)))
    angles = rolled.astype(F32)[:, None, :] * inv[None, :, None]
    cos, sin = jnp.cos(angles), jnp.sin(angles)

    part, earlier_grad, sums3 = states_call(mix_weights, earlier, cotangent)
    xr, cr, act, q, k, v = qkv_call(
        me_ref, shift, inputs, cotangent, g1[None], b1[None], bqkv.astype(F32)[:, None], cos, sin, wqkv
    )
    o, lse = attend_call(segc, segr, q, k, v)
    values = {
        "me": me_ref, "mix": mix_weights, "x": xr, "cot": cr, "a": o, "bo": bo[None], "gain": g2[None],
        "bias": b2[None], "bu": bu[None], "bd": bd[None],
    }
    pieces = {"wo": wo, "wu": wu, "wd": wd}
    packs, dbus = [], []
    for index in range(MLP_PARTS):
        got = mlp_call(index, MLP_PARTS, values, pieces)
        packs.append(got["dw"])
        dbus.append(got["dbu"])
        values |= {"up_in": got["up"], "back_in": got.get("back"), "dwd_in": got.get("dwd")}
        values |= {name: got[name] for name in ("hid", "act") if name in got}
    block_out, gh, ga, sums2 = (got[name] for name in ("up", "gh", "ga", "sum"))
    gq, gk, gv, sums1 = attend_back_call(segc, segr, q, k, v, o, ga, lse, cos, sin)
    packs.append(qkv_grad_call(members, gq, gk, gv, act))
    output = mix_call(shift, mix_weights, part, block_out)
    input_grad, sums0 = first_back_call(me_ref, shift, gq, gk, gv, xr, gh, g1[None], wqkv)

    first, second, third = [reduce_packed(p) for p in packs]
    own = width // members
    deep = down_weight.shape[0]

    def wide(blocks):
        return jnp.concatenate([blocks[at : at + own] for at in range(0, blocks.shape[0], own)], axis=1)

    more = second.shape[0] - deep - own
    d_up = jnp.concatenate([wide(first), wide(second[:more])], axis=1)
    d_down, d_out, d_qkv = second[more : more + deep], second[more + deep :], wide(third)

    sums = [
        sums0[0], sums0[1], jnp.sum(sums1, axis=(0, 3)).reshape(-1), sums2[2], sums2[0], sums2[1],
        jnp.concatenate(dbus, axis=1)[0], sums2[3],
    ]
    tail = jnp.concatenate([jnp.sum(sums3[:4], axis=1), jnp.sum(sums2[4])[None]])
    small = jnp.concatenate([v.reshape(members, -1) for v in sums], axis=1)
    used = small.shape[1]
    tail = jnp.broadcast_to(tail[None], (members, tail.shape[0]))
    small = jnp.concatenate([small, tail, jnp.zeros((members, -(used + 5) % 128), F32)], axis=1)
    small = reduce_small(small)
    mix_grad = small[0, used : used + 5]
    small = lax.dynamic_index_in_dim(small, me, 0, keepdims=False)
    parts, at = [], 0
    for size in sizes:
        parts.append(small[at : at + size])
        at += size
    return (
        output, input_grad, earlier_grad, mix_grad,
        parts[0], parts[1], d_qkv, parts[2], d_out, parts[3], parts[4], parts[5],
        d_up, parts[6], d_down, parts[7],
    )


def solution(mesh):
    rows, shard = P(("rep", "shard"), None), P("shard")
    mat, deep = P("shard", None), P(None, ("rep", "shard"), None)
    return jax.shard_map(
        shards,
        mesh=mesh,
        in_specs=(
            rows, deep, rows, rows, P(),
            shard, shard, mat, shard, mat, shard, shard, shard, mat, shard, mat, shard,
        ),
        out_specs=(
            rows, rows, deep, P(),
            shard, shard, mat, shard, mat, shard, shard, shard, mat, shard, mat, shard,
        ),
        check_vma=False,
    )
```

```python
import math

import jax
import jax.numpy as jnp
import numpy as np
from jax import lax
from jax.experimental import pallas as pl
from jax.experimental.pallas import tpu as pltpu
from jax.sharding import PartitionSpec as P

HEADS = 12
HEAD = 64
PAIR = 2 * HEAD
EPSILON = 1e-05
LOG2E = math.log2(math.e)
NEG = -1e30
GELU_A = math.sqrt(2.0 / math.pi)
GELU_B = GELU_A * 0.044715
BF = jnp.bfloat16
F32 = jnp.float32
MIB = 1 << 20

COST_SHARE = 1.5


def cost(us):
    return pl.CostEstimate(flops=int(us * COST_SHARE * 1.15e9), bytes_accessed=1024, transcendentals=0)


def dot_nn(a, b):
    return lax.dot_general(a, b, (((1,), (0,)), ((), ())), preferred_element_type=F32)


def dot_nt(a, b):
    return lax.dot_general(a, b, (((1,), (1,)), ((), ())), preferred_element_type=F32)


def dot_tn(a, b):
    return lax.dot_general(a, b, (((0,), (0,)), ((), ())), preferred_element_type=F32)


def dot_tt(a, b):
    return lax.dot_general(a, b, (((0,), (1,)), ((), ())), preferred_element_type=F32)


def params(vmem):
    return pltpu.CompilerParams(vmem_limit_bytes=vmem * MIB)


ANY = pl.BlockSpec(memory_space=pl.ANY)


def load_pieces(me, pieces, target, sems, start, cols=None):
    copies = []
    for j, piece in enumerate(pieces):
        rows = piece.shape[0]
        at = pl.multiple_of((me ^ j) * rows, rows)
        source = piece if cols is None else piece.at[:, cols]
        copies.append(pltpu.make_async_copy(source, target.at[pl.ds(at, rows), :], sems.at[j]))
    for copy in copies:
        if start:
            copy.start()
        else:
            copy.wait()


def pack(target, source, base, own, sides, groups, at):
    rows, cols = own // groups, source.shape[-1] // sides
    for side in range(sides):
        for group in range(groups):
            for j in range(cols // 128):
                here = at + j * rows
                col = side * cols + j * 128
                target[side, group, here : here + rows, :] = source[
                    pl.ds(base + group * rows, rows), col : col + 128
                ].astype(BF)


def pack_all(targets, me, source, own, at):
    for t, target in enumerate(targets):
        count, sides, groups = target.shape[:3]
        for i in range(count):
            place = i if len(targets) == 1 else 2 * i + ((me % 2) ^ t)
            pack(target.at[i], source, pl.multiple_of(place * own, own), own, sides, groups, at)


def unpack(v, at, own, cols):
    sides, groups = v.shape[:2]
    rows, wide = own // groups, cols // sides
    count = wide // 128
    part = v[:, :, at : at + rows * count].reshape(sides, groups, count, rows, 128)
    return part.transpose(1, 3, 0, 2, 4).reshape(own, cols)


def packed_rows(own, cols, sides, groups):
    return own * cols // (128 * sides * groups)


def packed_shapes(form, members, own_cols):
    sides, groups = form
    n = sum(packed_rows(own, cols, sides, groups) for own, cols in own_cols)
    split = 1 if form == (1, 1) else 2
    shape = (members // split, sides, groups, n, 128)
    return [(whole(shape), jax.ShapeDtypeStruct(shape, BF)) for _ in range(split)]


def whole(shape):
    zeros = (0,) * len(shape)
    return pl.BlockSpec(shape, lambda *_: zeros, pipeline_mode=pl.Buffered(1))


SMEM = pl.BlockSpec(memory_space=pltpu.SMEM)


def ring_shape(length, width):
    return pltpu.VMEM((width // 128, 2 * length, 128), F32)


def ring_put(ring, at, value):
    for j in range(ring.shape[0]):
        part = value[:, j * 128 : (j + 1) * 128]
        ring[j, at : at + value.shape[0]] = part
        twin = ring.shape[1] // 2 + at
        ring[j, twin : twin + value.shape[0]] = part


def ring_get(ring, start, rows):
    return jnp.concatenate([ring[j, pl.ds(start, rows), :] for j in range(ring.shape[0])], axis=1)


def norm_parts(v):
    mean = jnp.mean(v, axis=-1, keepdims=True)
    centred = v - mean
    var = jnp.mean(centred * centred, axis=-1, keepdims=True)
    r = lax.rsqrt(var + EPSILON)
    return centred * r, r


ROWS = ("g1", "b1", "bqkv", "bo", "g2", "b2", "bu", "bd")


def vec(ref, name, base=0, share=None):
    row = ROWS.index(name)
    size = share or ref.shape[2] // DEEP_ROWS[name]
    parts = [ref[m, row : row + 1, base : base + size] for m in range(ref.shape[0])]
    return jnp.concatenate(parts, axis=1).astype(F32)


DEEP_ROWS = {"g1": 4, "b1": 4, "bo": 4, "g2": 4, "b2": 4, "bd": 4, "bu": 1}


def column(row):
    return jnp.broadcast_to(row, (128, row.shape[1])).T[:, :1]


def roll_kernel(x_ref, cot_ref, seg_ref, small_ref, tab_ref, *refs):
    shift_ref, xr_ref, cr_ref, act_ref, seg_out, cos_ref, sin_ref, ring = refs[-8:]
    length = x_ref.shape[0]
    half = length // 2
    seg = jnp.broadcast_to(seg_ref[0].astype(F32), (8, length))
    place = lax.broadcasted_iota(jnp.int32, (8, length), 1)
    same = (seg == pltpu.roll(seg, length - (half - 1), 1)) & (place <= half)
    shift = jnp.min(jnp.where(same, place.astype(F32), float(length))).astype(jnp.int32)
    shift_ref[pl.program_id(0)] = shift
    back = lax.rem(length - shift, length)
    seg_out[0] = pltpu.roll(seg, back, 1)[:, half:]
    cos_ref[0] = pltpu.roll(tab_ref[0], back, 1)
    sin_ref[0] = pltpu.roll(tab_ref[1], back, 1)
    for source, target in ((cot_ref, cr_ref), (x_ref, xr_ref)):
        ring_put(ring, 0, source[...].astype(F32))
        target[...] = ring_get(ring, shift, length).astype(BF)
    gain, bias = vec(small_ref, "g1"), vec(small_ref, "b1")
    rows = 256
    for at in range(0, length, rows):
        n, _ = norm_parts(xr_ref[at : at + rows].astype(F32))
        act_ref[at : at + rows] = (n * gain + bias).astype(BF)


def roll_call(x, cot, seg, small, tables, deps):
    tokens, width = x.shape
    nseq, length = seg.shape
    row = pl.BlockSpec((length, width), lambda s: (s, 0))
    tab = pl.BlockSpec((1, HEAD // 2, length), lambda s: (s, 0, 0))
    low = jax.ShapeDtypeStruct((tokens, width), BF)
    turn = jax.ShapeDtypeStruct((nseq, HEAD // 2, length), F32)
    return pl.pallas_call(
        roll_kernel,
        grid=(nseq,),
        in_specs=[
            row, row, pl.BlockSpec((1, 1, length), lambda s: (s, 0, 0)), whole(small.shape), whole(tables.shape),
            *(ANY for _ in deps),
        ],
        out_specs=[SMEM, row, row, row, pl.BlockSpec((1, 8, length // 2), lambda s: (s, 0, 0)), tab, tab],
        out_shape=[
            jax.ShapeDtypeStruct((nseq,), jnp.int32), low, low, low,
            jax.ShapeDtypeStruct((nseq, 8, length // 2), F32), turn, turn,
        ],
        scratch_shapes=[ring_shape(length, width)],
        compiler_params=params(62),
        cost_estimate=cost(10),
        name="roll",
    )(x, cot, seg[:, None, :], small, tables, *deps)


def qkv_kernel(me_ref, act_ref, small_ref, cos_ref, sin_ref, *refs):
    pieces, (q_ref, k_ref, v_ref, w_ref, sems) = refs[:-5], refs[-5:]
    width = act_ref.shape[1]

    @pl.when(pl.program_id(0) == 0)
    def _():
        load_pieces(me_ref[0], pieces, w_ref, sems, True)
        load_pieces(me_ref[0], pieces, w_ref, sems, False)

    half = HEAD // 2
    rows = 256
    bias = vec(small_ref, "bqkv", 0, 3 * width // small_ref.shape[0])
    cos, sin = cos_ref[0], sin_ref[0]
    for part, out in enumerate((q_ref, k_ref, v_ref)):
        scale = LOG2E * HEAD**-0.5 if part == 0 else 1.0
        for base in range(0, width, rows):
            at = part * width + base
            cols = slice(at, at + rows)
            y = dot_tt(w_ref[:, cols], act_ref[...]) + column(bias[:, cols])
            if part == 2:
                out[0, base : base + rows, :] = y.astype(BF)
                continue
            for h in range(0, rows, HEAD):
                u, w = y[h : h + half], y[h + half : h + HEAD]
                a, b = u * cos - w * sin, w * cos + u * sin
                if part == 0:
                    a, b = a * scale, b * scale
                out[0, base + h : base + h + half, :] = a.astype(BF)
                out[0, base + h + half : base + h + HEAD, :] = b.astype(BF)


def qkv_call(me, act, small, cos, sin, pieces):
    tokens, width = act.shape
    nseq, _, length = cos.shape
    col = pl.BlockSpec((1, width, length), lambda s: (s, 0, 0))
    tab = pl.BlockSpec((1, HEAD // 2, length), lambda s: (s, 0, 0))
    turned = jax.ShapeDtypeStruct((nseq, width, length), BF)
    return pl.pallas_call(
        qkv_kernel,
        grid=(nseq,),
        in_specs=[
            SMEM, pl.BlockSpec((length, width), lambda s: (s, 0)), whole(small.shape), tab, tab,
            *(ANY for _ in pieces),
        ],
        out_specs=[col, col, col],
        out_shape=[turned, turned, turned],
        scratch_shapes=[
            pltpu.VMEM((width, 3 * width), BF),
            pltpu.SemaphoreType.DMA((len(pieces),)),
        ],
        compiler_params=params(62),
        cost_estimate=cost(15),
        name="qkv",
    )(me, act, small, cos, sin, *pieces)


def fill_masks(seg_ref, mask, blk):
    row = seg_ref[0, 0:1, :]
    col = column(row)
    kk = lax.broadcasted_iota(jnp.int32, (blk, blk), 0)
    qq = lax.broadcasted_iota(jnp.int32, (blk, blk), 1)
    causal = kk <= qq
    mask[0] = jnp.where(causal, 0.0, NEG)
    for i, (kb, qb) in enumerate(((0, 0), (0, 1), (1, 1))):
        same = col[kb * blk : (kb + 1) * blk] == row[:, qb * blk : (qb + 1) * blk]
        keep = same if kb != qb else same & causal
        mask[1 + i] = jnp.where(keep, 0.0, NEG)


def scores_of(keys, query, mask, half, qb, blk):
    top = dot_nn(keys[: (qb + 1) * blk], query)
    if half == 0:
        diag = top[qb * blk :] + mask[0]
        return diag if qb == 0 else jnp.concatenate([top[:blk], diag], axis=0)
    if qb == 0:
        return top + mask[1]
    return jnp.concatenate([top[:blk] + mask[2], top[blk:] + mask[3]], axis=0)


def one_head(pair_rows, head):
    zero = jnp.zeros((HEAD, pair_rows.shape[1]), pair_rows.dtype)
    rows = pair_rows[head * HEAD : (head + 1) * HEAD]
    return jnp.concatenate([rows, zero] if head == 0 else [zero, rows], axis=0)


def attend_kernel(seg_ref, q_ref, k_ref, v_ref, o_ref, l_ref, mask):
    length = q_ref.shape[2]
    blk = length // 4

    @pl.when(pl.program_id(1) == 0)
    def _():
        fill_masks(seg_ref, mask, blk)

    for half in range(2):
        base = half * 2 * blk
        keys = k_ref[0, :, base : base + 2 * blk].T
        for head in range(2):
            hs = slice(head * HEAD, (head + 1) * HEAD)
            for qb in range(2):
                qs = slice(base + qb * blk, base + (qb + 1) * blk)
                s = scores_of(keys, one_head(q_ref[0, :, qs], head), mask, half, qb, blk)
                top = jnp.max(s, axis=0, keepdims=True)
                p = jnp.exp2(s - top)
                total = jnp.sum(p, axis=0, keepdims=True)
                o = dot_nn(v_ref[0, hs, base : base + (qb + 1) * blk], p.astype(BF))
                o_ref[0, hs, qs] = (o / total).astype(BF)
                l_ref[0, 0, head : head + 1, qs] = top + jnp.log2(total)


def attend_call(seg, q, k, v):
    nseq, width, length = q.shape
    pairs = width // PAIR
    blk = length // 4
    blockspec = pl.BlockSpec((1, PAIR, length), lambda s, h: (s, h, 0))
    return pl.pallas_call(
        attend_kernel,
        grid=(nseq, pairs),
        in_specs=[
            pl.BlockSpec((1, 8, 2 * blk), lambda s, h: (s, 0, 0)),
            blockspec, blockspec, blockspec,
        ],
        out_specs=[blockspec, pl.BlockSpec((1, 1, 2, length), lambda s, h: (s, h, 0, 0))],
        out_shape=[
            jax.ShapeDtypeStruct((nseq, width, length), BF),
            jax.ShapeDtypeStruct((nseq, pairs, 2, length), F32),
        ],
        scratch_shapes=[pltpu.VMEM((4, blk, blk), F32)],
        compiler_params=params(62),
        cost_estimate=cost(30),
        name="attend",
    )(seg, q, k, v)


def attend_back_kernel(
    seg_ref, q_ref, k_ref, v_ref, o_ref, g_ref, l_ref, cos_ref, sin_ref, *refs
):
    gq_ref, gk_ref, gv_ref, sum_ref, mask, turn = refs[-6:]
    length = q_ref.shape[2]
    blk = length // 4
    hd = HEAD // 2

    @pl.when(pl.program_id(1) == 0)
    def _():
        fill_masks(seg_ref, mask, blk)

    for half in range(2):
        base = half * 2 * blk
        ks = slice(base, base + 2 * blk)
        keys = k_ref[0, :, ks].T
        values = v_ref[0, :, ks].T
        for head in range(2):
            hs = slice(head * HEAD, (head + 1) * HEAD)
            for qb in range(2):
                qs = slice(base + qb * blk, base + (qb + 1) * blk)
                span = slice(base, base + (qb + 1) * blk)
                g = g_ref[0, hs, qs]
                delta = jnp.sum(g.astype(F32) * o_ref[0, hs, qs].astype(F32), axis=0, keepdims=True)
                s = scores_of(keys, one_head(q_ref[0, :, qs], head), mask, half, qb, blk)
                p = jnp.exp2(s - l_ref[0, 0, head : head + 1, qs])
                gp = dot_nn(values[: (qb + 1) * blk], one_head(g_ref[0, :, qs], head))
                ds = (p * (gp - delta)).astype(BF)
                dv = dot_nt(g, p.astype(BF))
                dk = dot_nt(q_ref[0, hs, qs], ds)
                turn[0, hs, qs] = dot_nn(k_ref[0, hs, span], ds)
                if qb == 0:
                    held_k, held_v = dk, dv
                else:
                    turn[1, hs, base : base + blk] = dk[:, :blk] + held_k
                    turn[1, hs, base + blk : base + 2 * blk] = dk[:, blk:]
                    turn[2, hs, base : base + blk] = dv[:, :blk] + held_v
                    turn[2, hs, base + blk : base + 2 * blk] = dv[:, blk:]
    cos, sin = cos_ref[0], sin_ref[0]

    ones = jnp.ones((8, length), BF)
    for part, (out, scale) in enumerate(((gq_ref, HEAD**-0.5), (gk_ref, 1.0 / LOG2E), (gv_ref, 1.0))):
        for head in range(2):
            at = head * HEAD
            u = turn[part, at : at + hd]
            w = turn[part, at + hd : at + HEAD]
            if part < 2:
                u, w = (u * cos + w * sin) * scale, (w * cos - u * sin) * scale
            out[0, at : at + hd, :] = u.astype(BF)
            out[0, at + hd : at + HEAD, :] = w.astype(BF)
        sum_ref[0, part] = dot_nt(ones, out[0])


def attend_back_call(seg, q, k, v, o, g, lse, cos, sin, base, pairs, deps, us=15):
    nseq, width, length = q.shape
    blk = length // 4
    source = pl.BlockSpec((1, PAIR, length), lambda s, h: (s, base + h, 0))
    target = pl.BlockSpec((1, PAIR, length), lambda s, h: (s, h, 0))
    tab = pl.BlockSpec((1, HEAD // 2, length), lambda s, h: (s, 0, 0))
    turned = jax.ShapeDtypeStruct((nseq, pairs * PAIR, length), BF)
    return pl.pallas_call(
        attend_back_kernel,
        grid=(nseq, pairs),
        in_specs=[
            pl.BlockSpec((1, 8, 2 * blk), lambda s, h: (s, 0, 0)),
            source, source, source, source, source,
            pl.BlockSpec((1, 1, 2, length), lambda s, h: (s, base + h, 0, 0)),
            tab, tab, *(ANY for _ in deps),
        ],
        out_specs=[
            target, target, target,
            pl.BlockSpec((1, 3, 8, PAIR), lambda s, h: (s, 0, 0, h)),
        ],
        out_shape=[turned, turned, turned, jax.ShapeDtypeStruct((nseq, 3, 8, pairs * PAIR), F32)],
        scratch_shapes=[pltpu.VMEM((4, blk, blk), F32), pltpu.VMEM((3, PAIR, length), F32)],
        compiler_params=params(62),
        cost_estimate=cost(us),
        name="attend_back",
    )(seg, q, k, v, o, g, lse, cos, sin, *deps)


def mlp_kernel(base, first, last, names, members, *refs):
    ref = dict(zip(names, refs))
    rows, width = ref["cot"].shape
    step = pl.program_id(0)
    final = pl.num_programs(0) - 1
    acc_u, acc_d, low = ref["acc_u"], ref["acc_d"], ref["low"]
    span = acc_u.shape[1]
    me, sems = ref["me"][0], ref["sems"]
    share = span // members
    small = ref["small"]

    def weights(start):
        copy = pltpu.make_async_copy(ref["wu_in"], ref["wu"], sems.at[members])
        if start:
            copy.start()
        else:
            copy.wait()
        load_pieces(me, [ref["wd", j] for j in range(members)], ref["wd"], sems, start)

    @pl.when(step == 0)
    def _():
        weights(True)
        acc_u[...] = jnp.zeros_like(acc_u)
        acc_d[...] = jnp.zeros_like(acc_d)
        ref["dbu"][...] = jnp.zeros_like(ref["dbu"])

    alpha = ref["mix"][4]
    cot = ref["cot"][...].astype(F32)
    g_out = cot * alpha
    low[...] = g_out.astype(BF)
    if first:
        hidden = ref["x"][...].astype(F32) + dot_tn(ref["a"][0], ref["wo"][...]) + vec(small, "bo")
        n, _ = norm_parts(hidden)
        ref["hid"][...] = hidden
        ref["act"][...] = (n * vec(small, "g2") + vec(small, "b2")).astype(BF)

    @pl.when(step == 0)
    def _():
        weights(False)

    act2 = ref["act"]
    if first:
        total_up = ref["hid"][...] + vec(small, "bd")
        total_back = None
    else:
        total_up, total_back = ref["up_in"][...], ref["back_in"][...]
    chunk = width + width // 3
    bu = vec(small, "bu", base, share)
    for at in range(0, span, chunk):
        cols = slice(at, at + chunk)
        wu, wd = ref["wu"][:, cols], ref["wd"][cols, :]
        pre = dot_nn(act2[...], wu) + bu[:, cols]
        g_act = dot_nt(low[...], wd)
        square = pre * pre
        h = 0.5 + 0.5 * jnp.tanh(pre * (GELU_A + GELU_B * square))
        act = (pre * h).astype(BF)
        slope = h + (pre * (h * (1.0 - h))) * (2.0 * GELU_A + 6.0 * GELU_B * square)
        g_pre = g_act * slope
        ref["dbu"][:, cols] += jnp.sum(g_pre, axis=0, keepdims=True)
        g_low = g_pre.astype(BF)
        total_up = total_up + dot_nn(act, wd)
        more = dot_nt(g_low, wu)
        total_back = more if total_back is None else total_back + more
        acc_d[cols, :] += dot_tn(act, low[...])
        acc_u[:, cols] += dot_tn(act2[...], g_low)
    ref["up"][...] = total_up
    if not last:
        ref["back"][...] = total_back
    else:
        e = total_back
        gain = vec(small, "g2")
        n, r = norm_parts(ref["hid"][...])
        eg = e * gain
        part = r * (
            eg - jnp.mean(eg, axis=-1, keepdims=True) - n * jnp.mean(eg * n, axis=-1, keepdims=True)
        )
        g_hidden = g_out + part
        ref["gh"][...] = g_hidden
        g_low = g_hidden.astype(BF)

        @pl.when(step == 0)
        def _():
            ref["sum"][...] = jnp.zeros_like(ref["sum"])
            ref["acc_o"][...] = jnp.zeros_like(ref["acc_o"])

        for i, term in enumerate((e * n, e, g_hidden, g_out, total_up * cot)):
            ref["sum"][i : i + 1, :] += jnp.sum(term, axis=0, keepdims=True)
        ref["acc_o"][...] += dot_nn(ref["a"][0], g_low)
        ref["ga"][0] = dot_nt(ref["wo"][...], g_low).astype(BF)

    @pl.when(step == final)
    def _():
        targets = [ref[name] for name in ("dw0", "dw1") if name in ref]
        sides, groups = targets[0].shape[1:3]
        at = 0
        for source in (acc_u, acc_d, ref["acc_o"]) if last else (acc_u, acc_d):
            own = source.shape[0] // members
            pack_all(targets, me, source, own, at)
            at += packed_rows(own, source.shape[1], sides, groups)


def mlp_call(base, share, first, last, values, form, members, deps):
    tokens, width = values["cot"].shape
    nseq, _, length = values["a"].shape
    span = share * members
    rows = length // 2
    row = pl.BlockSpec((rows, width), lambda i: (i, 0))
    col = pl.BlockSpec((1, width, rows), lambda i: (i // 2, 0, i % 2))
    f32row = jax.ShapeDtypeStruct((tokens, width), F32)
    ins = {
        "me": SMEM,
        "mix": SMEM,
        "cot": row,
        "small": whole(values["small"].shape),
        "wu_in": ANY,
    }
    parts = [(width // members, span), (span // members, width)]
    if last:
        parts.append((width // members, width))
    outs = {f"dw{i}": pair for i, pair in enumerate(packed_shapes(form, members, parts))}
    outs |= {
        "dbu": (whole((1, span)), jax.ShapeDtypeStruct((1, span), F32)),
        "up": (row, f32row),
    }
    scratch = {
        "acc_u": pltpu.VMEM((width, span), F32),
        "acc_d": pltpu.VMEM((span, width), F32),
        "low": pltpu.VMEM((rows, width), BF),
        "wu": pltpu.VMEM((width, span), BF),
        "wd": pltpu.VMEM((span, width), BF),
        "sems": pltpu.SemaphoreType.DMA((members + 1,)),
    }
    if first:
        ins |= {"x": row}
        outs |= {"hid": (row, f32row), "act": (row, jax.ShapeDtypeStruct((tokens, width), BF))}
    else:
        ins |= {"act": row, "up_in": row, "back_in": row}
    if last:
        ins |= {"hid": row}
        outs |= {
            "gh": (row, f32row),
            "ga": (col, jax.ShapeDtypeStruct(values["a"].shape, BF)),
            "sum": (whole((8, width)), jax.ShapeDtypeStruct((8, width), F32)),
        }
        scratch |= {"acc_o": pltpu.VMEM((width, width), F32)}
    else:
        outs |= {"back": (row, f32row)}
    if first or last:
        ins |= {"a": col, "wo": whole((width, width))}
    names = [*ins, *(("wd", j) for j in range(members)), *(("dep", i) for i in range(len(deps))), *outs, *scratch]
    result = pl.pallas_call(
        lambda *refs: mlp_kernel(base, first, last, names, members, *refs),
        grid=(tokens // rows,),
        in_specs=[*ins.values(), *(ANY for _ in range(members + len(deps)))],
        out_specs=[spec for spec, _ in outs.values()],
        out_shape=[shape for _, shape in outs.values()],
        scratch_shapes=list(scratch.values()),
        compiler_params=params(62),
        cost_estimate=cost(45),
        name="mlp",
    )(*(values[name] for name in ins), *values["wd"], *deps)
    return dict(zip(outs, result))


def qkv_grad_kernel(parts, deps, me_ref, act_ref, *refs):
    grads, targets, acc = refs[:parts], refs[parts + deps : -1], refs[-1]
    step = pl.program_id(0)
    last = pl.num_programs(0) - 1
    width = act_ref.shape[1]
    at = 0
    for g in grads:
        cols = slice(at, at + g.shape[1])
        at += g.shape[1]
        term = dot_tt(act_ref[...], g[0])
        acc[:, cols] = jnp.where(step == 0, term, acc[:, cols] + term)

    @pl.when(step == last)
    def _():
        split = len(targets)
        pack_all(targets, me_ref[0], acc, width // (targets[0].shape[0] * split), 0)


def turned_spec(v):
    return pl.BlockSpec((1, *v.shape[1:]), lambda s: (s, 0, 0))


def qkv_grad_call(me, grads, act, form, members, deps):
    tokens, width = act.shape
    nseq, _, length = grads[0].shape
    outs = packed_shapes(form, members, [(width // members, 3 * width)])
    return pl.pallas_call(
        lambda *refs: qkv_grad_kernel(len(grads), len(deps), *refs),
        grid=(nseq,),
        in_specs=[
            SMEM, pl.BlockSpec((length, width), lambda s: (s, 0)),
            *(turned_spec(g) for g in grads), *(ANY for _ in deps),
        ],
        out_specs=[spec for spec, _ in outs],
        out_shape=[shape for _, shape in outs],
        scratch_shapes=[pltpu.VMEM((width, 3 * width), F32)],
        compiler_params=params(62),
        cost_estimate=cost(13),
        name="qkv_grad",
    )(me, act, *grads, *deps)


def first_back_kernel(parts, deps, me_ref, shift_ref, x_ref, gh_ref, small_ref, *refs):
    smalls = refs[parts : parts + parts // 3 + 4]
    grads, pieces = refs[:parts], refs[parts + len(smalls) : -5 - deps]
    gx_ref, sum_ref, ring, w_ref, sems = refs[-5:]
    length, width = x_ref.shape
    step = pl.program_id(0)
    shift = shift_ref[step]

    @pl.when(step == 0)
    def _():
        load_pieces(me_ref[0], pieces, w_ref, sems, True)
        sum_ref[...] = jnp.zeros_like(sum_ref)
        heads, (after, up0, up1, states) = smalls[:-4], smalls[-4:]
        for part in range(3):
            row = [sum(g[s, part, 0:1] for s in range(g.shape[0])) for g in heads]
            sum_ref[2 + part : 3 + part] = jnp.concatenate(row, axis=1)
        members = small_ref.shape[0]
        cuts = [v.shape[1] // members for v in (up0, up1)]
        segments = [
            v[:, m * cut : (m + 1) * cut] for m in range(members) for v, cut in zip((up0, up1), cuts)
        ]
        per = width // sum(cuts)
        for i in range(members // per):
            sum_ref[8 + i : 9 + i] = jnp.concatenate(segments[2 * per * i : 2 * per * (i + 1)], axis=1)
        for target, source, place, count in (
            (5, after, 2, 1), (6, after, 0, 2), (12, after, 3, 1), (13, states, 0, 4), (17, after, 4, 1)
        ):
            sum_ref[target : target + count] = source[place : place + count]
        load_pieces(me_ref[0], pieces, w_ref, sems, False)

    rows = 256
    gain = vec(small_ref, "g1")
    sum_n = jnp.zeros((1, width), F32)
    sum_e = jnp.zeros((1, width), F32)
    for at in range(0, length, rows):
        rs = slice(at, at + rows)
        whole_g = jnp.concatenate([g[0, :, rs] for g in grads], axis=0)
        e = dot_tt(whole_g, w_ref[...])
        n, r = norm_parts(x_ref[rs].astype(F32))
        eg = e * gain
        part = r * (
            eg - jnp.mean(eg, axis=-1, keepdims=True) - n * jnp.mean(eg * n, axis=-1, keepdims=True)
        )
        sum_n += jnp.sum(e * n, axis=0, keepdims=True)
        sum_e += jnp.sum(e, axis=0, keepdims=True)
        ring_put(ring, at, gh_ref[rs] + part)
    sum_ref[0:1] += sum_n
    sum_ref[1:2] += sum_e
    gx_ref[...] = ring_get(ring, length - shift, length)


def first_back_call(me, shift, grads, x, gh, small, pieces, smalls, deps):
    tokens, width = x.shape
    nseq, _, length = grads[0].shape
    row = pl.BlockSpec((length, width), lambda s: (s, 0))
    return pl.pallas_call(
        lambda *refs: first_back_kernel(len(grads), len(deps), *refs),
        grid=(nseq,),
        in_specs=[
            SMEM, SMEM, row, row, whole(small.shape),
            *(turned_spec(g) for g in grads), *(whole(v.shape) for v in smalls),
            *(ANY for _ in (*pieces, *deps)),
        ],
        out_specs=[row, whole((24, width))],
        out_shape=[
            jax.ShapeDtypeStruct((tokens, width), F32),
            jax.ShapeDtypeStruct((24, width), F32),
        ],
        scratch_shapes=[
            ring_shape(length, width),
            pltpu.VMEM((width, 3 * width), BF),
            pltpu.SemaphoreType.DMA((len(pieces),)),
        ],
        compiler_params=params(62),
        cost_estimate=cost(20),
        name="first_back",
    )(me, shift, x, gh, small, *grads, *smalls, *pieces, *deps)


def states_kernel(mix_ref, e_ref, c_ref, part_ref, sum_ref):
    @pl.when(pl.program_id(0) == 0)
    def _():
        sum_ref[...] = jnp.zeros_like(sum_ref)

    cot = c_ref[...].astype(F32)
    total = None
    for j in range(e_ref.shape[0]):
        e = e_ref[j].astype(F32)
        term = mix_ref[j] * e
        total = term if total is None else total + term
        sum_ref[j : j + 1] += jnp.sum(e * cot, axis=0, keepdims=True)
    part_ref[...] = total


def states_call(mix, earlier, cot):
    states, tokens, width = earlier.shape
    rows = 256
    row = pl.BlockSpec((rows, width), lambda i: (i, 0))
    stack = pl.BlockSpec((states, rows, width), lambda i: (0, i, 0))
    return pl.pallas_call(
        states_kernel,
        grid=(tokens // rows,),
        in_specs=[SMEM, stack, row],
        out_specs=[row, whole((8, width))],
        out_shape=[
            jax.ShapeDtypeStruct((tokens, width), F32),
            jax.ShapeDtypeStruct((8, width), F32),
        ],
        compiler_params=params(62),
        cost_estimate=cost(11),
        name="states",
    )(mix, earlier, cot)


def spread_kernel(mix_ref, c_ref, *refs):
    out = refs[-1]
    cot = c_ref[...].astype(F32)
    for j in range(out.shape[0]):
        out[j] = mix_ref[j] * cot


def spread_call(states, mix, cot, deps):
    tokens, width = cot.shape
    rows = 256
    return pl.pallas_call(
        spread_kernel,
        grid=(tokens // rows,),
        in_specs=[SMEM, pl.BlockSpec((rows, width), lambda i: (i, 0)), *(ANY for _ in deps)],
        out_specs=pl.BlockSpec((states, rows, width), lambda i: (0, i, 0)),
        out_shape=jax.ShapeDtypeStruct((states, tokens, width), F32),
        compiler_params=params(62),
        cost_estimate=cost(20),
        name="spread",
    )(mix, cot, *deps)


def split_kernel(members, shares, wo_ref, wu_ref, wd_ref, *refs):
    outs = refs[-5:]
    outs[0][...] = wo_ref[...]
    deep = wu_ref.shape[1] // members
    base = 0
    for i, share in enumerate(shares):
        for m in range(members):
            outs[1 + i][:, m * share : (m + 1) * share] = wu_ref[:, m * deep + base : m * deep + base + share]
        outs[3 + i][...] = wd_ref[base : base + share]
        base += share


def split_call(members, shares, wo, wu, wd, deps):
    own = wu.shape[0]
    width = wd.shape[1]
    low = [(own, width), *((own, members * v) for v in shares), *((v, width) for v in shares)]
    full = pl.BlockSpec(memory_space=pltpu.VMEM)
    return pl.pallas_call(
        lambda *refs: split_kernel(members, shares, *refs),
        in_specs=[full, full, full, *(ANY for _ in deps)],
        out_specs=[full] * 5,
        out_shape=[jax.ShapeDtypeStruct(shape, BF) for shape in low],
        compiler_params=params(62),
        cost_estimate=cost(3),
        name="split",
    )(wo, wu, wd, *deps)


def mix_kernel(shift_ref, mix_ref, part_ref, b_ref, *refs):
    out_ref, ring = refs[-2:]
    length = b_ref.shape[0]
    ring_put(ring, 0, b_ref[...])
    rolled = ring_get(ring, length - shift_ref[pl.program_id(0)], length)
    out_ref[...] = (part_ref[...] + mix_ref[4] * rolled).astype(BF)


def mix_call(shift, mix, part, block_out, deps):
    tokens, width = part.shape
    nseq = shift.shape[0]
    length = tokens // nseq
    row = pl.BlockSpec((length, width), lambda s: (s, 0))
    return pl.pallas_call(
        mix_kernel,
        grid=(nseq,),
        in_specs=[SMEM, SMEM, row, row, *(ANY for _ in deps)],
        out_specs=row,
        out_shape=jax.ShapeDtypeStruct((tokens, width), BF),
        scratch_shapes=[ring_shape(length, width)],
        compiler_params=params(62),
        cost_estimate=cost(20),
        name="mix",
    )(shift, mix, part, block_out, *deps)


def swap(v, axis, bits):
    size = lax.axis_size(axis)
    return lax.ppermute(v, axis, [(i, i ^ bits) for i in range(size)])


def gate(arrays, deps):
    count = len(arrays)
    return pl.pallas_call(
        lambda *refs: None,
        in_specs=[ANY] * (count + len(deps)),
        out_specs=[ANY] * count,
        out_shape=[jax.ShapeDtypeStruct(v.shape, v.dtype) for v in arrays],
        input_output_aliases={i: i for i in range(count)},
        cost_estimate=cost(0.3),
        name="gate",
    )(*arrays, *deps)


def far_pieces(v):
    return [v, *(swap(v, "shard", 2 * k) for k in range(1, lax.axis_size("shard") // 2))]


def near_pieces(far, own=None):
    pieces = []
    for k, v in enumerate(far):
        pieces += [v, own if own is not None and k == 0 else swap(v, "shard", 1)]
    return pieces


def gather_pieces(v):
    return near_pieces(far_pieces(v))


def in_order(pieces, mine):
    stack = jnp.stack(pieces)
    return [lax.dynamic_index_in_dim(stack, j ^ mine, 0, keepdims=False) for j in range(len(pieces))]


def total_of(terms):
    total = terms[0].astype(F32)
    for term in terms[1:]:
        total = total + term.astype(F32)
    return total


def chain_start(pair):
    keep, send = pair
    return {"keep": keep, "near": swap(send, "shard", 1)}


def step_parts(kind, chain):
    keep, near = chain["keep"], chain["near"]
    chips, sides, groups, n, lanes = keep.shape
    half = (groups, n, lanes)

    def at(side):
        spec = pl.BlockSpec((1, 1, *half), lambda i, idx: (idx[0], side(idx), 0, 0, 0))
        deep = pl.BlockSpec((1, *half), lambda i, idx: (side(idx), 0, 0, 0))
        return [(keep, spec), (near, spec), *((far, deep) for far in chain["far"])]

    def total(refs, group):
        out = None
        for ref in refs:
            piece = ref[(0,) * (len(ref.shape) - 3) + (group,)].astype(F32)
            out = piece if out is None else out + piece
        return out

    if kind == "x":
        ins = []
        for k in range(1, chips):
            spec = pl.BlockSpec((1, sides, *half), lambda i, idx, k=k: (idx[0] ^ k, 0, 0, 0, 0))
            ins += [(keep, spec), (near, spec)]

        def body(idx, ins, outs):
            for k, out in enumerate(outs):
                out[...] = (ins[2 * k][0].astype(F32) + ins[2 * k + 1][0].astype(F32)).astype(BF)

        return ins, [(sides, *half)] * (chips - 1), body
    if kind == "y":

        def body(idx, ins, outs):
            for g in range(groups):
                outs[0][g] = total(ins, g).astype(BF)

        return at(lambda idx: 1 - idx[1]), [half], body
    if kind == "half":
        ins = [(v, whole(v.shape)) for v in (chain["done"], *chain["zg"])]

        def body(idx, ins, outs):
            for k, ref in enumerate(ins):
                outs[0][idx[2] ^ k] = ref[...]

        return ins, [half], body
    ins = [*at(lambda idx: idx[1]), (chain["yr"], whole(half))]
    if kind == "z":

        def body(idx, ins, outs):
            for k, out in enumerate(outs):
                out[...] = total(ins, idx[2] ^ (k + 1)).astype(BF)

        return ins, [(n, lanes)] * (groups - 1), body
    count = len(ins)
    ins += [(v, whole(v.shape)) for v in chain["zr"]]

    def body(idx, ins, outs):
        out = total(ins[:count], idx[2])
        for ref in ins[count:]:
            out = out + ref[...].astype(F32)
        outs[0][...] = out.astype(BF)

    return ins, [(n, lanes)], body


def step_call(idx, steps, deps):
    plans = [step_parts(kind, chain) for kind, chain in steps]
    ins = [pair for plan in plans for pair in plan[0]]
    outs = [shape for plan in plans for shape in plan[1]]

    def kernel(idx_ref, *refs):
        at, out_at = 0, len(ins) + len(deps)
        for some, shapes, body in plans:
            body(idx_ref, refs[at : at + len(some)], refs[out_at : out_at + len(shapes)])
            at += len(some)
            out_at += len(shapes)

    results = pl.pallas_call(
        kernel,
        grid_spec=pltpu.PrefetchScalarGridSpec(
            num_scalar_prefetch=1,
            grid=(1,),
            in_specs=[*(spec for _, spec in ins), *(ANY for _ in deps)],
            out_specs=[whole(shape) for shape in outs],
        ),
        out_shape=[jax.ShapeDtypeStruct(shape, BF) for shape in outs],
        compiler_params=params(62),
        cost_estimate=cost(3),
        name="_".join(["step", *(kind for kind, _ in steps)]),
    )(idx, *(v for v, _ in ins), *deps)
    at = 0
    for (kind, chain), (_, shapes, _) in zip(steps, plans):
        sends = results[at : at + len(shapes)]
        at += len(shapes)
        far = [swap(v, "shard" if kind == "x" else "rep", 2 * (k + 1)) for k, v in enumerate(sends)] if kind in "xz" else None
        if kind == "x":
            chain["far"] = far
        elif kind == "z":
            chain["zr"] = far
        elif kind == "y":
            chain["yr"] = swap(sends[0], "rep", 1)
        elif kind == "half":
            chain["half"] = sends[0]
            chain["twin"] = swap(sends[0], "rep", 1)
        else:
            chain["done"] = sends[0]
            chain["zg"] = [swap(sends[0], "rep", 2 * k) for k in range(1, lax.axis_size("rep") // 2)]
    return results[0]


def finish_call(idx, chains, plans, shapes, deps):
    ins = [v for chain in chains for v in (chain["half"], chain["twin"])]

    def kernel(idx_ref, *refs):
        outs = refs[len(ins) + len(deps) : len(ins) + len(deps) + len(shapes)]
        scratch = refs[-len(chains) :]
        for c, plan in enumerate(plans):
            both = scratch[c]
            both[idx_ref[1]] = refs[2 * c][...]
            both[1 - idx_ref[1]] = refs[2 * c + 1][...]
            sides, groups = both.shape[:2]
            at = 0
            for out, own, cols, place in plan:
                rows, wide = own // groups, cols // sides
                for j in range(wide // 128):
                    for side in range(sides):
                        for group in range(groups):
                            row, col = place(group * rows, side * wide + j * 128)
                            outs[out][row : row + rows, col : col + 128] = both[
                                side, group, at : at + rows, :
                            ].astype(F32)
                    at += rows

    return pl.pallas_call(
        kernel,
        in_specs=[SMEM, *(pl.BlockSpec(memory_space=pltpu.VMEM) for _ in ins), *(ANY for _ in deps)],
        out_specs=[pl.BlockSpec(memory_space=pltpu.VMEM) for _ in shapes],
        out_shape=[jax.ShapeDtypeStruct(shape, F32) for shape in shapes],
        scratch_shapes=[pltpu.VMEM((2, *chain["half"].shape), BF) for chain in chains],
        compiler_params=params(62),
        cost_estimate=cost(4),
        name="finish",
    )(idx, *ins, *deps)


def reduce_plain(packed):
    flat = packed.reshape(-1, 128)
    return lax.psum(lax.psum_scatter(flat, "shard", scatter_dimension=0, tiled=True), "rep")[None, None]


def reduce_small(v):
    for axis in ("shard", "rep"):
        bits = 1
        while bits < lax.axis_size(axis):
            v = v + swap(v, axis, bits)
            bits *= 2
    return v


def shards(
    inputs, earlier, segments, cotangent, mix_weights,
    ln1_gain, ln1_bias, qkv_weight, qkv_bias, out_weight, out_bias,
    ln2_gain, ln2_bias, up_weight, up_bias, down_weight, down_bias,
):
    nseq, length = segments.shape
    width = inputs.shape[1]
    blk = length // 2
    members, replicas = lax.axis_size("shard"), lax.axis_size("rep")
    me = lax.axis_index("shard").astype(jnp.int32)
    rep = lax.axis_index("rep").astype(jnp.int32)
    side = rep % 2
    me_ref = me[None]
    idx = jnp.stack([me // 2, side, rep // 2])
    own = width // members
    deep = down_weight.shape[0]
    ff = deep * members
    shares = [2 * deep // 3, deep - 2 * deep // 3]
    fits = own % (8 * replicas) == 0 and all(v % (8 * replicas) == 0 and v % 128 == 0 for v in shares)
    form = (2, replicas // 2) if fits else (1, 1)

    wqkv = far_pieces(qkv_weight)
    wqkv_near = swap(qkv_weight, "shard", 1)
    vectors = [ln1_gain, ln1_bias, qkv_bias, out_bias, ln2_gain, ln2_bias, up_bias, down_bias]
    sizes = [v.shape[0] for v in vectors]
    wide = max(sizes)
    small = jnp.stack([jnp.pad(v, (0, wide - v.shape[0])) for v in vectors])
    small = [small, *(swap(small, "shard", k) for k in range(1, members))]
    small = jnp.stack(in_order(small, me))

    part, sums3 = states_call(mix_weights, earlier, cotangent)
    inv = np.exp(np.arange(HEAD // 2) * (-math.log(10000.0) / (HEAD // 2)))
    angles = np.arange(length)[None, :] * inv[:, None]
    tables = jnp.asarray(np.stack([np.cos(angles), np.sin(angles)]), F32)
    shift, xr, cr, act, seg, cos, sin = roll_call(inputs, cotangent, segments, small, tables, [sums3])
    if any(v % 128 for v in (deep, *shares)):

        def shared(v):
            halves = jnp.split(v.reshape(v.shape[0], members, deep), [shares[0]], axis=-1)
            return [h.reshape(v.shape[0], -1) for h in halves]

        pieces = [out_weight, *shared(up_weight), down_weight[: shares[0]], down_weight[shares[0] :]]
    else:
        pieces = split_call(members, shares, out_weight, up_weight, down_weight, [act, *wqkv])
    wo, wu0, wu1 = [lax.all_gather(v, "shard", axis=0, tiled=True) for v in pieces[:3]]
    wd0 = far_pieces(pieces[3])

    wqkv = near_pieces([qkv_weight, *gate(wqkv[1:], [act])], wqkv_near)
    q, k, v = qkv_call(me_ref, act, small, cos, sin, wqkv)
    wd0 = near_pieces(gate(wd0, [q]))
    o, lse = attend_call(seg, q, k, v)
    wd1 = far_pieces(*gate(pieces[4:], [lse]))
    values = {"me": me_ref, "mix": mix_weights, "small": small, "x": xr, "cot": cr, "a": o, "wo": wo}
    got = mlp_call(0, shares[0], True, False, values | {"wu_in": wu0, "wd": wd0}, form, members, [])
    values |= {"up_in": got["up"], "back_in": got["back"], "hid": got["hid"], "act": got["act"]}
    wd1 = near_pieces(gate(wd1, [got["dbu"]]))
    first, dbu = [got[name] for name in ("dw0", "dw1") if name in got], [got["dbu"]]
    spread = [earlier.shape[0], mix_weights, cotangent]
    if fits:
        early = chain_start(first)
        earlier_grad = spread_call(*spread, [first[0]])
        deps = [step_call(idx, [("x", early)], [earlier_grad])]
    else:
        earlier_grad, deps = spread_call(*spread, []), []
    got = mlp_call(
        shares[0], shares[1], False, True, values | {"wu_in": wu1, "wd": wd1}, form, members, deps
    )
    second = [got[name] for name in ("dw0", "dw1") if name in got]
    dbu.append(got["dbu"])
    block_out, gh, ga, sums2 = (got[name] for name in ("up", "gh", "ga", "sum"))

    groups = width // PAIR // 2
    back = [seg, q, k, v, o, ga, lse, cos, sin]

    def up_place(base, share):
        def place(row, col):
            return row, col // share * deep + base + col % share

        return place

    if fits:
        late = chain_start(second)
        t = step_call(idx, [("y", early)], [late["keep"]])
        gs = [attend_back_call(*back, 0, 2, [t])]
        t = step_call(idx, [("z", early), ("x", late)], [gs[0][0]])
        gs.append(attend_back_call(*back, 2, 2, [t]))
        t = step_call(idx, [("sum", early)], [gs[1][0]])
        for i in range(2, groups):
            gs.append(attend_back_call(*back, 2 * i, 2, [t, gs[-1][0]], 0.5))
        early["zg"] = gate(early["zg"], [gs[-1][0]])
        t = step_call(idx, [("y", late)], [gs[-1][0]])
        smalls = [*(g[3] for g in gs), sums2, *dbu, sums3]
        grads = [g[i] for i in range(3) for g in gs]
        pack = qkv_grad_call(me_ref, grads, act, form, members, [t])
        tail = chain_start(pack)
        t = step_call(idx, [("half", early), ("z", late)], [pack[0]])
        output = mix_call(shift, mix_weights, part, block_out, [t])
        t = step_call(idx, [("x", tail)], [output])
        input_grad, sums = first_back_call(me_ref, shift, grads, xr, gh, small, wqkv, smalls, [t])
        t = step_call(idx, [("sum", late), ("y", tail)], [sums])
        t = step_call(idx, [("half", late), ("z", tail)], [])
        t = step_call(idx, [("sum", tail)], [])
        d_up, d_down, d_out = finish_call(
            idx,
            [early, late],
            [
                [
                    (0, own, shares[0] * members, up_place(0, shares[0])),
                    (1, shares[0], width, lambda row, col: (row, col)),
                ],
                [
                    (0, own, shares[1] * members, up_place(shares[0], shares[1])),
                    (1, shares[1], width, lambda row, col: (row + shares[0], col)),
                    (2, own, width, lambda row, col: (row, col)),
                ],
            ],
            [(own, ff), (deep, width), (own, width)],
            [t],
        )
        t = step_call(idx, [("half", tail)], [d_out])
        (d_qkv,) = finish_call(
            idx, [tail], [[(0, own, 3 * width, lambda row, col: (row, col))]], [(own, 3 * width)], []
        )
    else:
        gs = [attend_back_call(*back, 2 * i, 2, []) for i in range(groups)]
        smalls = [*(g[3] for g in gs), sums2, *dbu, sums3]
        grads = [g[i] for i in range(3) for g in gs]
        pack = qkv_grad_call(me_ref, grads, act, form, members, [])
        output = mix_call(shift, mix_weights, part, block_out, [])
        input_grad, sums = first_back_call(me_ref, shift, grads, xr, gh, small, wqkv, smalls, [])
        ups, downs = [], []
        first, second, third = [reduce_plain(p[0]) for p in (first, second, pack)]
        for v, share in ((first, shares[0]), (second, shares[1])):
            at = packed_rows(own, share * members, *v.shape[:2])
            ups.append(unpack(v, 0, own, share * members).reshape(own, members, share))
            downs.append(unpack(v, at, share, width))
            at += packed_rows(share, width, *v.shape[:2])
        d_out = unpack(second, at, own, width).astype(F32)
        d_up = jnp.concatenate(ups, axis=2).reshape(own, -1).astype(F32)
        d_down = jnp.concatenate(downs, axis=0).astype(F32)
        d_qkv = unpack(third, 0, own, 3 * width).astype(F32)

    parts, at = [], 0
    flat = reduce_small(sums).reshape(-1)
    for size in sizes:
        parts.append(lax.dynamic_slice(flat, (at + me * size,), (size,)))
        at += size * members
    mix_grad = jnp.sum(flat[at : at + 5 * width].reshape(5, width), axis=1)
    return (
        output, input_grad, earlier_grad, mix_grad,
        parts[0], parts[1], d_qkv, parts[2], d_out, parts[3], parts[4], parts[5],
        d_up, parts[6], d_down, parts[7],
    )


def solution(mesh):
    rows, shard = P(("rep", "shard"), None), P("shard")
    mat, deep = P("shard", None), P(None, ("rep", "shard"), None)
    return jax.shard_map(
        shards,
        mesh=mesh,
        in_specs=(
            rows, deep, rows, rows, P(),
            shard, shard, mat, shard, mat, shard, shard, shard, mat, shard, mat, shard,
        ),
        out_specs=(
            rows, rows, deep, P(),
            shard, shard, mat, shard, mat, shard, shard, shard, mat, shard, mat, shard,
        ),
        check_vma=False,
    )
```

```python
import math

import jax
import jax.numpy as jnp
import numpy as np
from jax import lax
from jax.experimental import pallas as pl
from jax.experimental.pallas import tpu as pltpu
from jax.sharding import PartitionSpec as P

HEADS = 12
HEAD = 64
PAIR = 2 * HEAD
EPSILON = 1e-05
LOG2E = math.log2(math.e)
NEG = -1e30
GELU_A = math.sqrt(2.0 / math.pi)
GELU_B = GELU_A * 0.044715
BF = jnp.bfloat16
F32 = jnp.float32
MIB = 1 << 20

COST_SHARE = 1.5


def cost(us):
    return pl.CostEstimate(flops=int(us * COST_SHARE * 1.15e9), bytes_accessed=1024, transcendentals=0)


def dot_nn(a, b):
    return lax.dot_general(a, b, (((1,), (0,)), ((), ())), preferred_element_type=F32)


def dot_nt(a, b):
    return lax.dot_general(a, b, (((1,), (1,)), ((), ())), preferred_element_type=F32)


def dot_tn(a, b):
    return lax.dot_general(a, b, (((0,), (0,)), ((), ())), preferred_element_type=F32)


def dot_tt(a, b):
    return lax.dot_general(a, b, (((0,), (1,)), ((), ())), preferred_element_type=F32)


def params(vmem):
    return pltpu.CompilerParams(vmem_limit_bytes=vmem * MIB)


ANY = pl.BlockSpec(memory_space=pl.ANY)


def load_pieces(me, pieces, target, sems, start, cols=None):
    copies = []
    for j, piece in enumerate(pieces):
        rows = piece.shape[0]
        at = pl.multiple_of((me ^ j) * rows, rows)
        source = piece if cols is None else piece.at[:, cols]
        copies.append(pltpu.make_async_copy(source, target.at[pl.ds(at, rows), :], sems.at[j]))
    for copy in copies:
        if start:
            copy.start()
        else:
            copy.wait()


def pack(target, source, base, own, sides, groups, at):
    rows, cols = own // groups, source.shape[-1] // sides
    for side in range(sides):
        for group in range(groups):
            for j in range(cols // 128):
                here = at + j * rows
                col = side * cols + j * 128
                target[side, group, here : here + rows, :] = source[
                    pl.ds(base + group * rows, rows), col : col + 128
                ].astype(BF)


def pack_all(targets, me, source, own, at):
    for t, target in enumerate(targets):
        count, sides, groups = target.shape[:3]
        for i in range(count):
            place = i if len(targets) == 1 else 2 * i + ((me % 2) ^ t)
            pack(target.at[i], source, pl.multiple_of(place * own, own), own, sides, groups, at)


def unpack(v, at, own, cols):
    sides, groups = v.shape[:2]
    rows, wide = own // groups, cols // sides
    count = wide // 128
    part = v[:, :, at : at + rows * count].reshape(sides, groups, count, rows, 128)
    return part.transpose(1, 3, 0, 2, 4).reshape(own, cols)


def packed_rows(own, cols, sides, groups):
    return own * cols // (128 * sides * groups)


def packed_shapes(form, members, own_cols):
    sides, groups = form
    n = sum(packed_rows(own, cols, sides, groups) for own, cols in own_cols)
    split = 1 if form == (1, 1) else 2
    shape = (members // split, sides, groups, n, 128)
    return [(whole(shape), jax.ShapeDtypeStruct(shape, BF)) for _ in range(split)]


def whole(shape):
    zeros = (0,) * len(shape)
    return pl.BlockSpec(shape, lambda *_: zeros, pipeline_mode=pl.Buffered(1))


SMEM = pl.BlockSpec(memory_space=pltpu.SMEM)


def ring_shape(length, width):
    return pltpu.VMEM((width // 128, 2 * length, 128), F32)


def ring_put(ring, at, value):
    for j in range(ring.shape[0]):
        part = value[:, j * 128 : (j + 1) * 128]
        ring[j, pl.ds(at, value.shape[0]), :] = part
        ring[j, pl.ds(ring.shape[1] // 2 + at, value.shape[0]), :] = part


def ring_get(ring, start, rows):
    return jnp.concatenate([ring[j, pl.ds(start, rows), :] for j in range(ring.shape[0])], axis=1)


def norm_parts(v):
    mean = jnp.mean(v, axis=-1, keepdims=True)
    centred = v - mean
    var = jnp.mean(centred * centred, axis=-1, keepdims=True)
    r = lax.rsqrt(var + EPSILON)
    return centred * r, r


ROWS = ("g1", "b1", "bqkv", "bo", "g2", "b2", "bu", "bd")


def vec(ref, name, base=0, share=None):
    row = ROWS.index(name)
    size = share or ref.shape[2] // DEEP_ROWS[name]
    parts = [ref[m, row : row + 1, base : base + size] for m in range(ref.shape[0])]
    return jnp.concatenate(parts, axis=1).astype(F32)


DEEP_ROWS = {"g1": 4, "b1": 4, "bo": 4, "g2": 4, "b2": 4, "bd": 4, "bu": 1}


def column(row):
    return jnp.broadcast_to(row, (128, row.shape[1])).T[:, :1]


def roll_kernel(x_ref, cot_ref, seg_ref, small_ref, tab_ref, *refs):
    shift_ref, xr_ref, cr_ref, act_ref, seg_out, cos_ref, sin_ref, ring = refs[-8:]
    length = x_ref.shape[0]
    half = length // 2
    seg = jnp.broadcast_to(seg_ref[0].astype(F32), (8, length))
    place = lax.broadcasted_iota(jnp.int32, (8, length), 1)
    same = (seg == pltpu.roll(seg, length - (half - 1), 1)) & (place <= half)
    shift = jnp.min(jnp.where(same, place.astype(F32), float(length))).astype(jnp.int32)
    shift_ref[pl.program_id(0)] = shift
    back = lax.rem(length - shift, length)
    seg_out[0] = pltpu.roll(seg, back, 1)[:, half:]
    cos_ref[0] = pltpu.roll(tab_ref[0], back, 1)
    sin_ref[0] = pltpu.roll(tab_ref[1], back, 1)
    for source, target in ((cot_ref, cr_ref), (x_ref, xr_ref)):
        ring_put(ring, 0, source[...].astype(F32))
        target[...] = ring_get(ring, shift, length).astype(BF)
    gain, bias = vec(small_ref, "g1"), vec(small_ref, "b1")
    rows = 256
    for at in range(0, length, rows):
        n, _ = norm_parts(xr_ref[at : at + rows].astype(F32))
        act_ref[at : at + rows] = (n * gain + bias).astype(BF)


def roll_call(x, cot, seg, small, tables, deps):
    tokens, width = x.shape
    nseq, length = seg.shape
    row = pl.BlockSpec((length, width), lambda s: (s, 0))
    tab = pl.BlockSpec((1, HEAD // 2, length), lambda s: (s, 0, 0))
    low = jax.ShapeDtypeStruct((tokens, width), BF)
    turn = jax.ShapeDtypeStruct((nseq, HEAD // 2, length), F32)
    return pl.pallas_call(
        roll_kernel,
        grid=(nseq,),
        in_specs=[
            row, row, pl.BlockSpec((1, 1, length), lambda s: (s, 0, 0)), whole(small.shape), whole(tables.shape),
            *(ANY for _ in deps),
        ],
        out_specs=[SMEM, row, row, row, pl.BlockSpec((1, 8, length // 2), lambda s: (s, 0, 0)), tab, tab],
        out_shape=[
            jax.ShapeDtypeStruct((nseq,), jnp.int32), low, low, low,
            jax.ShapeDtypeStruct((nseq, 8, length // 2), F32), turn, turn,
        ],
        scratch_shapes=[ring_shape(length, width)],
        compiler_params=params(62),
        cost_estimate=cost(10),
        name="roll",
    )(x, cot, seg[:, None, :], small, tables, *deps)


def qkv_kernel(me_ref, act_ref, small_ref, cos_ref, sin_ref, *refs):
    pieces, (out_ref, w_ref, sems) = refs[:-3], refs[-3:]
    width = act_ref.shape[1]
    half = HEAD // 2
    rows = 256
    bias = vec(small_ref, "bqkv", 0, 3 * width // small_ref.shape[0])

    def load(part, start):
        cols = slice(part * width, (part + 1) * width)
        load_pieces(me_ref[0], pieces, w_ref.at[part], sems.at[part], start, cols)

    @pl.when((pl.program_id(0) == 0) & (pl.program_id(1) == 0))
    def _():
        for part in range(3):
            load(part, True)

    def project(part):
        @pl.when(pl.program_id(0) == 0)
        def _():
            load(part, False)

        cos, sin = cos_ref[0], sin_ref[0]
        for base in range(0, width, rows):
            cols = slice(base, base + rows)
            at = part * width + base
            y = dot_tt(w_ref[part, :, cols], act_ref[...]) + column(bias[:, at : at + rows])
            if part == 2:
                out_ref[0, base : base + rows, :] = y.astype(BF)
                continue
            for h in range(0, rows, HEAD):
                u, w = y[h : h + half], y[h + half : h + HEAD]
                a, b = u * cos - w * sin, w * cos + u * sin
                if part == 0:
                    a, b = a * (LOG2E * HEAD**-0.5), b * (LOG2E * HEAD**-0.5)
                out_ref[0, base + h : base + h + half, :] = a.astype(BF)
                out_ref[0, base + h + half : base + h + HEAD, :] = b.astype(BF)

    for part in range(3):
        pl.when(pl.program_id(1) == part)(lambda part=part: project(part))


def qkv_call(me, act, small, cos, sin, pieces):
    tokens, width = act.shape
    nseq, _, length = cos.shape
    tab = pl.BlockSpec((1, HEAD // 2, length), lambda s, p: (s, 0, 0))
    return pl.pallas_call(
        qkv_kernel,
        grid=(nseq, 3),
        in_specs=[
            SMEM, pl.BlockSpec((length, width), lambda s, p: (s, 0)), whole(small.shape), tab, tab,
            *(ANY for _ in pieces),
        ],
        out_specs=pl.BlockSpec((1, None, width, length), lambda s, p: (s, p, 0, 0)),
        out_shape=jax.ShapeDtypeStruct((nseq, 3, width, length), BF),
        scratch_shapes=[
            pltpu.VMEM((3, width, width), BF),
            pltpu.SemaphoreType.DMA((3, len(pieces))),
        ],
        compiler_params=params(62),
        cost_estimate=cost(15),
        name="qkv",
    )(me, act, small, cos, sin, *pieces)


def head_specs(base):
    return [
        lambda length, part=part: pl.BlockSpec((1, None, PAIR, length), lambda s, h: (s, part, base + h, 0))
        for part in range(3)
    ]


def fill_masks(seg_ref, mask, blk):
    row = seg_ref[0, 0:1, :]
    col = column(row)
    kk = lax.broadcasted_iota(jnp.int32, (blk, blk), 0)
    qq = lax.broadcasted_iota(jnp.int32, (blk, blk), 1)
    causal = kk <= qq
    mask[0] = jnp.where(causal, 0.0, NEG)
    for i, (kb, qb) in enumerate(((0, 0), (0, 1), (1, 1))):
        same = col[kb * blk : (kb + 1) * blk] == row[:, qb * blk : (qb + 1) * blk]
        keep = same if kb != qb else same & causal
        mask[1 + i] = jnp.where(keep, 0.0, NEG)


def scores_of(keys, query, mask, half, qb, blk):
    top = dot_nn(keys[: (qb + 1) * blk], query)
    if half == 0:
        diag = top[qb * blk :] + mask[0]
        return diag if qb == 0 else jnp.concatenate([top[:blk], diag], axis=0)
    if qb == 0:
        return top + mask[1]
    return jnp.concatenate([top[:blk] + mask[2], top[blk:] + mask[3]], axis=0)


def one_head(pair_rows, head):
    zero = jnp.zeros((HEAD, pair_rows.shape[1]), pair_rows.dtype)
    rows = pair_rows[head * HEAD : (head + 1) * HEAD]
    return jnp.concatenate([rows, zero] if head == 0 else [zero, rows], axis=0)


def attend_kernel(seg_ref, q_ref, k_ref, v_ref, o_ref, l_ref, mask):
    length = q_ref.shape[2]
    blk = length // 4

    @pl.when(pl.program_id(1) == 0)
    def _():
        fill_masks(seg_ref, mask, blk)

    units = [(half, head, qb) for qb in range(2) for half in range(2) for head in range(2)]
    keys = [k_ref[0, :, half * 2 * blk : (half + 1) * 2 * blk].T for half in range(2)]

    def place(half, head, qb):
        base = half * 2 * blk
        qs = slice(base + qb * blk, base + (qb + 1) * blk)
        return base, qs, slice(head * HEAD, (head + 1) * HEAD)

    scores = []
    for half, head, qb in units:
        _, qs, _ = place(half, head, qb)
        scores.append(scores_of(keys[half], one_head(q_ref[0, :, qs], head), mask, half, qb, blk))
    tops = [jnp.max(s, axis=0, keepdims=True) for s in scores]
    probs = [jnp.exp2(s - top) for s, top in zip(scores, tops)]
    totals = [jnp.sum(p, axis=0, keepdims=True) for p in probs]
    lows = [p.astype(BF) for p in probs]
    for (half, head, qb), p, top, total in zip(units, lows, tops, totals):
        base, qs, hs = place(half, head, qb)
        o = dot_nn(v_ref[0, hs, base : base + (qb + 1) * blk], p)
        o_ref[0, hs, qs] = (o / total).astype(BF)
        l_ref[0, 0, head : head + 1, qs] = top + jnp.log2(total)


def attend_call(seg, qkv):
    nseq, _, width, length = qkv.shape
    pairs = width // PAIR
    blk = length // 4
    blockspec = pl.BlockSpec((1, PAIR, length), lambda s, h: (s, h, 0))
    return pl.pallas_call(
        attend_kernel,
        grid=(nseq, pairs),
        in_specs=[
            pl.BlockSpec((1, 8, 2 * blk), lambda s, h: (s, 0, 0)),
            *(spec(length) for spec in head_specs(0)),
        ],
        out_specs=[blockspec, pl.BlockSpec((1, 1, 2, length), lambda s, h: (s, h, 0, 0))],
        out_shape=[
            jax.ShapeDtypeStruct((nseq, width, length), BF),
            jax.ShapeDtypeStruct((nseq, pairs, 2, length), F32),
        ],
        scratch_shapes=[pltpu.VMEM((4, blk, blk), F32)],
        compiler_params=params(62),
        cost_estimate=cost(30),
        name="attend",
    )(seg, qkv, qkv, qkv)


def attend_back_kernel(
    seg_ref, q_ref, k_ref, v_ref, o_ref, g_ref, l_ref, cos_ref, sin_ref, *refs
):
    gq_ref, gk_ref, gv_ref, sum_ref, mask, turn = refs[-6:]
    length = q_ref.shape[2]
    blk = length // 4
    hd = HEAD // 2

    @pl.when(pl.program_id(1) == 0)
    def _():
        fill_masks(seg_ref, mask, blk)

    units = [(half, head, qb) for qb in range(2) for half in range(2) for head in range(2)]
    keys = [k_ref[0, :, half * 2 * blk : (half + 1) * 2 * blk].T for half in range(2)]
    values = [v_ref[0, :, half * 2 * blk : (half + 1) * 2 * blk].T for half in range(2)]

    def place(half, head, qb):
        base = half * 2 * blk
        qs = slice(base + qb * blk, base + (qb + 1) * blk)
        return base, qs, slice(head * HEAD, (head + 1) * HEAD)

    def products(unit):
        half, head, qb = unit
        _, qs, hs = place(*unit)
        s = scores_of(keys[half], one_head(q_ref[0, :, qs], head), mask, half, qb, blk)
        gp = dot_nn(values[half][: (qb + 1) * blk], one_head(g_ref[0, :, qs], head))
        g = g_ref[0, hs, qs].astype(F32) * o_ref[0, hs, qs].astype(F32)
        return s, gp, jnp.sum(g, axis=0, keepdims=True)

    def softmax(unit, held):
        s, gp, delta = held
        _, qs, _ = place(*unit)
        p = jnp.exp2(s - l_ref[0, 0, unit[1] : unit[1] + 1, qs])
        return p.astype(BF), (p * (gp - delta)).astype(BF)

    def finish(unit, pair):
        half, head, qb = unit
        p, ds = pair
        base, qs, hs = place(*unit)
        dv = dot_nt(g_ref[0, hs, qs], p)
        dk = dot_nt(q_ref[0, hs, qs], ds)
        turn[0, hs, qs] = dot_nn(k_ref[0, hs, base : base + (qb + 1) * blk], ds)
        first_half, second_half = slice(base, base + blk), slice(base + blk, base + 2 * blk)
        if qb == 0:
            turn[1, hs, first_half], turn[2, hs, first_half] = dk, dv
        else:
            turn[1, hs, first_half] += dk[:, :blk]
            turn[2, hs, first_half] += dv[:, :blk]
            turn[1, hs, second_half], turn[2, hs, second_half] = dk[:, blk:], dv[:, blk:]

    before = None
    for unit in (*units, None):
        held = products(unit) if unit else None
        if before:
            finish(before[0], softmax(*before))
        before = (unit, held)
    cos, sin = cos_ref[0], sin_ref[0]

    ones = jnp.ones((8, length), BF)
    for part, (out, scale) in enumerate(((gq_ref, HEAD**-0.5), (gk_ref, 1.0 / LOG2E), (gv_ref, 1.0))):
        for head in range(2):
            at = head * HEAD
            u = turn[part, at : at + hd]
            w = turn[part, at + hd : at + HEAD]
            if part < 2:
                u, w = (u * cos + w * sin) * scale, (w * cos - u * sin) * scale
            out[0, at : at + hd, :] = u.astype(BF)
            out[0, at + hd : at + HEAD, :] = w.astype(BF)
        sum_ref[0, part] = dot_nt(ones, out[0])


def attend_back_call(seg, qkv, o, g, lse, cos, sin, base, pairs, deps, us=15):
    nseq, _, _, length = qkv.shape
    blk = length // 4
    source = pl.BlockSpec((1, PAIR, length), lambda s, h: (s, base + h, 0))
    target = pl.BlockSpec((1, PAIR, length), lambda s, h: (s, h, 0))
    tab = pl.BlockSpec((1, HEAD // 2, length), lambda s, h: (s, 0, 0))
    turned = jax.ShapeDtypeStruct((nseq, pairs * PAIR, length), BF)
    return pl.pallas_call(
        attend_back_kernel,
        grid=(nseq, pairs),
        in_specs=[
            pl.BlockSpec((1, 8, 2 * blk), lambda s, h: (s, 0, 0)),
            *(spec(length) for spec in head_specs(base)), source, source,
            pl.BlockSpec((1, 1, 2, length), lambda s, h: (s, base + h, 0, 0)),
            tab, tab, *(ANY for _ in deps),
        ],
        out_specs=[
            target, target, target,
            pl.BlockSpec((1, 3, 8, PAIR), lambda s, h: (s, 0, 0, h)),
        ],
        out_shape=[turned, turned, turned, jax.ShapeDtypeStruct((nseq, 3, 8, pairs * PAIR), F32)],
        scratch_shapes=[pltpu.VMEM((4, blk, blk), F32), pltpu.VMEM((3, PAIR, length), F32)],
        compiler_params=params(62),
        cost_estimate=cost(us),
        name="attend_back",
    )(seg, qkv, qkv, qkv, o, g, lse, cos, sin, *deps)


def mlp_kernel(base, first, last, names, members, *refs):
    ref = dict(zip(names, refs))
    rows, width = ref["cot"].shape
    step = pl.program_id(0)
    final = pl.num_programs(0) - 1
    acc_u, acc_d, low = ref["acc_u"], ref["acc_d"], ref["low"]
    span = acc_u.shape[1]
    me, sems = ref["me"][0], ref["sems"]
    share = span // members
    small = ref["small"]

    def weights(start):
        for i, name in enumerate(("wu", "wd")):
            pieces = [ref[key] for key in ref if key[0] == name]
            load_pieces(me if len(pieces) > 1 else 0, pieces, ref[name], sems.at[i], start)

    @pl.when(step == 0)
    def _():
        weights(True)
        acc_u[...] = jnp.zeros_like(acc_u)
        acc_d[...] = jnp.zeros_like(acc_d)
        ref["dbu"][...] = jnp.zeros_like(ref["dbu"])

    alpha = ref["mix"][4]
    cot = ref["cot"][...].astype(F32)
    g_out = cot * alpha
    low[...] = g_out.astype(BF)
    if first:
        hidden = ref["x"][...].astype(F32) + dot_tn(ref["a"][0], ref["wo"][...]) + vec(small, "bo")
        n, _ = norm_parts(hidden)
        ref["hid"][...] = hidden
        ref["act"][...] = (n * vec(small, "g2") + vec(small, "b2")).astype(BF)

    @pl.when(step == 0)
    def _():
        weights(False)

    act2 = ref["act"]
    if first:
        total_up = ref["hid"][...] + vec(small, "bd")
        total_back = None
    else:
        total_up, total_back = ref["up_in"][...], ref["back_in"][...]
    chunk = width + width // 3
    bu = vec(small, "bu", base, share)
    for at in range(0, span, chunk):
        cols = slice(at, at + chunk)
        wu, wd = ref["wu"][:, cols], ref["wd"][cols, :]
        pre = dot_nn(act2[...], wu) + bu[:, cols]
        g_act = dot_nt(low[...], wd)
        square = pre * pre
        h = 0.5 + 0.5 * jnp.tanh(pre * (GELU_A + GELU_B * square))
        act = (pre * h).astype(BF)
        slope = h + (pre * (h * (1.0 - h))) * (2.0 * GELU_A + 6.0 * GELU_B * square)
        g_pre = g_act * slope
        ref["dbu"][:, cols] += jnp.sum(g_pre, axis=0, keepdims=True)
        g_low = g_pre.astype(BF)
        total_up = total_up + dot_nn(act, wd)
        more = dot_nt(g_low, wu)
        total_back = more if total_back is None else total_back + more
        acc_d[cols, :] += dot_tn(act, low[...])
        acc_u[:, cols] += dot_tn(act2[...], g_low)
    ref["up"][...] = total_up
    if not last:
        ref["back"][...] = total_back
    else:
        e = total_back
        gain = vec(small, "g2")
        n, r = norm_parts(ref["hid"][...])
        eg = e * gain
        part = r * (
            eg - jnp.mean(eg, axis=-1, keepdims=True) - n * jnp.mean(eg * n, axis=-1, keepdims=True)
        )
        g_hidden = g_out + part
        ref["gh"][...] = g_hidden
        g_low = g_hidden.astype(BF)

        @pl.when(step == 0)
        def _():
            ref["sum"][...] = jnp.zeros_like(ref["sum"])
            ref["acc_o"][...] = jnp.zeros_like(ref["acc_o"])

        for i, term in enumerate((e * n, e, g_hidden, g_out, total_up * cot)):
            ref["sum"][i : i + 1, :] += jnp.sum(term, axis=0, keepdims=True)
        ref["acc_o"][...] += dot_nn(ref["a"][0], g_low)
        ref["ga"][0] = dot_nt(ref["wo"][...], g_low).astype(BF)

    @pl.when(step == final)
    def _():
        targets = [ref[name] for name in ("dw0", "dw1") if name in ref]
        sides, groups = targets[0].shape[1:3]
        at = 0
        for source in (acc_u, acc_d, ref["acc_o"]) if last else (acc_u, acc_d):
            own = source.shape[0] // members
            pack_all(targets, me, source, own, at)
            at += packed_rows(own, source.shape[1], sides, groups)


def mlp_call(base, share, first, last, values, form, members, deps):
    tokens, width = values["cot"].shape
    nseq, _, length = values["a"].shape
    span = share * members
    rows = length // 2
    row = pl.BlockSpec((rows, width), lambda i: (i, 0))
    col = pl.BlockSpec((1, width, rows), lambda i: (i // 2, 0, i % 2))
    f32row = jax.ShapeDtypeStruct((tokens, width), F32)
    ins = {
        "me": SMEM,
        "mix": SMEM,
        "cot": row,
        "small": whole(values["small"].shape),
    }
    parts = [(width // members, span), (span // members, width)]
    if last:
        parts.append((width // members, width))
    outs = {f"dw{i}": pair for i, pair in enumerate(packed_shapes(form, members, parts))}
    outs |= {
        "dbu": (whole((1, span)), jax.ShapeDtypeStruct((1, span), F32)),
        "up": (row, f32row),
    }
    scratch = {
        "acc_u": pltpu.VMEM((width, span), F32),
        "acc_d": pltpu.VMEM((span, width), F32),
        "low": pltpu.VMEM((rows, width), BF),
        "wu": pltpu.VMEM((width, span), BF),
        "wd": pltpu.VMEM((span, width), BF),
        "sems": pltpu.SemaphoreType.DMA((2, members)),
    }
    if first:
        ins |= {"x": row}
        outs |= {"hid": (row, f32row), "act": (row, jax.ShapeDtypeStruct((tokens, width), BF))}
    else:
        ins |= {"act": row, "up_in": row, "back_in": row}
    if last:
        ins |= {"hid": row}
        outs |= {
            "gh": (row, f32row),
            "ga": (col, jax.ShapeDtypeStruct(values["a"].shape, BF)),
            "sum": (whole((8, width)), jax.ShapeDtypeStruct((8, width), F32)),
        }
        scratch |= {"acc_o": pltpu.VMEM((width, width), F32)}
    else:
        outs |= {"back": (row, f32row)}
    if first or last:
        ins |= {"a": col, "wo": whole((width, width))}
    pieces = {(name, j): piece for name in ("wu", "wd") for j, piece in enumerate(values[name])}
    names = [*ins, *pieces, *(("dep", i) for i in range(len(deps))), *outs, *scratch]
    result = pl.pallas_call(
        lambda *refs: mlp_kernel(base, first, last, names, members, *refs),
        grid=(tokens // rows,),
        in_specs=[*ins.values(), *(ANY for _ in (*pieces, *deps))],
        out_specs=[spec for spec, _ in outs.values()],
        out_shape=[shape for _, shape in outs.values()],
        scratch_shapes=list(scratch.values()),
        compiler_params=params(62),
        cost_estimate=cost(45),
        name="mlp",
    )(*(values[name] for name in ins), *pieces.values(), *deps)
    return dict(zip(outs, result))


def qkv_grad_kernel(parts, deps, me_ref, act_ref, *refs):
    grads, targets, acc = refs[:parts], refs[parts + deps : -1], refs[-1]
    step = pl.program_id(0)
    last = pl.num_programs(0) - 1
    width = act_ref.shape[1]
    at = 0
    for g in grads:
        cols = slice(at, at + g.shape[1])
        at += g.shape[1]
        term = dot_tt(act_ref[...], g[0])
        acc[:, cols] = jnp.where(step == 0, term, acc[:, cols] + term)

    @pl.when(step == last)
    def _():
        split = len(targets)
        pack_all(targets, me_ref[0], acc, width // (targets[0].shape[0] * split), 0)


def turned_spec(v):
    return pl.BlockSpec((1, *v.shape[1:]), lambda s: (s, 0, 0))


def qkv_grad_call(me, grads, act, form, members, deps):
    tokens, width = act.shape
    nseq, _, length = grads[0].shape
    outs = packed_shapes(form, members, [(width // members, 3 * width)])
    return pl.pallas_call(
        lambda *refs: qkv_grad_kernel(len(grads), len(deps), *refs),
        grid=(nseq,),
        in_specs=[
            SMEM, pl.BlockSpec((length, width), lambda s: (s, 0)),
            *(turned_spec(g) for g in grads), *(ANY for _ in deps),
        ],
        out_specs=[spec for spec, _ in outs],
        out_shape=[shape for _, shape in outs],
        scratch_shapes=[pltpu.VMEM((width, 3 * width), F32)],
        compiler_params=params(62),
        cost_estimate=cost(13),
        name="qkv_grad",
    )(me, act, *grads, *deps)


def first_back_kernel(parts, deps, me_ref, shift_ref, x_ref, gh_ref, small_ref, *refs):
    smalls = refs[parts : parts + parts // 3 + 4]
    grads, pieces = refs[:parts], refs[parts + len(smalls) : -5 - deps]
    gx_ref, sum_ref, ring, w_ref, sems = refs[-5:]
    rows, width = x_ref.shape
    length = gx_ref.shape[0]
    seq, step = pl.program_id(0), pl.program_id(1)

    @pl.when((seq == 0) & (step == 0))
    def _():
        load_pieces(me_ref[0], pieces, w_ref, sems, True)
        sum_ref[...] = jnp.zeros_like(sum_ref)
        heads, (after, up0, up1, states) = smalls[:-4], smalls[-4:]
        for part in range(3):
            row = [sum(g[s, part, 0:1] for s in range(g.shape[0])) for g in heads]
            sum_ref[2 + part : 3 + part] = jnp.concatenate(row, axis=1)
        members = small_ref.shape[0]
        cuts = [v.shape[1] // members for v in (up0, up1)]
        segments = [
            v[:, m * cut : (m + 1) * cut] for m in range(members) for v, cut in zip((up0, up1), cuts)
        ]
        per = width // sum(cuts)
        for i in range(members // per):
            sum_ref[8 + i : 9 + i] = jnp.concatenate(segments[2 * per * i : 2 * per * (i + 1)], axis=1)
        for target, source, place, count in (
            (5, after, 2, 1), (6, after, 0, 2), (12, after, 3, 1), (13, states, 0, 4), (17, after, 4, 1)
        ):
            sum_ref[target : target + count] = source[place : place + count]
        load_pieces(me_ref[0], pieces, w_ref, sems, False)

    gain = vec(small_ref, "g1")
    e = dot_tt(jnp.concatenate([g[0] for g in grads], axis=0), w_ref[...])
    n, r = norm_parts(x_ref[...].astype(F32))
    eg = e * gain
    part = r * (
        eg - jnp.mean(eg, axis=-1, keepdims=True) - n * jnp.mean(eg * n, axis=-1, keepdims=True)
    )
    sum_ref[0:1] += jnp.sum(e * n, axis=0, keepdims=True)
    sum_ref[1:2] += jnp.sum(e, axis=0, keepdims=True)
    ring_put(ring, pl.multiple_of(step * rows, rows), gh_ref[...] + part)

    @pl.when(step == pl.num_programs(1) - 1)
    def _():
        gx_ref[...] = ring_get(ring, length - shift_ref[seq], length)


def first_back_call(me, shift, grads, x, gh, small, pieces, smalls, deps):
    tokens, width = x.shape
    nseq, _, length = grads[0].shape
    steps = 4
    rows = length // steps
    row = pl.BlockSpec((rows, width), lambda s, i: (s * steps + i, 0))
    return pl.pallas_call(
        lambda *refs: first_back_kernel(len(grads), len(deps), *refs),
        grid=(nseq, steps),
        in_specs=[
            SMEM, SMEM, row, row, whole(small.shape),
            *(pl.BlockSpec((1, g.shape[1], rows), lambda s, i: (s, 0, i)) for g in grads), *(whole(v.shape) for v in smalls),
            *(ANY for _ in (*pieces, *deps)),
        ],
        out_specs=[pl.BlockSpec((length, width), lambda s, i: (s, 0)), whole((24, width))],
        out_shape=[
            jax.ShapeDtypeStruct((tokens, width), F32),
            jax.ShapeDtypeStruct((24, width), F32),
        ],
        scratch_shapes=[
            ring_shape(length, width),
            pltpu.VMEM((width, 3 * width), BF),
            pltpu.SemaphoreType.DMA((len(pieces),)),
        ],
        compiler_params=params(62),
        cost_estimate=cost(20),
        name="first_back",
    )(me, shift, x, gh, small, *grads, *smalls, *pieces, *deps)


def states_kernel(mix_ref, e_ref, c_ref, part_ref, sum_ref):
    @pl.when(pl.program_id(0) == 0)
    def _():
        sum_ref[...] = jnp.zeros_like(sum_ref)

    cot = c_ref[...].astype(F32)
    total = None
    for j in range(e_ref.shape[0]):
        e = e_ref[j].astype(F32)
        term = mix_ref[j] * e
        total = term if total is None else total + term
        sum_ref[j : j + 1] += jnp.sum(e * cot, axis=0, keepdims=True)
    part_ref[...] = total


def states_call(mix, earlier, cot):
    states, tokens, width = earlier.shape
    rows = 256
    row = pl.BlockSpec((rows, width), lambda i: (i, 0))
    stack = pl.BlockSpec((states, rows, width), lambda i: (0, i, 0))
    return pl.pallas_call(
        states_kernel,
        grid=(tokens // rows,),
        in_specs=[SMEM, stack, row],
        out_specs=[row, whole((8, width))],
        out_shape=[
            jax.ShapeDtypeStruct((tokens, width), F32),
            jax.ShapeDtypeStruct((8, width), F32),
        ],
        compiler_params=params(62),
        cost_estimate=cost(11),
        name="states",
    )(mix, earlier, cot)


def spread_kernel(mix_ref, c_ref, *refs):
    out = refs[-1]
    cot = c_ref[...].astype(F32)
    for j in range(out.shape[0]):
        out[j] = mix_ref[j] * cot


def spread_call(states, mix, cot, deps):
    tokens, width = cot.shape
    rows = 256
    return pl.pallas_call(
        spread_kernel,
        grid=(tokens // rows,),
        in_specs=[SMEM, pl.BlockSpec((rows, width), lambda i: (i, 0)), *(ANY for _ in deps)],
        out_specs=pl.BlockSpec((states, rows, width), lambda i: (0, i, 0)),
        out_shape=jax.ShapeDtypeStruct((states, tokens, width), F32),
        compiler_params=params(62),
        cost_estimate=cost(20),
        name="spread",
    )(mix, cot, *deps)


def split_kernel(members, shares, wo_ref, wu_ref, wd_ref, *refs):
    outs = refs[-5:]
    outs[0][...] = wo_ref[...]
    deep = wu_ref.shape[1] // members
    base = 0
    for i, share in enumerate(shares):
        for m in range(members):
            outs[1 + i][:, m * share : (m + 1) * share] = wu_ref[:, m * deep + base : m * deep + base + share]
        outs[3 + i][...] = wd_ref[base : base + share]
        base += share


def split_call(members, shares, wo, wu, wd, deps):
    own = wu.shape[0]
    width = wd.shape[1]
    low = [(own, width), *((own, members * v) for v in shares), *((v, width) for v in shares)]
    full = pl.BlockSpec(memory_space=pltpu.VMEM)
    return pl.pallas_call(
        lambda *refs: split_kernel(members, shares, *refs),
        in_specs=[full, full, full, *(ANY for _ in deps)],
        out_specs=[full] * 5,
        out_shape=[jax.ShapeDtypeStruct(shape, BF) for shape in low],
        compiler_params=params(62),
        cost_estimate=cost(3),
        name="split",
    )(wo, wu, wd, *deps)


def mix_kernel(shift_ref, mix_ref, part_ref, b_ref, *refs):
    out_ref, ring = refs[-2:]
    length = b_ref.shape[0]
    ring_put(ring, 0, b_ref[...])
    rolled = ring_get(ring, length - shift_ref[pl.program_id(0)], length)
    out_ref[...] = (part_ref[...] + mix_ref[4] * rolled).astype(BF)


def mix_call(shift, mix, part, block_out, deps):
    tokens, width = part.shape
    nseq = shift.shape[0]
    length = tokens // nseq
    row = pl.BlockSpec((length, width), lambda s: (s, 0))
    return pl.pallas_call(
        mix_kernel,
        grid=(nseq,),
        in_specs=[SMEM, SMEM, row, row, *(ANY for _ in deps)],
        out_specs=row,
        out_shape=jax.ShapeDtypeStruct((tokens, width), BF),
        scratch_shapes=[ring_shape(length, width)],
        compiler_params=params(62),
        cost_estimate=cost(20),
        name="mix",
    )(shift, mix, part, block_out, *deps)


def swap(v, axis, bits):
    size = lax.axis_size(axis)
    return lax.ppermute(v, axis, [(i, i ^ bits) for i in range(size)])


def gate(arrays, deps):
    count = len(arrays)
    return pl.pallas_call(
        lambda *refs: None,
        in_specs=[ANY] * (count + len(deps)),
        out_specs=[ANY] * count,
        out_shape=[jax.ShapeDtypeStruct(v.shape, v.dtype) for v in arrays],
        input_output_aliases={i: i for i in range(count)},
        cost_estimate=cost(0.3),
        name="gate",
    )(*arrays, *deps)


def far_pieces(v):
    return [v, *(swap(v, "shard", 2 * k) for k in range(1, lax.axis_size("shard") // 2))]


def near_pieces(far, own=None):
    pieces = []
    for k, v in enumerate(far):
        pieces += [v, own if own is not None and k == 0 else swap(v, "shard", 1)]
    return pieces


def gather_pieces(v):
    return near_pieces(far_pieces(v))


def in_order(pieces, mine):
    stack = jnp.stack(pieces)
    return [lax.dynamic_index_in_dim(stack, j ^ mine, 0, keepdims=False) for j in range(len(pieces))]


def total_of(terms):
    total = terms[0].astype(F32)
    for term in terms[1:]:
        total = total + term.astype(F32)
    return total


def chain_start(pair):
    keep, send = pair
    return {"keep": keep, "near": swap(send, "shard", 1)}


def step_parts(kind, chain):
    if kind == "small":

        def body(idx, ins, outs):
            outs[0][...] = ins[0][...] + ins[1][...]

        return [(v, whole(v.shape)) for v in (chain["sum"], chain["got"])], [(*chain["sum"].shape, F32)], body
    keep, near = chain["keep"], chain["near"]
    chips, sides, groups, n, lanes = keep.shape
    half = (groups, n, lanes)

    def at(side):
        spec = pl.BlockSpec((1, 1, *half), lambda i, idx: (idx[0], side(idx), 0, 0, 0))
        deep = pl.BlockSpec((1, *half), lambda i, idx: (side(idx), 0, 0, 0))
        return [(keep, spec), (near, spec), *((far, deep) for far in chain["far"])]

    def total(refs, group):
        out = None
        for ref in refs:
            piece = ref[(0,) * (len(ref.shape) - 3) + (group,)].astype(F32)
            out = piece if out is None else out + piece
        return out

    if kind == "x":
        ins = []
        for k in range(1, chips):
            spec = pl.BlockSpec((1, sides, *half), lambda i, idx, k=k: (idx[0] ^ k, 0, 0, 0, 0))
            ins += [(keep, spec), (near, spec)]

        def body(idx, ins, outs):
            for k, out in enumerate(outs):
                out[...] = (ins[2 * k][0].astype(F32) + ins[2 * k + 1][0].astype(F32)).astype(BF)

        return ins, [(sides, *half)] * (chips - 1), body
    if kind == "y":

        def body(idx, ins, outs):
            for g in range(groups):
                outs[0][g] = total(ins, g).astype(BF)

        return at(lambda idx: 1 - idx[1]), [half], body
    if kind == "half":
        ins = [(v, whole(v.shape)) for v in (chain["done"], *chain["zg"])]

        def body(idx, ins, outs):
            for k, ref in enumerate(ins):
                outs[0][idx[2] ^ k] = ref[...]

        return ins, [half], body
    if kind == "z":

        def body(idx, ins, outs):
            for k in range(groups):
                outs[k][...] = total(ins, idx[2] ^ k).astype(outs[k].dtype)

        return [*at(lambda idx: idx[1]), (chain["yr"], whole(half))], [(n, lanes, F32), *[(n, lanes)] * (groups - 1)], body

    def body(idx, ins, outs):
        out = ins[0][...]
        for ref in ins[1:]:
            out = out + ref[...].astype(F32)
        outs[0][...] = out.astype(BF)

    return [(v, whole(v.shape)) for v in (chain["mine"], *chain["zr"])], [(n, lanes)], body


def step_call(idx, steps, deps):
    plans = [step_parts(kind, chain) for kind, chain in steps]
    ins = [pair for plan in plans for pair in plan[0]]
    outs = [shape for plan in plans for shape in plan[1]]
    types = [F32 if shape[-1] == F32 else BF for shape in outs]
    outs = [shape[:-1] if shape[-1] == F32 else shape for shape in outs]

    def kernel(idx_ref, *refs):
        at, out_at = 0, len(ins) + len(deps)
        for some, shapes, body in plans:
            body(idx_ref, refs[at : at + len(some)], refs[out_at : out_at + len(shapes)])
            at += len(some)
            out_at += len(shapes)

    results = pl.pallas_call(
        kernel,
        grid_spec=pltpu.PrefetchScalarGridSpec(
            num_scalar_prefetch=1,
            grid=(1,),
            in_specs=[*(spec for _, spec in ins), *(ANY for _ in deps)],
            out_specs=[whole(shape) for shape in outs],
        ),
        out_shape=[jax.ShapeDtypeStruct(shape, dtype) for shape, dtype in zip(outs, types)],
        compiler_params=params(62),
        cost_estimate=cost(3),
        name="_".join(["step", *(kind for kind, _ in steps)]),
    )(idx, *(v for v, _ in ins), *deps)
    at = 0
    others = range(1, lax.axis_size("rep") // 2)
    for (kind, chain), (_, shapes, _) in zip(steps, plans):
        sends = results[at : at + len(shapes)]
        at += len(shapes)
        if kind == "x":
            chain["far"] = [swap(v, "shard", 2 * (k + 1)) for k, v in enumerate(sends)]
        elif kind == "y":
            chain["yr"] = swap(sends[0], "rep", 1)
        elif kind == "z":
            chain["mine"] = sends[0]
            chain["zr"] = [swap(sends[k], "rep", 2 * k) for k in others]
        elif kind == "sum":
            chain["done"] = sends[0]
            chain["zg"] = [swap(sends[0], "rep", 2 * k) for k in others]
        elif kind == "half":
            chain["half"] = sends[0]
            chain["twin"] = swap(sends[0], "rep", 1)
        else:
            small_next(chain, sends[0])
    return results[0]


def small_next(chain, sums):
    chain["sum"] = sums
    count = chain["steps"] = chain.get("steps", -1) + 1
    bits = [("shard", 1 << b) for b in range(lax.axis_size("shard").bit_length() - 1)] + [("rep", 1)]
    if count < len(bits):
        chain["got"] = swap(sums, *bits[count])
    else:
        chain["got"] = [swap(sums, "rep", 2 * k) for k in range(1, lax.axis_size("rep") // 2)]


def small_end(chain, group):
    return total_of(in_order([chain["sum"], *chain["got"]], group))


def finish_call(idx, chains, plans, shapes, deps):
    ins = [v for chain in chains for v in (chain["half"], chain["twin"])]

    def kernel(idx_ref, *refs):
        outs = refs[len(ins) + len(deps) : len(ins) + len(deps) + len(shapes)]
        scratch = refs[-len(chains) :]
        for c, plan in enumerate(plans):
            both = scratch[c]
            both[idx_ref[1]] = refs[2 * c][...]
            both[1 - idx_ref[1]] = refs[2 * c + 1][...]
            sides, groups = both.shape[:2]
            at = 0
            for out, own, cols, place in plan:
                rows, wide = own // groups, cols // sides
                for j in range(wide // 128):
                    for side in range(sides):
                        for group in range(groups):
                            row, col = place(group * rows, side * wide + j * 128)
                            outs[out][row : row + rows, col : col + 128] = both[
                                side, group, at : at + rows, :
                            ].astype(F32)
                    at += rows

    return pl.pallas_call(
        kernel,
        in_specs=[SMEM, *(pl.BlockSpec(memory_space=pltpu.VMEM) for _ in ins), *(ANY for _ in deps)],
        out_specs=[pl.BlockSpec(memory_space=pltpu.VMEM) for _ in shapes],
        out_shape=[jax.ShapeDtypeStruct(shape, F32) for shape in shapes],
        scratch_shapes=[pltpu.VMEM((2, *chain["half"].shape), BF) for chain in chains],
        compiler_params=params(62),
        cost_estimate=cost(4),
        name="finish",
    )(idx, *ins, *deps)


def reduce_plain(packed):
    flat = packed.reshape(-1, 128)
    return lax.psum(lax.psum_scatter(flat, "shard", scatter_dimension=0, tiled=True), "rep")[None, None]


def reduce_small(v):
    for axis in ("shard", "rep"):
        bits = 1
        while bits < lax.axis_size(axis):
            v = v + swap(v, axis, bits)
            bits *= 2
    return v


def shards(
    inputs, earlier, segments, cotangent, mix_weights,
    ln1_gain, ln1_bias, qkv_weight, qkv_bias, out_weight, out_bias,
    ln2_gain, ln2_bias, up_weight, up_bias, down_weight, down_bias,
):
    nseq, length = segments.shape
    width = inputs.shape[1]
    blk = length // 2
    members, replicas = lax.axis_size("shard"), lax.axis_size("rep")
    me = lax.axis_index("shard").astype(jnp.int32)
    rep = lax.axis_index("rep").astype(jnp.int32)
    side = rep % 2
    me_ref = me[None]
    idx = jnp.stack([me // 2, side, rep // 2])
    own = width // members
    deep = down_weight.shape[0]
    ff = deep * members
    shares = [2 * deep // 3, deep - 2 * deep // 3]
    fits = own % (8 * replicas) == 0 and all(v % (8 * replicas) == 0 and v % 128 == 0 for v in shares)
    form = (2, replicas // 2) if fits else (1, 1)

    wqkv = far_pieces(qkv_weight)
    wqkv_near = swap(qkv_weight, "shard", 1)
    vectors = [ln1_gain, ln1_bias, qkv_bias, out_bias, ln2_gain, ln2_bias, up_bias, down_bias]
    sizes = [v.shape[0] for v in vectors]
    wide = max(sizes)
    small = jnp.stack([jnp.pad(v, (0, wide - v.shape[0])) for v in vectors])
    small = [small, *(swap(small, "shard", k) for k in range(1, members))]
    small = jnp.stack(in_order(small, me))

    part, sums3 = states_call(mix_weights, earlier, cotangent)
    inv = np.exp(np.arange(HEAD // 2) * (-math.log(10000.0) / (HEAD // 2)))
    angles = np.arange(length)[None, :] * inv[:, None]
    tables = jnp.asarray(np.stack([np.cos(angles), np.sin(angles)]), F32)
    shift, xr, cr, act, seg, cos, sin = roll_call(inputs, cotangent, segments, small, tables, [sums3])
    if any(v % 128 for v in (deep, *shares)):

        def shared(v):
            halves = jnp.split(v.reshape(v.shape[0], members, deep), [shares[0]], axis=-1)
            return [h.reshape(v.shape[0], -1) for h in halves]

        pieces = [out_weight, *shared(up_weight), down_weight[: shares[0]], down_weight[shares[0] :]]
    else:
        pieces = split_call(members, shares, out_weight, up_weight, down_weight, [act, *wqkv])
    wo = lax.all_gather(pieces[0], "shard", axis=0, tiled=True)
    wd0 = far_pieces(pieces[3])

    wqkv = near_pieces([qkv_weight, *gate(wqkv[1:], [act])], wqkv_near)
    qkv = qkv_call(me_ref, act, small, cos, sin, wqkv)
    *wd0, wu0 = gate([*wd0, pieces[1]], [qkv])
    wd0 = near_pieces(wd0)
    wu0, wu0_near = far_pieces(wu0), swap(wu0, "shard", 1)
    o, lse = attend_call(seg, qkv)
    wd0[1::2], (*wu0, wu1, wd1) = gate(wd0[1::2], [lse]), gate([*wu0, pieces[2], pieces[4]], [lse])
    wu0 = near_pieces(wu0, wu0_near)
    wu1 = lax.all_gather(wu1, "shard", axis=0, tiled=True)
    wd1 = far_pieces(wd1)
    values = {"me": me_ref, "mix": mix_weights, "small": small, "x": xr, "cot": cr, "a": o, "wo": wo}
    got = mlp_call(0, shares[0], True, False, values | {"wu": wu0, "wd": wd0}, form, members, [])
    values |= {"up_in": got["up"], "back_in": got["back"], "hid": got["hid"], "act": got["act"]}
    wd1 = near_pieces(gate(wd1, [got["dbu"]]))
    first, dbu = [got[name] for name in ("dw0", "dw1") if name in got], [got["dbu"]]
    spread = [earlier.shape[0], mix_weights, cotangent]
    if fits:
        early = chain_start(first)
        earlier_grad = spread_call(*spread, [first[0]])
        deps = [step_call(idx, [("x", early)], [earlier_grad])]
    else:
        earlier_grad, deps = spread_call(*spread, []), []
    got = mlp_call(
        shares[0], shares[1], False, True, values | {"wu": [wu1], "wd": wd1}, form, members, deps
    )
    second = [got[name] for name in ("dw0", "dw1") if name in got]
    dbu.append(got["dbu"])
    block_out, gh, ga, sums2 = (got[name] for name in ("up", "gh", "ga", "sum"))

    groups = width // PAIR // 2
    back = [seg, qkv, o, ga, lse, cos, sin]

    def up_place(base, share):
        def place(row, col):
            return row, col // share * deep + base + col % share

        return place

    if fits:
        late = chain_start(second)
        t = step_call(idx, [("y", early)], [late["keep"]])
        gs = [attend_back_call(*back, 0, 2, [t])]
        t = step_call(idx, [("z", early), ("x", late)], [gs[0][0]])
        gs.append(attend_back_call(*back, 2, 2, [t]))
        t = step_call(idx, [("sum", early)], [gs[1][0]])
        for i in range(2, groups):
            gs.append(attend_back_call(*back, 2 * i, 2, [t, gs[-1][0]], 0.5))
        early["zg"] = gate(early["zg"], [gs[-1][0]])
        t = step_call(idx, [("y", late)], [gs[-1][0]])
        smalls = [*(g[3] for g in gs), sums2, *dbu, sums3]
        grads = [g[i] for i in range(3) for g in gs]
        pack = qkv_grad_call(me_ref, grads, act, form, members, [t])
        tail = chain_start(pack)
        t = step_call(idx, [("half", early), ("z", late)], [pack[0]])
        output = mix_call(shift, mix_weights, part, block_out, [t])
        t = step_call(idx, [("x", tail)], [output])
        input_grad, sums = first_back_call(me_ref, shift, grads, xr, gh, small, wqkv, smalls, [t])
        (early["twin"],) = gate([early["twin"]], [sums])
        sums_chain = {}
        small_next(sums_chain, sums)
        t = step_call(idx, [("sum", late), ("y", tail)], [sums])
        t = step_call(idx, [("half", late), ("z", tail), ("small", sums_chain)], [])
        t = step_call(idx, [("sum", tail), ("small", sums_chain)], [])
        d_up, d_down, d_out = finish_call(
            idx,
            [early, late],
            [
                [
                    (0, own, shares[0] * members, up_place(0, shares[0])),
                    (1, shares[0], width, lambda row, col: (row, col)),
                ],
                [
                    (0, own, shares[1] * members, up_place(shares[0], shares[1])),
                    (1, shares[1], width, lambda row, col: (row + shares[0], col)),
                    (2, own, width, lambda row, col: (row, col)),
                ],
            ],
            [(own, ff), (deep, width), (own, width)],
            [t],
        )
        t = step_call(idx, [("half", tail), ("small", sums_chain)], [d_out])
        flat = small_end(sums_chain, rep // 2).reshape(-1)
        (d_qkv,) = finish_call(
            idx, [tail], [[(0, own, 3 * width, lambda row, col: (row, col))]], [(own, 3 * width)], []
        )
    else:
        gs = [attend_back_call(*back, 2 * i, 2, []) for i in range(groups)]
        smalls = [*(g[3] for g in gs), sums2, *dbu, sums3]
        grads = [g[i] for i in range(3) for g in gs]
        pack = qkv_grad_call(me_ref, grads, act, form, members, [])
        output = mix_call(shift, mix_weights, part, block_out, [])
        input_grad, sums = first_back_call(me_ref, shift, grads, xr, gh, small, wqkv, smalls, [])
        ups, downs = [], []
        first, second, third = [reduce_plain(p[0]) for p in (first, second, pack)]
        for v, share in ((first, shares[0]), (second, shares[1])):
            at = packed_rows(own, share * members, *v.shape[:2])
            ups.append(unpack(v, 0, own, share * members).reshape(own, members, share))
            downs.append(unpack(v, at, share, width))
            at += packed_rows(share, width, *v.shape[:2])
        d_out = unpack(second, at, own, width).astype(F32)
        d_up = jnp.concatenate(ups, axis=2).reshape(own, -1).astype(F32)
        d_down = jnp.concatenate(downs, axis=0).astype(F32)
        d_qkv = unpack(third, 0, own, 3 * width).astype(F32)
        flat = reduce_small(sums).reshape(-1)

    parts, at = [], 0
    for size in sizes:
        parts.append(lax.dynamic_slice(flat, (at + me * size,), (size,)))
        at += size * members
    mix_grad = jnp.sum(flat[at : at + 5 * width].reshape(5, width), axis=1)
    return (
        output, input_grad, earlier_grad, mix_grad,
        parts[0], parts[1], d_qkv, parts[2], d_out, parts[3], parts[4], parts[5],
        d_up, parts[6], d_down, parts[7],
    )


def solution(mesh):
    rows, shard = P(("rep", "shard"), None), P("shard")
    mat, deep = P("shard", None), P(None, ("rep", "shard"), None)
    return jax.shard_map(
        shards,
        mesh=mesh,
        in_specs=(
            rows, deep, rows, rows, P(),
            shard, shard, mat, shard, mat, shard, shard, shard, mat, shard, mat, shard,
        ),
        out_specs=(
            rows, rows, deep, P(),
            shard, shard, mat, shard, mat, shard, shard, shard, mat, shard, mat, shard,
        ),
        check_vma=False,
    )
```

```python
import math

import jax
import jax.numpy as jnp
import numpy as np
from jax import lax
from jax.experimental import pallas as pl
from jax.experimental.pallas import tpu as pltpu
from jax.sharding import PartitionSpec as P

HEADS = 12
HEAD = 64
PAIR = 2 * HEAD
EPSILON = 1e-05
LOG2E = math.log2(math.e)
NEG = -1e30
GELU_A = math.sqrt(2.0 / math.pi)
GELU_B = GELU_A * 0.044715
BF = jnp.bfloat16
F32 = jnp.float32
MIB = 1 << 20

COST_SHARE = 1.5


def cost(us):
    return pl.CostEstimate(flops=int(us * COST_SHARE * 1.15e9), bytes_accessed=1024, transcendentals=0)


def dot_nn(a, b):
    return lax.dot_general(a, b, (((1,), (0,)), ((), ())), preferred_element_type=F32)


def dot_nt(a, b):
    return lax.dot_general(a, b, (((1,), (1,)), ((), ())), preferred_element_type=F32)


def dot_tn(a, b):
    return lax.dot_general(a, b, (((0,), (0,)), ((), ())), preferred_element_type=F32)


def dot_tt(a, b):
    return lax.dot_general(a, b, (((0,), (1,)), ((), ())), preferred_element_type=F32)


def params(vmem):
    return pltpu.CompilerParams(vmem_limit_bytes=vmem * MIB)


ANY = pl.BlockSpec(memory_space=pl.ANY)


def load_pieces(me, pieces, target, sems, start, cols=None):
    copies = []
    for j, piece in enumerate(pieces):
        rows = piece.shape[0]
        at = pl.multiple_of((me ^ j) * rows, rows)
        source = piece if cols is None else piece.at[:, cols]
        copies.append(pltpu.make_async_copy(source, target.at[pl.ds(at, rows), :], sems.at[j]))
    for copy in copies:
        if start:
            copy.start()
        else:
            copy.wait()


def pack(target, source, base, own, sides, groups, at):
    rows, cols = own // groups, source.shape[-1] // sides
    for side in range(sides):
        for group in range(groups):
            for j in range(cols // 128):
                here = at + j * rows
                col = side * cols + j * 128
                target[side, group, here : here + rows, :] = source[
                    pl.ds(base + group * rows, rows), col : col + 128
                ].astype(BF)


def pack_all(targets, me, source, own, at):
    for t, target in enumerate(targets):
        count, sides, groups = target.shape[:3]
        for i in range(count):
            place = i if len(targets) == 1 else 2 * i + ((me % 2) ^ t)
            pack(target.at[i], source, pl.multiple_of(place * own, own), own, sides, groups, at)


def unpack(v, at, own, cols):
    sides, groups = v.shape[:2]
    rows, wide = own // groups, cols // sides
    count = wide // 128
    part = v[:, :, at : at + rows * count].reshape(sides, groups, count, rows, 128)
    return part.transpose(1, 3, 0, 2, 4).reshape(own, cols)


def packed_rows(own, cols, sides, groups):
    return own * cols // (128 * sides * groups)


def packed_shapes(form, members, own_cols):
    sides, groups = form
    n = sum(packed_rows(own, cols, sides, groups) for own, cols in own_cols)
    split = 1 if form == (1, 1) else 2
    shape = (members // split, sides, groups, n, 128)
    return [(whole(shape), jax.ShapeDtypeStruct(shape, BF)) for _ in range(split)]


def whole(shape):
    zeros = (0,) * len(shape)
    return pl.BlockSpec(shape, lambda *_: zeros, pipeline_mode=pl.Buffered(1))


SMEM = pl.BlockSpec(memory_space=pltpu.SMEM)


def ring_shape(length, width):
    return pltpu.VMEM((width // 128, 2 * length, 128), F32)


def ring_put(ring, at, value):
    for j in range(ring.shape[0]):
        part = value[:, j * 128 : (j + 1) * 128]
        ring[j, pl.ds(at, value.shape[0]), :] = part
        ring[j, pl.ds(ring.shape[1] // 2 + at, value.shape[0]), :] = part


def ring_get(ring, start, rows):
    return jnp.concatenate([ring[j, pl.ds(start, rows), :] for j in range(ring.shape[0])], axis=1)


def norm_parts(v):
    mean = jnp.mean(v, axis=-1, keepdims=True)
    centred = v - mean
    var = jnp.mean(centred * centred, axis=-1, keepdims=True)
    r = lax.rsqrt(var + EPSILON)
    return centred * r, r


ROWS = ("g1", "b1", "bqkv", "bo", "g2", "b2", "bu", "bd")
FF_RATIO = 4


def vec(ref, name, base=0, share=None):
    row = ROWS.index(name)
    size = share or ref.shape[2] // FF_RATIO
    parts = [ref[m, row : row + 1, base : base + size] for m in range(ref.shape[0])]
    return jnp.concatenate(parts, axis=1).astype(F32)


def column(row):
    return jnp.broadcast_to(row, (128, row.shape[1])).T[:, :1]


def roll_kernel(x_ref, cot_ref, seg_ref, small_ref, tab_ref, *refs):
    shift_ref, xr_ref, cr_ref, act_ref, seg_out, cos_ref, sin_ref, ring = refs[-8:]
    length = x_ref.shape[0]
    half = length // 2
    seg = jnp.broadcast_to(seg_ref[0].astype(F32), (8, length))
    place = lax.broadcasted_iota(jnp.int32, (8, length), 1)
    same = (seg == pltpu.roll(seg, length - (half - 1), 1)) & (place <= half)
    shift = jnp.min(jnp.where(same, place.astype(F32), float(length))).astype(jnp.int32)
    shift_ref[pl.program_id(0)] = shift
    back = lax.rem(length - shift, length)
    seg_out[0] = pltpu.roll(seg, back, 1)[:, half:]
    cos_ref[0] = pltpu.roll(tab_ref[0], back, 1)
    sin_ref[0] = pltpu.roll(tab_ref[1], back, 1)
    for source, target in ((cot_ref, cr_ref), (x_ref, xr_ref)):
        ring_put(ring, 0, source[...].astype(F32))
        target[...] = ring_get(ring, shift, length).astype(BF)
    gain, bias = vec(small_ref, "g1"), vec(small_ref, "b1")
    rows = 256
    for at in range(0, length, rows):
        n, _ = norm_parts(xr_ref[at : at + rows].astype(F32))
        act_ref[at : at + rows] = (n * gain + bias).astype(BF)


def roll_call(x, cot, seg, small, tables, deps):
    tokens, width = x.shape
    nseq, length = seg.shape
    row = pl.BlockSpec((length, width), lambda s: (s, 0))
    tab = pl.BlockSpec((1, HEAD // 2, length), lambda s: (s, 0, 0))
    low = jax.ShapeDtypeStruct((tokens, width), BF)
    turn = jax.ShapeDtypeStruct((nseq, HEAD // 2, length), F32)
    return pl.pallas_call(
        roll_kernel,
        grid=(nseq,),
        in_specs=[
            row, row, pl.BlockSpec((1, 1, length), lambda s: (s, 0, 0)), whole(small.shape), whole(tables.shape),
            *(ANY for _ in deps),
        ],
        out_specs=[SMEM, row, row, row, pl.BlockSpec((1, 8, length // 2), lambda s: (s, 0, 0)), tab, tab],
        out_shape=[
            jax.ShapeDtypeStruct((nseq,), jnp.int32), low, low, low,
            jax.ShapeDtypeStruct((nseq, 8, length // 2), F32), turn, turn,
        ],
        scratch_shapes=[ring_shape(length, width)],
        compiler_params=params(62),
        cost_estimate=cost(10),
        name="roll",
    )(x, cot, seg[:, None, :], small, tables, *deps)


def qkv_kernel(me_ref, act_ref, small_ref, cos_ref, sin_ref, *refs):
    pieces, (out_ref, w_ref, sems) = refs[:-3], refs[-3:]
    width = act_ref.shape[1]
    half = HEAD // 2
    rows = 256
    bias = vec(small_ref, "bqkv", 0, 3 * width // small_ref.shape[0])

    def load(part, start):
        cols = slice(part * width, (part + 1) * width)
        load_pieces(me_ref[0], pieces, w_ref.at[part], sems.at[part], start, cols)

    @pl.when((pl.program_id(0) == 0) & (pl.program_id(1) == 0))
    def _():
        for part in range(3):
            load(part, True)

    def project(part):
        @pl.when(pl.program_id(0) == 0)
        def _():
            load(part, False)

        cos, sin = cos_ref[0], sin_ref[0]
        for base in range(0, width, rows):
            cols = slice(base, base + rows)
            at = part * width + base
            y = dot_tt(w_ref[part, :, cols], act_ref[...]) + column(bias[:, at : at + rows])
            if part == 2:
                out_ref[0, base : base + rows, :] = y.astype(BF)
                continue
            for h in range(0, rows, HEAD):
                u, w = y[h : h + half], y[h + half : h + HEAD]
                a, b = u * cos - w * sin, w * cos + u * sin
                if part == 0:
                    a, b = a * (LOG2E * HEAD**-0.5), b * (LOG2E * HEAD**-0.5)
                out_ref[0, base + h : base + h + half, :] = a.astype(BF)
                out_ref[0, base + h + half : base + h + HEAD, :] = b.astype(BF)

    for part in range(3):
        pl.when(pl.program_id(1) == part)(lambda part=part: project(part))


def qkv_call(me, act, small, cos, sin, pieces):
    tokens, width = act.shape
    nseq, _, length = cos.shape
    tab = pl.BlockSpec((1, HEAD // 2, length), lambda s, p: (s, 0, 0))
    return pl.pallas_call(
        qkv_kernel,
        grid=(nseq, 3),
        in_specs=[
            SMEM, pl.BlockSpec((length, width), lambda s, p: (s, 0)), whole(small.shape), tab, tab,
            *(ANY for _ in pieces),
        ],
        out_specs=pl.BlockSpec((1, None, width, length), lambda s, p: (s, p, 0, 0)),
        out_shape=jax.ShapeDtypeStruct((nseq, 3, width, length), BF),
        scratch_shapes=[
            pltpu.VMEM((3, width, width), BF),
            pltpu.SemaphoreType.DMA((3, len(pieces))),
        ],
        compiler_params=params(62),
        cost_estimate=cost(15),
        name="qkv",
    )(me, act, small, cos, sin, *pieces)


def head_specs(base):
    return [
        lambda length, part=part: pl.BlockSpec((1, None, PAIR, length), lambda s, h: (s, part, base + h, 0))
        for part in range(3)
    ]


def fill_masks(seg_ref, mask, blk):
    row = seg_ref[0, 0:1, :]
    col = column(row)
    kk = lax.broadcasted_iota(jnp.int32, (blk, blk), 0)
    qq = lax.broadcasted_iota(jnp.int32, (blk, blk), 1)
    causal = kk <= qq
    mask[0] = jnp.where(causal, 0.0, NEG)
    for i, (kb, qb) in enumerate(((0, 0), (0, 1), (1, 1))):
        same = col[kb * blk : (kb + 1) * blk] == row[:, qb * blk : (qb + 1) * blk]
        keep = same if kb != qb else same & causal
        mask[1 + i] = jnp.where(keep, 0.0, NEG)


def scores_of(keys, query, mask, half, qb, blk):
    top = dot_nn(keys[: (qb + 1) * blk], query)
    if half == 0:
        diag = top[qb * blk :] + mask[0]
        return diag if qb == 0 else jnp.concatenate([top[:blk], diag], axis=0)
    if qb == 0:
        return top + mask[1]
    return jnp.concatenate([top[:blk] + mask[2], top[blk:] + mask[3]], axis=0)


def one_head(pair_rows, head):
    zero = jnp.zeros((HEAD, pair_rows.shape[1]), pair_rows.dtype)
    rows = pair_rows[head * HEAD : (head + 1) * HEAD]
    return jnp.concatenate([rows, zero] if head == 0 else [zero, rows], axis=0)


def attend_kernel(seg_ref, q_ref, k_ref, v_ref, o_ref, l_ref, mask):
    length = q_ref.shape[2]
    blk = length // 4

    @pl.when(pl.program_id(1) == 0)
    def _():
        fill_masks(seg_ref, mask, blk)

    units = [(half, head, qb) for qb in range(2) for half in range(2) for head in range(2)]
    keys = [k_ref[0, :, half * 2 * blk : (half + 1) * 2 * blk].T for half in range(2)]

    def place(half, head, qb):
        base = half * 2 * blk
        qs = slice(base + qb * blk, base + (qb + 1) * blk)
        return base, qs, slice(head * HEAD, (head + 1) * HEAD)

    scores = []
    for half, head, qb in units:
        _, qs, _ = place(half, head, qb)
        scores.append(scores_of(keys[half], one_head(q_ref[0, :, qs], head), mask, half, qb, blk))
    tops = [jnp.max(s, axis=0, keepdims=True) for s in scores]
    probs = [jnp.exp2(s - top) for s, top in zip(scores, tops)]
    totals = [jnp.sum(p, axis=0, keepdims=True) for p in probs]
    lows = [p.astype(BF) for p in probs]
    for (half, head, qb), p, top, total in zip(units, lows, tops, totals):
        base, qs, hs = place(half, head, qb)
        o = dot_nn(v_ref[0, hs, base : base + (qb + 1) * blk], p)
        o_ref[0, hs, qs] = (o / total).astype(BF)
        l_ref[0, 0, head : head + 1, qs] = top + jnp.log2(total)


def attend_call(seg, qkv):
    nseq, _, width, length = qkv.shape
    pairs = width // PAIR
    blk = length // 4
    blockspec = pl.BlockSpec((1, PAIR, length), lambda s, h: (s, h, 0))
    return pl.pallas_call(
        attend_kernel,
        grid=(nseq, pairs),
        in_specs=[
            pl.BlockSpec((1, 8, 2 * blk), lambda s, h: (s, 0, 0)),
            *(spec(length) for spec in head_specs(0)),
        ],
        out_specs=[blockspec, pl.BlockSpec((1, 1, 2, length), lambda s, h: (s, h, 0, 0))],
        out_shape=[
            jax.ShapeDtypeStruct((nseq, width, length), BF),
            jax.ShapeDtypeStruct((nseq, pairs, 2, length), F32),
        ],
        scratch_shapes=[pltpu.VMEM((4, blk, blk), F32)],
        compiler_params=params(62),
        cost_estimate=cost(30),
        name="attend",
    )(seg, qkv, qkv, qkv)


def attend_back_kernel(
    seg_ref, q_ref, k_ref, v_ref, o_ref, g_ref, l_ref, cos_ref, sin_ref, *refs
):
    gq_ref, gk_ref, gv_ref, sum_ref, mask, turn = refs[-6:]
    length = q_ref.shape[2]
    blk = length // 4
    hd = HEAD // 2

    @pl.when(pl.program_id(1) == 0)
    def _():
        fill_masks(seg_ref, mask, blk)

    units = [(half, head, qb) for qb in range(2) for half in range(2) for head in range(2)]
    keys = [k_ref[0, :, half * 2 * blk : (half + 1) * 2 * blk].T for half in range(2)]
    values = [v_ref[0, :, half * 2 * blk : (half + 1) * 2 * blk].T for half in range(2)]

    def place(half, head, qb):
        base = half * 2 * blk
        qs = slice(base + qb * blk, base + (qb + 1) * blk)
        return base, qs, slice(head * HEAD, (head + 1) * HEAD)

    def products(unit):
        half, head, qb = unit
        _, qs, hs = place(*unit)
        s = scores_of(keys[half], one_head(q_ref[0, :, qs], head), mask, half, qb, blk)
        gp = dot_nn(values[half][: (qb + 1) * blk], one_head(g_ref[0, :, qs], head))
        g = g_ref[0, hs, qs].astype(F32) * o_ref[0, hs, qs].astype(F32)
        return s, gp, jnp.sum(g, axis=0, keepdims=True)

    def softmax(unit, held):
        s, gp, delta = held
        _, qs, _ = place(*unit)
        p = jnp.exp2(s - l_ref[0, 0, unit[1] : unit[1] + 1, qs])
        return p.astype(BF), (p * (gp - delta)).astype(BF)

    def finish(unit, pair):
        half, head, qb = unit
        p, ds = pair
        base, qs, hs = place(*unit)
        dv = dot_nt(g_ref[0, hs, qs], p)
        dk = dot_nt(q_ref[0, hs, qs], ds)
        turn[0, hs, qs] = dot_nn(k_ref[0, hs, base : base + (qb + 1) * blk], ds)
        first_half, second_half = slice(base, base + blk), slice(base + blk, base + 2 * blk)
        if qb == 0:
            turn[1, hs, first_half], turn[2, hs, first_half] = dk, dv
        else:
            turn[1, hs, first_half] += dk[:, :blk]
            turn[2, hs, first_half] += dv[:, :blk]
            turn[1, hs, second_half], turn[2, hs, second_half] = dk[:, blk:], dv[:, blk:]

    before = None
    for unit in (*units, None):
        held = products(unit) if unit else None
        if before:
            finish(before[0], softmax(*before))
        before = (unit, held)
    cos, sin = cos_ref[0], sin_ref[0]

    ones = jnp.ones((8, length), BF)
    for part, (out, scale) in enumerate(((gq_ref, HEAD**-0.5), (gk_ref, 1.0 / LOG2E), (gv_ref, 1.0))):
        for head in range(2):
            at = head * HEAD
            u = turn[part, at : at + hd]
            w = turn[part, at + hd : at + HEAD]
            if part < 2:
                u, w = (u * cos + w * sin) * scale, (w * cos - u * sin) * scale
            out[0, at : at + hd, :] = u.astype(BF)
            out[0, at + hd : at + HEAD, :] = w.astype(BF)
        sum_ref[0, part] = dot_nt(ones, out[0])


def attend_back_call(seg, qkv, o, g, lse, cos, sin, base, pairs, deps, us=15):
    nseq, _, _, length = qkv.shape
    blk = length // 4
    source = pl.BlockSpec((1, PAIR, length), lambda s, h: (s, base + h, 0))
    target = pl.BlockSpec((1, PAIR, length), lambda s, h: (s, h, 0))
    tab = pl.BlockSpec((1, HEAD // 2, length), lambda s, h: (s, 0, 0))
    turned = jax.ShapeDtypeStruct((nseq, pairs * PAIR, length), BF)
    return pl.pallas_call(
        attend_back_kernel,
        grid=(nseq, pairs),
        in_specs=[
            pl.BlockSpec((1, 8, 2 * blk), lambda s, h: (s, 0, 0)),
            *(spec(length) for spec in head_specs(base)), source, source,
            pl.BlockSpec((1, 1, 2, length), lambda s, h: (s, base + h, 0, 0)),
            tab, tab, *(ANY for _ in deps),
        ],
        out_specs=[
            target, target, target,
            pl.BlockSpec((1, 3, 8, PAIR), lambda s, h: (s, 0, 0, h)),
        ],
        out_shape=[turned, turned, turned, jax.ShapeDtypeStruct((nseq, 3, 8, pairs * PAIR), F32)],
        scratch_shapes=[pltpu.VMEM((4, blk, blk), F32), pltpu.VMEM((3, PAIR, length), F32)],
        compiler_params=params(62),
        cost_estimate=cost(us),
        name="attend_back",
    )(seg, qkv, qkv, qkv, o, g, lse, cos, sin, *deps)


def mlp_kernel(base, first, last, names, members, *refs):
    ref = dict(zip(names, refs))
    rows, width = ref["cot"].shape
    step = pl.program_id(0)
    final = pl.num_programs(0) - 1
    acc_u, acc_d, low = ref["acc_u"], ref["acc_d"], ref["low"]
    span = acc_u.shape[1]
    me, sems = ref["me"][0], ref["sems"]
    share = span // members
    small = ref["small"]

    def weights(start):
        for i, name in enumerate(("wu", "wd")):
            pieces = [ref[key] for key in ref if key[0] == name]
            load_pieces(me if len(pieces) > 1 else 0, pieces, ref[name], sems.at[i], start)

    @pl.when(step == 0)
    def _():
        weights(True)
        acc_u[...] = jnp.zeros_like(acc_u)
        acc_d[...] = jnp.zeros_like(acc_d)
        ref["dbu"][...] = jnp.zeros_like(ref["dbu"])

    alpha = ref["mix"][4]
    cot = ref["cot"][...].astype(F32)
    g_out = cot * alpha
    low[...] = g_out.astype(BF)
    if first:
        hidden = ref["x"][...].astype(F32) + dot_tn(ref["a"][0], ref["wo"][...]) + vec(small, "bo")
        n, _ = norm_parts(hidden)
        ref["hid"][...] = hidden
        ref["act"][...] = (n * vec(small, "g2") + vec(small, "b2")).astype(BF)

    @pl.when(step == 0)
    def _():
        weights(False)

    act2 = ref["act"]
    if first:
        total_up = ref["hid"][...] + vec(small, "bd")
        total_back = None
    else:
        total_up, total_back = ref["up_in"][...], ref["back_in"][...]
    chunk = width
    bu = vec(small, "bu", base, share)
    for at in range(0, span, chunk):
        cols = slice(at, at + chunk)
        wu, wd = ref["wu"][:, cols], ref["wd"][cols, :]
        pre = dot_nn(act2[...], wu) + bu[:, cols]
        g_act = dot_nt(low[...], wd)
        square = pre * pre
        h = 0.5 + 0.5 * jnp.tanh(pre * (GELU_A + GELU_B * square))
        act = (pre * h).astype(BF)
        slope = h + (pre * (h * (1.0 - h))) * (2.0 * GELU_A + 6.0 * GELU_B * square)
        g_pre = g_act * slope
        ref["dbu"][:, cols] += jnp.sum(g_pre, axis=0, keepdims=True)
        g_low = g_pre.astype(BF)
        total_up = total_up + dot_nn(act, wd)
        more = dot_nt(g_low, wu)
        total_back = more if total_back is None else total_back + more
        acc_d[cols, :] += dot_tn(act, low[...])
        acc_u[:, cols] += dot_tn(act2[...], g_low)
    ref["up"][...] = total_up
    if not last:
        ref["back"][...] = total_back
    else:
        e = total_back
        gain = vec(small, "g2")
        n, r = norm_parts(ref["hid"][...])
        eg = e * gain
        part = r * (
            eg - jnp.mean(eg, axis=-1, keepdims=True) - n * jnp.mean(eg * n, axis=-1, keepdims=True)
        )
        g_hidden = g_out + part
        ref["gh"][...] = g_hidden
        g_low = g_hidden.astype(BF)

        @pl.when(step == 0)
        def _():
            ref["sum"][...] = jnp.zeros_like(ref["sum"])
            ref["acc_o"][...] = jnp.zeros_like(ref["acc_o"])

        for i, term in enumerate((e * n, e, g_hidden, g_out, total_up * cot)):
            ref["sum"][i : i + 1, :] += jnp.sum(term, axis=0, keepdims=True)
        ref["acc_o"][...] += dot_nn(ref["a"][0], g_low)
        ref["ga"][0] = dot_nt(ref["wo"][...], g_low).astype(BF)

    @pl.when(step == final)
    def _():
        targets = [ref[name] for name in ("dw0", "dw1") if name in ref]
        sides, groups = targets[0].shape[1:3]
        at = 0
        for source in (acc_u, acc_d, ref["acc_o"]) if last else (acc_u, acc_d):
            own = source.shape[0] // members
            pack_all(targets, me, source, own, at)
            at += packed_rows(own, source.shape[1], sides, groups)


def mlp_call(base, share, first, last, values, form, members, deps):
    tokens, width = values["cot"].shape
    nseq, _, length = values["a"].shape
    span = share * members
    rows = length // 2
    row = pl.BlockSpec((rows, width), lambda i: (i, 0))
    col = pl.BlockSpec((1, width, rows), lambda i: (i // 2, 0, i % 2))
    f32row = jax.ShapeDtypeStruct((tokens, width), F32)
    ins = {
        "me": SMEM,
        "mix": SMEM,
        "cot": row,
        "small": whole(values["small"].shape),
    }
    parts = [(width // members, span), (span // members, width)]
    if last:
        parts.append((width // members, width))
    outs = {f"dw{i}": pair for i, pair in enumerate(packed_shapes(form, members, parts))}
    outs |= {
        "dbu": (whole((1, span)), jax.ShapeDtypeStruct((1, span), F32)),
        "up": (row, f32row),
    }
    scratch = {
        "acc_u": pltpu.VMEM((width, span), F32),
        "acc_d": pltpu.VMEM((span, width), F32),
        "low": pltpu.VMEM((rows, width), BF),
        "wu": pltpu.VMEM((width, span), BF),
        "wd": pltpu.VMEM((span, width), BF),
        "sems": pltpu.SemaphoreType.DMA((2, members)),
    }
    if first:
        ins |= {"x": row}
        outs |= {"hid": (row, f32row), "act": (row, jax.ShapeDtypeStruct((tokens, width), BF))}
    else:
        ins |= {"act": row, "up_in": row, "back_in": row}
    if last:
        ins |= {"hid": row}
        outs |= {
            "gh": (row, f32row),
            "ga": (col, jax.ShapeDtypeStruct(values["a"].shape, BF)),
            "sum": (whole((8, width)), jax.ShapeDtypeStruct((8, width), F32)),
        }
        scratch |= {"acc_o": pltpu.VMEM((width, width), F32)}
    else:
        outs |= {"back": (row, f32row)}
    if first or last:
        ins |= {"a": col, "wo": whole((width, width))}
    pieces = {(name, j): piece for name in ("wu", "wd") for j, piece in enumerate(values[name])}
    names = [*ins, *pieces, *(("dep", i) for i in range(len(deps))), *outs, *scratch]
    result = pl.pallas_call(
        lambda *refs: mlp_kernel(base, first, last, names, members, *refs),
        grid=(tokens // rows,),
        in_specs=[*ins.values(), *(ANY for _ in (*pieces, *deps))],
        out_specs=[spec for spec, _ in outs.values()],
        out_shape=[shape for _, shape in outs.values()],
        scratch_shapes=list(scratch.values()),
        compiler_params=params(62),
        cost_estimate=cost(45),
        name="mlp",
    )(*(values[name] for name in ins), *pieces.values(), *deps)
    return dict(zip(outs, result))


def qkv_grad_kernel(parts, deps, me_ref, act_ref, *refs):
    grads, targets, acc = refs[:parts], refs[parts + deps : -1], refs[-1]
    step = pl.program_id(0)
    last = pl.num_programs(0) - 1
    width = act_ref.shape[1]
    at = 0
    for g in grads:
        cols = slice(at, at + g.shape[1])
        at += g.shape[1]
        term = dot_tt(act_ref[...], g[0])
        acc[:, cols] = jnp.where(step == 0, term, acc[:, cols] + term)

    @pl.when(step == last)
    def _():
        split = len(targets)
        pack_all(targets, me_ref[0], acc, width // (targets[0].shape[0] * split), 0)


def turned_spec(v):
    return pl.BlockSpec((1, *v.shape[1:]), lambda s: (s, 0, 0))


def qkv_grad_call(me, grads, act, form, members, deps):
    tokens, width = act.shape
    nseq, _, length = grads[0].shape
    outs = packed_shapes(form, members, [(width // members, 3 * width)])
    return pl.pallas_call(
        lambda *refs: qkv_grad_kernel(len(grads), len(deps), *refs),
        grid=(nseq,),
        in_specs=[
            SMEM, pl.BlockSpec((length, width), lambda s: (s, 0)),
            *(turned_spec(g) for g in grads), *(ANY for _ in deps),
        ],
        out_specs=[spec for spec, _ in outs],
        out_shape=[shape for _, shape in outs],
        scratch_shapes=[pltpu.VMEM((width, 3 * width), F32)],
        compiler_params=params(62),
        cost_estimate=cost(13),
        name="qkv_grad",
    )(me, act, *grads, *deps)


def first_back_kernel(parts, deps, me_ref, shift_ref, x_ref, gh_ref, small_ref, *refs):
    smalls = refs[parts : parts + parts // 3 + 4]
    grads, pieces = refs[:parts], refs[parts + len(smalls) : -5 - deps]
    gx_ref, sum_ref, ring, w_ref, sems = refs[-5:]
    rows, width = x_ref.shape
    length = gx_ref.shape[0]
    seq, step = pl.program_id(0), pl.program_id(1)

    @pl.when((seq == 0) & (step == 0))
    def _():
        load_pieces(me_ref[0], pieces, w_ref, sems, True)
        sum_ref[...] = jnp.zeros_like(sum_ref)
        heads, (after, up0, up1, states) = smalls[:-4], smalls[-4:]
        for part in range(3):
            row = [sum(g[s, part, 0:1] for s in range(g.shape[0])) for g in heads]
            sum_ref[2 + part : 3 + part] = jnp.concatenate(row, axis=1)
        members = small_ref.shape[0]
        cuts = [v.shape[1] // members for v in (up0, up1)]
        segments = [
            v[:, m * cut : (m + 1) * cut] for m in range(members) for v, cut in zip((up0, up1), cuts)
        ]
        per = width // sum(cuts)
        for i in range(members // per):
            sum_ref[8 + i : 9 + i] = jnp.concatenate(segments[2 * per * i : 2 * per * (i + 1)], axis=1)
        for target, source, place, count in (
            (5, after, 2, 1), (6, after, 0, 2), (12, after, 3, 1), (13, states, 0, 4), (17, after, 4, 1)
        ):
            sum_ref[target : target + count] = source[place : place + count]
        load_pieces(me_ref[0], pieces, w_ref, sems, False)

    gain = vec(small_ref, "g1")
    e = dot_tt(jnp.concatenate([g[0] for g in grads], axis=0), w_ref[...])
    n, r = norm_parts(x_ref[...].astype(F32))
    eg = e * gain
    part = r * (
        eg - jnp.mean(eg, axis=-1, keepdims=True) - n * jnp.mean(eg * n, axis=-1, keepdims=True)
    )
    sum_ref[0:1] += jnp.sum(e * n, axis=0, keepdims=True)
    sum_ref[1:2] += jnp.sum(e, axis=0, keepdims=True)
    ring_put(ring, pl.multiple_of(step * rows, rows), gh_ref[...] + part)

    @pl.when(step == pl.num_programs(1) - 1)
    def _():
        gx_ref[...] = ring_get(ring, length - shift_ref[seq], length)


def first_back_call(me, shift, grads, x, gh, small, pieces, smalls, deps):
    tokens, width = x.shape
    nseq, _, length = grads[0].shape
    steps = 4
    rows = length // steps
    row = pl.BlockSpec((rows, width), lambda s, i: (s * steps + i, 0))
    return pl.pallas_call(
        lambda *refs: first_back_kernel(len(grads), len(deps), *refs),
        grid=(nseq, steps),
        in_specs=[
            SMEM, SMEM, row, row, whole(small.shape),
            *(pl.BlockSpec((1, g.shape[1], rows), lambda s, i: (s, 0, i)) for g in grads), *(whole(v.shape) for v in smalls),
            *(ANY for _ in (*pieces, *deps)),
        ],
        out_specs=[pl.BlockSpec((length, width), lambda s, i: (s, 0)), whole((24, width))],
        out_shape=[
            jax.ShapeDtypeStruct((tokens, width), F32),
            jax.ShapeDtypeStruct((24, width), F32),
        ],
        scratch_shapes=[
            ring_shape(length, width),
            pltpu.VMEM((width, 3 * width), BF),
            pltpu.SemaphoreType.DMA((len(pieces),)),
        ],
        compiler_params=params(62),
        cost_estimate=cost(20),
        name="first_back",
    )(me, shift, x, gh, small, *grads, *smalls, *pieces, *deps)


def states_kernel(mix_ref, e_ref, c_ref, part_ref, sum_ref):
    @pl.when(pl.program_id(0) == 0)
    def _():
        sum_ref[...] = jnp.zeros_like(sum_ref)

    cot = c_ref[...].astype(F32)
    total = None
    for j in range(e_ref.shape[0]):
        e = e_ref[j].astype(F32)
        term = mix_ref[j] * e
        total = term if total is None else total + term
        sum_ref[j : j + 1] += jnp.sum(e * cot, axis=0, keepdims=True)
    part_ref[...] = total


def states_call(mix, earlier, cot):
    states, tokens, width = earlier.shape
    rows = 256
    row = pl.BlockSpec((rows, width), lambda i: (i, 0))
    stack = pl.BlockSpec((states, rows, width), lambda i: (0, i, 0))
    return pl.pallas_call(
        states_kernel,
        grid=(tokens // rows,),
        in_specs=[SMEM, stack, row],
        out_specs=[row, whole((8, width))],
        out_shape=[
            jax.ShapeDtypeStruct((tokens, width), F32),
            jax.ShapeDtypeStruct((8, width), F32),
        ],
        compiler_params=params(62),
        cost_estimate=cost(11),
        name="states",
    )(mix, earlier, cot)


def spread_kernel(mix_ref, c_ref, *refs):
    out = refs[-1]
    cot = c_ref[...].astype(F32)
    for j in range(out.shape[0]):
        out[j] = mix_ref[j] * cot


def spread_call(states, mix, cot, deps):
    tokens, width = cot.shape
    rows = 256
    return pl.pallas_call(
        spread_kernel,
        grid=(tokens // rows,),
        in_specs=[SMEM, pl.BlockSpec((rows, width), lambda i: (i, 0)), *(ANY for _ in deps)],
        out_specs=pl.BlockSpec((states, rows, width), lambda i: (0, i, 0)),
        out_shape=jax.ShapeDtypeStruct((states, tokens, width), F32),
        compiler_params=params(62),
        cost_estimate=cost(20),
        name="spread",
    )(mix, cot, *deps)


def split_kernel(members, shares, wo_ref, wu_ref, wd_ref, *refs):
    outs = refs[-5:]
    outs[0][...] = wo_ref[...]
    deep = wu_ref.shape[1] // members
    base = 0
    for i, share in enumerate(shares):
        for m in range(members):
            outs[1 + i][:, m * share : (m + 1) * share] = wu_ref[:, m * deep + base : m * deep + base + share]
        outs[3 + i][...] = wd_ref[base : base + share]
        base += share


def split_call(members, shares, wo, wu, wd, deps):
    own = wu.shape[0]
    width = wd.shape[1]
    low = [(own, width), *((own, members * v) for v in shares), *((v, width) for v in shares)]
    full = pl.BlockSpec(memory_space=pltpu.VMEM)
    return pl.pallas_call(
        lambda *refs: split_kernel(members, shares, *refs),
        in_specs=[full, full, full, *(ANY for _ in deps)],
        out_specs=[full] * 5,
        out_shape=[jax.ShapeDtypeStruct(shape, BF) for shape in low],
        compiler_params=params(62),
        cost_estimate=cost(3),
        name="split",
    )(wo, wu, wd, *deps)


def mix_kernel(shift_ref, mix_ref, part_ref, b_ref, *refs):
    out_ref, ring = refs[-2:]
    length = b_ref.shape[0]
    ring_put(ring, 0, b_ref[...])
    rolled = ring_get(ring, length - shift_ref[pl.program_id(0)], length)
    out_ref[...] = (part_ref[...] + mix_ref[4] * rolled).astype(BF)


def mix_call(shift, mix, part, block_out, deps):
    tokens, width = part.shape
    nseq = shift.shape[0]
    length = tokens // nseq
    row = pl.BlockSpec((length, width), lambda s: (s, 0))
    return pl.pallas_call(
        mix_kernel,
        grid=(nseq,),
        in_specs=[SMEM, SMEM, row, row, *(ANY for _ in deps)],
        out_specs=row,
        out_shape=jax.ShapeDtypeStruct((tokens, width), BF),
        scratch_shapes=[ring_shape(length, width)],
        compiler_params=params(62),
        cost_estimate=cost(20),
        name="mix",
    )(shift, mix, part, block_out, *deps)


def swap(v, axis, bits):
    size = lax.axis_size(axis)
    return lax.ppermute(v, axis, [(i, i ^ bits) for i in range(size)])


def gate(arrays, deps):
    count = len(arrays)
    return pl.pallas_call(
        lambda *refs: None,
        in_specs=[ANY] * (count + len(deps)),
        out_specs=[ANY] * count,
        out_shape=[jax.ShapeDtypeStruct(v.shape, v.dtype) for v in arrays],
        input_output_aliases={i: i for i in range(count)},
        cost_estimate=cost(0.3),
        name="gate",
    )(*arrays, *deps)


def far_pieces(v):
    return [v, *(swap(v, "shard", 2 * k) for k in range(1, lax.axis_size("shard") // 2))]


def near_pieces(far, own=None):
    pieces = []
    for k, v in enumerate(far):
        pieces += [v, own if own is not None and k == 0 else swap(v, "shard", 1)]
    return pieces


def in_order(pieces, mine):
    stack = jnp.stack(pieces)
    return [lax.dynamic_index_in_dim(stack, j ^ mine, 0, keepdims=False) for j in range(len(pieces))]


def total_of(terms):
    total = terms[0].astype(F32)
    for term in terms[1:]:
        total = total + term.astype(F32)
    return total


def chain_start(pair):
    keep, send = pair
    return {"keep": keep, "near": swap(send, "shard", 1)}


def step_parts(kind, chain):
    if kind == "small":

        def body(idx, ins, outs):
            outs[0][...] = ins[0][...] + ins[1][...]

        return [(v, whole(v.shape)) for v in (chain["sum"], chain["got"])], [(*chain["sum"].shape, F32)], body
    keep, near = chain["keep"], chain["near"]
    chips, sides, groups, n, lanes = keep.shape
    half = (groups, n, lanes)

    def at(side):
        spec = pl.BlockSpec((1, 1, *half), lambda i, idx: (idx[0], side(idx), 0, 0, 0))
        deep = pl.BlockSpec((1, *half), lambda i, idx: (side(idx), 0, 0, 0))
        return [(keep, spec), (near, spec), *((far, deep) for far in chain["far"])]

    def total(refs, group):
        out = None
        for ref in refs:
            piece = ref[(0,) * (len(ref.shape) - 3) + (group,)].astype(F32)
            out = piece if out is None else out + piece
        return out

    if kind == "x":
        ins = []
        for k in range(1, chips):
            spec = pl.BlockSpec((1, sides, *half), lambda i, idx, k=k: (idx[0] ^ k, 0, 0, 0, 0))
            ins += [(keep, spec), (near, spec)]

        def body(idx, ins, outs):
            for k, out in enumerate(outs):
                out[...] = (ins[2 * k][0].astype(F32) + ins[2 * k + 1][0].astype(F32)).astype(BF)

        return ins, [(sides, *half)] * (chips - 1), body
    if kind == "y":

        def body(idx, ins, outs):
            for g in range(groups):
                outs[0][g] = total(ins, g).astype(BF)

        return at(lambda idx: 1 - idx[1]), [half], body
    if kind == "half":
        ins = [(v, whole(v.shape)) for v in (chain["done"], *chain["zg"])]

        def body(idx, ins, outs):
            for k, ref in enumerate(ins):
                outs[0][idx[2] ^ k] = ref[...]

        return ins, [half], body
    if kind == "z":

        def body(idx, ins, outs):
            for k in range(groups):
                outs[k][...] = total(ins, idx[2] ^ k).astype(outs[k].dtype)

        return [*at(lambda idx: idx[1]), (chain["yr"], whole(half))], [(n, lanes, F32), *[(n, lanes)] * (groups - 1)], body

    def body(idx, ins, outs):
        out = ins[0][...]
        for ref in ins[1:]:
            out = out + ref[...].astype(F32)
        outs[0][...] = out.astype(BF)

    return [(v, whole(v.shape)) for v in (chain["mine"], *chain["zr"])], [(n, lanes)], body


def step_call(idx, steps, deps):
    plans = [step_parts(kind, chain) for kind, chain in steps]
    ins = [pair for plan in plans for pair in plan[0]]
    outs = [shape for plan in plans for shape in plan[1]]
    types = [F32 if shape[-1] == F32 else BF for shape in outs]
    outs = [shape[:-1] if shape[-1] == F32 else shape for shape in outs]

    def kernel(idx_ref, *refs):
        at, out_at = 0, len(ins) + len(deps)
        for some, shapes, body in plans:
            body(idx_ref, refs[at : at + len(some)], refs[out_at : out_at + len(shapes)])
            at += len(some)
            out_at += len(shapes)

    results = pl.pallas_call(
        kernel,
        grid_spec=pltpu.PrefetchScalarGridSpec(
            num_scalar_prefetch=1,
            grid=(1,),
            in_specs=[*(spec for _, spec in ins), *(ANY for _ in deps)],
            out_specs=[whole(shape) for shape in outs],
        ),
        out_shape=[jax.ShapeDtypeStruct(shape, dtype) for shape, dtype in zip(outs, types)],
        compiler_params=params(62),
        cost_estimate=cost(3),
        name="_".join(["step", *(kind for kind, _ in steps)]),
    )(idx, *(v for v, _ in ins), *deps)
    at = 0
    others = range(1, lax.axis_size("rep") // 2)
    for (kind, chain), (_, shapes, _) in zip(steps, plans):
        sends = results[at : at + len(shapes)]
        at += len(shapes)
        if kind == "x":
            chain["far"] = [swap(v, "shard", 2 * (k + 1)) for k, v in enumerate(sends)]
        elif kind == "y":
            chain["yr"] = swap(sends[0], "rep", 1)
        elif kind == "z":
            chain["mine"] = sends[0]
            chain["zr"] = [swap(sends[k], "rep", 2 * k) for k in others]
        elif kind == "sum":
            chain["done"] = sends[0]
            chain["zg"] = [swap(sends[0], "rep", 2 * k) for k in others]
        elif kind == "half":
            chain["half"] = sends[0]
            chain["twin"] = swap(sends[0], "rep", 1)
        else:
            small_next(chain, sends[0])
    return results[0]


def small_next(chain, sums):
    chain["sum"] = sums
    count = chain["steps"] = chain.get("steps", -1) + 1
    bits = [("shard", 1 << b) for b in range(lax.axis_size("shard").bit_length() - 1)] + [("rep", 1)]
    if count < len(bits):
        chain["got"] = swap(sums, *bits[count])
    else:
        chain["got"] = [swap(sums, "rep", 2 * k) for k in range(1, lax.axis_size("rep") // 2)]


def small_end(chain, group):
    return total_of(in_order([chain["sum"], *chain["got"]], group))


def finish_call(idx, chains, plans, shapes, deps, us=4):
    ins = [v for chain in chains for v in (chain["half"], chain["twin"])]

    def kernel(idx_ref, *refs):
        outs = refs[len(ins) + len(deps) : len(ins) + len(deps) + len(shapes)]
        scratch = refs[-len(chains) :]
        for c, plan in enumerate(plans):
            both = scratch[c]
            both[idx_ref[1]] = refs[2 * c][...]
            both[1 - idx_ref[1]] = refs[2 * c + 1][...]
            sides, groups = both.shape[:2]
            at = 0
            for out, own, cols, place in plan:
                rows, wide = own // groups, cols // sides
                for j in range(wide // 128):
                    for side in range(sides):
                        for group in range(groups):
                            row, col = place(group * rows, side * wide + j * 128)
                            outs[out][row : row + rows, col : col + 128] = both[
                                side, group, at : at + rows, :
                            ].astype(F32)
                    at += rows

    return pl.pallas_call(
        kernel,
        in_specs=[SMEM, *(pl.BlockSpec(memory_space=pltpu.VMEM) for _ in ins), *(ANY for _ in deps)],
        out_specs=[pl.BlockSpec(memory_space=pltpu.VMEM) for _ in shapes],
        out_shape=[jax.ShapeDtypeStruct(shape, F32) for shape in shapes],
        scratch_shapes=[pltpu.VMEM((2, *chain["half"].shape), BF) for chain in chains],
        compiler_params=params(62),
        cost_estimate=cost(us),
        name="finish",
    )(idx, *ins, *deps)


def reduce_plain(packed):
    flat = packed.reshape(-1, 128)
    return lax.psum(lax.psum_scatter(flat, "shard", scatter_dimension=0, tiled=True), "rep")[None, None]


def reduce_small(v):
    for axis in ("shard", "rep"):
        bits = 1
        while bits < lax.axis_size(axis):
            v = v + swap(v, axis, bits)
            bits *= 2
    return v


def shards(
    inputs, earlier, segments, cotangent, mix_weights,
    ln1_gain, ln1_bias, qkv_weight, qkv_bias, out_weight, out_bias,
    ln2_gain, ln2_bias, up_weight, up_bias, down_weight, down_bias,
):
    nseq, length = segments.shape
    width = inputs.shape[1]
    blk = length // 2
    members, replicas = lax.axis_size("shard"), lax.axis_size("rep")
    me = lax.axis_index("shard").astype(jnp.int32)
    rep = lax.axis_index("rep").astype(jnp.int32)
    side = rep % 2
    me_ref = me[None]
    idx = jnp.stack([me // 2, side, rep // 2])
    own = width // members
    deep = down_weight.shape[0]
    ff = deep * members
    shares = [deep // 2, deep - deep // 2]
    fits = own % (8 * replicas) == 0 and all(v % (8 * replicas) == 0 and v % 128 == 0 for v in shares)
    form = (2, replicas // 2) if fits else (1, 1)

    wqkv = far_pieces(qkv_weight)
    wqkv_near = swap(qkv_weight, "shard", 1)
    vectors = [ln1_gain, ln1_bias, qkv_bias, out_bias, ln2_gain, ln2_bias, up_bias, down_bias]
    sizes = [v.shape[0] for v in vectors]
    wide = max(sizes)
    small = jnp.stack([jnp.pad(v, (0, wide - v.shape[0])) for v in vectors])
    small = [small, *(swap(small, "shard", k) for k in range(1, members))]
    small = jnp.stack(in_order(small, me))

    part, sums3 = states_call(mix_weights, earlier, cotangent)
    inv = np.exp(np.arange(HEAD // 2) * (-math.log(10000.0) / (HEAD // 2)))
    angles = np.arange(length)[None, :] * inv[:, None]
    tables = jnp.asarray(np.stack([np.cos(angles), np.sin(angles)]), F32)
    shift, xr, cr, act, seg, cos, sin = roll_call(inputs, cotangent, segments, small, tables, [sums3])
    if any(v % 128 for v in (deep, *shares)):

        def shared(v):
            halves = jnp.split(v.reshape(v.shape[0], members, deep), [shares[0]], axis=-1)
            return [h.reshape(v.shape[0], -1) for h in halves]

        pieces = [out_weight, *shared(up_weight), down_weight[: shares[0]], down_weight[shares[0] :]]
    else:
        pieces = split_call(members, shares, out_weight, up_weight, down_weight, [act, *wqkv])
    wo = lax.all_gather(pieces[0], "shard", axis=0, tiled=True)
    wd0, wd0_near = far_pieces(pieces[3]), swap(pieces[3], "shard", 1)
    wu0, wu0_near = far_pieces(pieces[1]), swap(pieces[1], "shard", 1)

    wqkv = near_pieces([qkv_weight, *gate(wqkv[1:], [act])], wqkv_near)
    qkv = qkv_call(me_ref, act, small, cos, sin, wqkv)
    o, lse = attend_call(seg, qkv)
    far = gate([*wd0[1:], *wu0[1:], pieces[2], pieces[4]], [lse])
    count = len(wd0) - 1
    wd0 = near_pieces([wd0[0], *far[:count]], wd0_near)
    wu0 = near_pieces([wu0[0], *far[count : 2 * count]], wu0_near)
    wu1, wd1 = far[2 * count :]
    wu1 = lax.all_gather(wu1, "shard", axis=0, tiled=True)
    wd1 = far_pieces(wd1)
    values = {"me": me_ref, "mix": mix_weights, "small": small, "x": xr, "cot": cr, "a": o, "wo": wo}
    got = mlp_call(0, shares[0], True, False, values | {"wu": wu0, "wd": wd0}, form, members, [])
    values |= {"up_in": got["up"], "back_in": got["back"], "hid": got["hid"], "act": got["act"]}
    wd1 = near_pieces(gate(wd1, [got["dbu"]]))
    first, dbu = [got[name] for name in ("dw0", "dw1") if name in got], [got["dbu"]]
    spread = [earlier.shape[0], mix_weights, cotangent]
    if fits:
        early = chain_start(first)
        earlier_grad = spread_call(*spread, [first[0]])
        deps = [step_call(idx, [("x", early)], [earlier_grad])]
    else:
        earlier_grad, deps = spread_call(*spread, []), []
    got = mlp_call(
        shares[0], shares[1], False, True, values | {"wu": [wu1], "wd": wd1}, form, members, deps
    )
    second = [got[name] for name in ("dw0", "dw1") if name in got]
    dbu.append(got["dbu"])
    block_out, gh, ga, sums2 = (got[name] for name in ("up", "gh", "ga", "sum"))

    groups = width // PAIR // 2
    back = [seg, qkv, o, ga, lse, cos, sin]

    def up_place(base, share):
        def place(row, col):
            return row, col // share * deep + base + col % share

        return place

    if fits:
        late = chain_start(second)
        t = step_call(idx, [("y", early)], [late["keep"]])
        gs = [attend_back_call(*back, 0, 2, [t])]
        t = step_call(idx, [("z", early), ("x", late)], [gs[0][0]])
        gs.append(attend_back_call(*back, 2, 2, [t]))
        t = step_call(idx, [("sum", early)], [gs[1][0]])
        for i in range(2, groups):
            gs.append(attend_back_call(*back, 2 * i, 2, [t, gs[-1][0]], 0.5))
        early["zg"] = gate(early["zg"], [gs[-1][0]])
        t = step_call(idx, [("y", late)], [gs[-1][0]])
        smalls = [*(g[3] for g in gs), sums2, *dbu, sums3]
        grads = [g[i] for i in range(3) for g in gs]
        pack = qkv_grad_call(me_ref, grads, act, form, members, [t])
        tail = chain_start(pack)
        t = step_call(idx, [("half", early), ("z", late)], [pack[0]])
        output = mix_call(shift, mix_weights, part, block_out, [t])
        t = step_call(idx, [("x", tail)], [output])
        input_grad, sums = first_back_call(me_ref, shift, grads, xr, gh, small, wqkv, smalls, [t])
        (early["twin"],) = gate([early["twin"]], [sums])
        sums_dep = [sums, early["twin"]]
        sums_chain = {}
        small_next(sums_chain, sums)
        t = step_call(idx, [("sum", late), ("y", tail)], sums_dep)
        t = step_call(idx, [("half", late), ("z", tail), ("small", sums_chain)], [])
        t = step_call(idx, [("sum", tail), ("small", sums_chain)], [])
        d_up, d_down, d_out = finish_call(
            idx,
            [early, late],
            [
                [
                    (0, own, shares[0] * members, up_place(0, shares[0])),
                    (1, shares[0], width, lambda row, col: (row, col)),
                ],
                [
                    (0, own, shares[1] * members, up_place(shares[0], shares[1])),
                    (1, shares[1], width, lambda row, col: (row + shares[0], col)),
                    (2, own, width, lambda row, col: (row, col)),
                ],
            ],
            [(own, ff), (deep, width), (own, width)],
            [t],
        )
        t = step_call(idx, [("half", tail)], [d_out])
        step_call(idx, [("small", sums_chain)], [t])
        (d_qkv,) = finish_call(
            idx, [tail], [[(0, own, 3 * width, lambda row, col: (row, col))]], [(own, 3 * width)], [], 0.01
        )
        sums_chain["got"] = gate(sums_chain["got"], [d_qkv])
        flat = small_end(sums_chain, rep // 2).reshape(-1)
    else:
        gs = [attend_back_call(*back, 2 * i, 2, []) for i in range(groups)]
        smalls = [*(g[3] for g in gs), sums2, *dbu, sums3]
        grads = [g[i] for i in range(3) for g in gs]
        pack = qkv_grad_call(me_ref, grads, act, form, members, [])
        output = mix_call(shift, mix_weights, part, block_out, [])
        input_grad, sums = first_back_call(me_ref, shift, grads, xr, gh, small, wqkv, smalls, [])
        ups, downs = [], []
        first, second, third = [reduce_plain(p[0]) for p in (first, second, pack)]
        for v, share in ((first, shares[0]), (second, shares[1])):
            at = packed_rows(own, share * members, *v.shape[:2])
            ups.append(unpack(v, 0, own, share * members).reshape(own, members, share))
            downs.append(unpack(v, at, share, width))
            at += packed_rows(share, width, *v.shape[:2])
        d_out = unpack(second, at, own, width).astype(F32)
        d_up = jnp.concatenate(ups, axis=2).reshape(own, -1).astype(F32)
        d_down = jnp.concatenate(downs, axis=0).astype(F32)
        d_qkv = unpack(third, 0, own, 3 * width).astype(F32)
        flat = reduce_small(sums).reshape(-1)

    parts, at = [], 0
    for size in sizes:
        parts.append(lax.dynamic_slice(flat, (at + me * size,), (size,)))
        at += size * members
    mix_grad = jnp.sum(flat[at : at + 5 * width].reshape(5, width), axis=1)
    return (
        output, input_grad, earlier_grad, mix_grad,
        parts[0], parts[1], d_qkv, parts[2], d_out, parts[3], parts[4], parts[5],
        d_up, parts[6], d_down, parts[7],
    )


def solution(mesh):
    rows, shard = P(("rep", "shard"), None), P("shard")
    mat, deep = P("shard", None), P(None, ("rep", "shard"), None)
    return jax.shard_map(
        shards,
        mesh=mesh,
        in_specs=(
            rows, deep, rows, rows, P(),
            shard, shard, mat, shard, mat, shard, shard, shard, mat, shard, mat, shard,
        ),
        out_specs=(
            rows, rows, deep, P(),
            shard, shard, mat, shard, mat, shard, shard, shard, mat, shard, mat, shard,
        ),
        check_vma=False,
    )
```

```python
import math

import jax
import jax.numpy as jnp
import numpy as np
from jax import lax
from jax.experimental import pallas as pl
from jax.experimental.pallas import tpu as pltpu
from jax.sharding import PartitionSpec as P

HEADS = 12
HEAD = 64
PAIR = 2 * HEAD
EPSILON = 1e-05
LOG2E = math.log2(math.e)
NEG = -1e30
GELU_A = math.sqrt(2.0 / math.pi)
GELU_B = GELU_A * 0.044715
BF = jnp.bfloat16
F32 = jnp.float32
MIB = 1 << 20

COST_SHARE = 1.5


def cost(us):
    return pl.CostEstimate(flops=int(us * COST_SHARE * 1.15e9), bytes_accessed=1024, transcendentals=0)


def dot_nn(a, b):
    return lax.dot_general(a, b, (((1,), (0,)), ((), ())), preferred_element_type=F32)


def dot_nt(a, b):
    return lax.dot_general(a, b, (((1,), (1,)), ((), ())), preferred_element_type=F32)


def dot_tn(a, b):
    return lax.dot_general(a, b, (((0,), (0,)), ((), ())), preferred_element_type=F32)


def dot_tt(a, b):
    return lax.dot_general(a, b, (((0,), (1,)), ((), ())), preferred_element_type=F32)


def params(vmem):
    return pltpu.CompilerParams(vmem_limit_bytes=vmem * MIB)


ANY = pl.BlockSpec(memory_space=pl.ANY)


def load_pieces(me, pieces, target, sems, start, cols=None):
    copies = []
    for j, piece in enumerate(pieces):
        rows = piece.shape[0]
        at = pl.multiple_of((me ^ j) * rows, rows)
        source = piece if cols is None else piece.at[:, cols]
        copies.append(pltpu.make_async_copy(source, target.at[pl.ds(at, rows), :], sems.at[j]))
    for copy in copies:
        if start:
            copy.start()
        else:
            copy.wait()


def pack(target, source, base, own, sides, groups, at):
    rows, cols = own // groups, source.shape[-1] // sides
    for side in range(sides):
        for group in range(groups):
            for j in range(cols // 128):
                here = at + j * rows
                col = side * cols + j * 128
                target[side, group, here : here + rows, :] = source[
                    pl.ds(base + group * rows, rows), col : col + 128
                ].astype(BF)


def pack_all(targets, me, source, own, at):
    for t, target in enumerate(targets):
        count, sides, groups = target.shape[:3]
        for i in range(count):
            place = i if len(targets) == 1 else 2 * i + ((me % 2) ^ t)
            pack(target.at[i], source, pl.multiple_of(place * own, own), own, sides, groups, at)


def unpack(v, at, own, cols):
    sides, groups = v.shape[:2]
    rows, wide = own // groups, cols // sides
    count = wide // 128
    part = v[:, :, at : at + rows * count].reshape(sides, groups, count, rows, 128)
    return part.transpose(1, 3, 0, 2, 4).reshape(own, cols)


def packed_rows(own, cols, sides, groups):
    return own * cols // (128 * sides * groups)


def packed_shapes(form, members, own_cols):
    sides, groups = form
    n = sum(packed_rows(own, cols, sides, groups) for own, cols in own_cols)
    split = 1 if form == (1, 1) else 2
    shape = (members // split, sides, groups, n, 128)
    return [(whole(shape), jax.ShapeDtypeStruct(shape, BF)) for _ in range(split)]


def whole(shape):
    zeros = (0,) * len(shape)
    return pl.BlockSpec(shape, lambda *_: zeros, pipeline_mode=pl.Buffered(1))


SMEM = pl.BlockSpec(memory_space=pltpu.SMEM)


def ring_shape(length, width):
    return pltpu.VMEM((width // 128, 2 * length, 128), F32)


def ring_put(ring, at, value):
    for j in range(ring.shape[0]):
        part = value[:, j * 128 : (j + 1) * 128]
        ring[j, pl.ds(at, value.shape[0]), :] = part
        ring[j, pl.ds(ring.shape[1] // 2 + at, value.shape[0]), :] = part


def ring_get(ring, start, rows):
    return jnp.concatenate([ring[j, pl.ds(start, rows), :] for j in range(ring.shape[0])], axis=1)


def norm_parts(v):
    mean = jnp.mean(v, axis=-1, keepdims=True)
    centred = v - mean
    var = jnp.mean(centred * centred, axis=-1, keepdims=True)
    r = lax.rsqrt(var + EPSILON)
    return centred * r, r


ROWS = ("g1", "b1", "bqkv", "bo", "g2", "b2", "bu", "bd")
FF_RATIO = 4


def vec(ref, name, base=0, share=None):
    row = ROWS.index(name)
    size = share or ref.shape[2] // FF_RATIO
    parts = [ref[m, row : row + 1, base : base + size] for m in range(ref.shape[0])]
    return jnp.concatenate(parts, axis=1).astype(F32)


def column(row):
    return jnp.broadcast_to(row, (128, row.shape[1])).T[:, :1]


def roll_kernel(x_ref, cot_ref, seg_ref, small_ref, tab_ref, *refs):
    shift_ref, xr_ref, cr_ref, act_ref, seg_out, cos_ref, sin_ref, ring = refs[-8:]
    length = x_ref.shape[0]
    half = length // 2
    seg = jnp.broadcast_to(seg_ref[0].astype(F32), (8, length))
    place = lax.broadcasted_iota(jnp.int32, (8, length), 1)
    same = (seg == pltpu.roll(seg, length - (half - 1), 1)) & (place <= half)
    shift = jnp.min(jnp.where(same, place.astype(F32), float(length))).astype(jnp.int32)
    shift_ref[pl.program_id(0)] = shift
    back = lax.rem(length - shift, length)
    seg_out[0] = pltpu.roll(seg, back, 1)[:, half:]
    cos_ref[0] = pltpu.roll(tab_ref[0], back, 1)
    sin_ref[0] = pltpu.roll(tab_ref[1], back, 1)
    for source, target in ((cot_ref, cr_ref), (x_ref, xr_ref)):
        ring_put(ring, 0, source[...].astype(F32))
        target[...] = ring_get(ring, shift, length).astype(BF)
    gain, bias = vec(small_ref, "g1"), vec(small_ref, "b1")
    rows = 256
    for at in range(0, length, rows):
        n, _ = norm_parts(xr_ref[at : at + rows].astype(F32))
        act_ref[at : at + rows] = (n * gain + bias).astype(BF)


def roll_call(x, cot, seg, small, tables, deps):
    tokens, width = x.shape
    nseq, length = seg.shape
    row = pl.BlockSpec((length, width), lambda s: (s, 0))
    tab = pl.BlockSpec((1, HEAD // 2, length), lambda s: (s, 0, 0))
    low = jax.ShapeDtypeStruct((tokens, width), BF)
    turn = jax.ShapeDtypeStruct((nseq, HEAD // 2, length), F32)
    return pl.pallas_call(
        roll_kernel,
        grid=(nseq,),
        in_specs=[
            row, row, pl.BlockSpec((1, 1, length), lambda s: (s, 0, 0)), whole(small.shape), whole(tables.shape),
            *(ANY for _ in deps),
        ],
        out_specs=[SMEM, row, row, row, pl.BlockSpec((1, 8, length // 2), lambda s: (s, 0, 0)), tab, tab],
        out_shape=[
            jax.ShapeDtypeStruct((nseq,), jnp.int32), low, low, low,
            jax.ShapeDtypeStruct((nseq, 8, length // 2), F32), turn, turn,
        ],
        scratch_shapes=[ring_shape(length, width)],
        compiler_params=params(62),
        cost_estimate=cost(10),
        name="roll",
    )(x, cot, seg[:, None, :], small, tables, *deps)


def qkv_kernel(me_ref, act_ref, small_ref, cos_ref, sin_ref, *refs):
    pieces, (out_ref, w_ref, sems) = refs[:-3], refs[-3:]
    width = act_ref.shape[1]
    half = HEAD // 2
    rows = 256
    bias = vec(small_ref, "bqkv", 0, 3 * width // small_ref.shape[0])

    def load(part, start):
        cols = slice(part * width, (part + 1) * width)
        load_pieces(me_ref[0], pieces, w_ref.at[part], sems.at[part], start, cols)

    @pl.when((pl.program_id(0) == 0) & (pl.program_id(1) == 0))
    def _():
        for part in range(3):
            load(part, True)

    def project(part):
        @pl.when(pl.program_id(0) == 0)
        def _():
            load(part, False)

        cos, sin = cos_ref[0], sin_ref[0]
        for base in range(0, width, rows):
            cols = slice(base, base + rows)
            at = part * width + base
            y = dot_tt(w_ref[part, :, cols], act_ref[...]) + column(bias[:, at : at + rows])
            if part == 2:
                out_ref[0, base : base + rows, :] = y.astype(BF)
                continue
            for h in range(0, rows, HEAD):
                u, w = y[h : h + half], y[h + half : h + HEAD]
                a, b = u * cos - w * sin, w * cos + u * sin
                if part == 0:
                    a, b = a * (LOG2E * HEAD**-0.5), b * (LOG2E * HEAD**-0.5)
                out_ref[0, base + h : base + h + half, :] = a.astype(BF)
                out_ref[0, base + h + half : base + h + HEAD, :] = b.astype(BF)

    for part in range(3):
        pl.when(pl.program_id(1) == part)(lambda part=part: project(part))


def qkv_call(me, act, small, cos, sin, pieces):
    tokens, width = act.shape
    nseq, _, length = cos.shape
    tab = pl.BlockSpec((1, HEAD // 2, length), lambda s, p: (s, 0, 0))
    return pl.pallas_call(
        qkv_kernel,
        grid=(nseq, 3),
        in_specs=[
            SMEM, pl.BlockSpec((length, width), lambda s, p: (s, 0)), whole(small.shape), tab, tab,
            *(ANY for _ in pieces),
        ],
        out_specs=pl.BlockSpec((1, None, width, length), lambda s, p: (s, p, 0, 0)),
        out_shape=jax.ShapeDtypeStruct((nseq, 3, width, length), BF),
        scratch_shapes=[
            pltpu.VMEM((3, width, width), BF),
            pltpu.SemaphoreType.DMA((3, len(pieces))),
        ],
        compiler_params=params(62),
        cost_estimate=cost(15),
        name="qkv",
    )(me, act, small, cos, sin, *pieces)


def head_specs(base):
    return [
        lambda length, part=part: pl.BlockSpec((1, None, PAIR, length), lambda s, h: (s, part, base + h, 0))
        for part in range(3)
    ]


def fill_masks(seg_ref, mask, blk):
    row = seg_ref[0, 0:1, :]
    col = column(row)
    kk = lax.broadcasted_iota(jnp.int32, (blk, blk), 0)
    qq = lax.broadcasted_iota(jnp.int32, (blk, blk), 1)
    causal = kk <= qq
    mask[0] = jnp.where(causal, 0.0, NEG)
    for i, (kb, qb) in enumerate(((0, 0), (0, 1), (1, 1))):
        same = col[kb * blk : (kb + 1) * blk] == row[:, qb * blk : (qb + 1) * blk]
        keep = same if kb != qb else same & causal
        mask[1 + i] = jnp.where(keep, 0.0, NEG)


def scores_of(keys, query, mask, half, qb, blk):
    top = dot_nn(keys[: (qb + 1) * blk], query)
    if half == 0:
        diag = top[qb * blk :] + mask[0]
        return diag if qb == 0 else jnp.concatenate([top[:blk], diag], axis=0)
    if qb == 0:
        return top + mask[1]
    return jnp.concatenate([top[:blk] + mask[2], top[blk:] + mask[3]], axis=0)


def one_head(pair_rows, head):
    zero = jnp.zeros((HEAD, pair_rows.shape[1]), pair_rows.dtype)
    rows = pair_rows[head * HEAD : (head + 1) * HEAD]
    return jnp.concatenate([rows, zero] if head == 0 else [zero, rows], axis=0)


def attend_kernel(seg_ref, q_ref, k_ref, v_ref, o_ref, l_ref, mask):
    length = q_ref.shape[2]
    blk = length // 4

    @pl.when(pl.program_id(1) == 0)
    def _():
        fill_masks(seg_ref, mask, blk)

    units = [(half, head, qb) for qb in range(2) for half in range(2) for head in range(2)]
    keys = [k_ref[0, :, half * 2 * blk : (half + 1) * 2 * blk].T for half in range(2)]

    def place(half, head, qb):
        base = half * 2 * blk
        qs = slice(base + qb * blk, base + (qb + 1) * blk)
        return base, qs, slice(head * HEAD, (head + 1) * HEAD)

    scores = []
    for half, head, qb in units:
        _, qs, _ = place(half, head, qb)
        scores.append(scores_of(keys[half], one_head(q_ref[0, :, qs], head), mask, half, qb, blk))
    tops = [jnp.max(s, axis=0, keepdims=True) for s in scores]
    probs = [jnp.exp2(s - top) for s, top in zip(scores, tops)]
    totals = [jnp.sum(p, axis=0, keepdims=True) for p in probs]
    lows = [p.astype(BF) for p in probs]
    for (half, head, qb), p, top, total in zip(units, lows, tops, totals):
        base, qs, hs = place(half, head, qb)
        o = dot_nn(v_ref[0, hs, base : base + (qb + 1) * blk], p)
        o_ref[0, hs, qs] = (o / total).astype(BF)
        l_ref[0, 0, head : head + 1, qs] = top + jnp.log2(total)


def attend_call(seg, qkv):
    nseq, _, width, length = qkv.shape
    pairs = width // PAIR
    blk = length // 4
    blockspec = pl.BlockSpec((1, PAIR, length), lambda s, h: (s, h, 0))
    return pl.pallas_call(
        attend_kernel,
        grid=(nseq, pairs),
        in_specs=[
            pl.BlockSpec((1, 8, 2 * blk), lambda s, h: (s, 0, 0)),
            *(spec(length) for spec in head_specs(0)),
        ],
        out_specs=[blockspec, pl.BlockSpec((1, 1, 2, length), lambda s, h: (s, h, 0, 0))],
        out_shape=[
            jax.ShapeDtypeStruct((nseq, width, length), BF),
            jax.ShapeDtypeStruct((nseq, pairs, 2, length), F32),
        ],
        scratch_shapes=[pltpu.VMEM((4, blk, blk), F32)],
        compiler_params=params(62),
        cost_estimate=cost(30),
        name="attend",
    )(seg, qkv, qkv, qkv)


def attend_back_kernel(
    seg_ref, q_ref, k_ref, v_ref, o_ref, g_ref, l_ref, cos_ref, sin_ref, *refs
):
    gq_ref, gk_ref, gv_ref, sum_ref, mask, turn = refs[-6:]
    length = q_ref.shape[2]
    blk = length // 4
    hd = HEAD // 2

    @pl.when(pl.program_id(1) == 0)
    def _():
        fill_masks(seg_ref, mask, blk)

    units = [(half, head, qb) for qb in range(2) for half in range(2) for head in range(2)]
    keys = [k_ref[0, :, half * 2 * blk : (half + 1) * 2 * blk].T for half in range(2)]
    values = [v_ref[0, :, half * 2 * blk : (half + 1) * 2 * blk].T for half in range(2)]

    def place(half, head, qb):
        base = half * 2 * blk
        qs = slice(base + qb * blk, base + (qb + 1) * blk)
        return base, qs, slice(head * HEAD, (head + 1) * HEAD)

    def products(unit):
        half, head, qb = unit
        _, qs, hs = place(*unit)
        s = scores_of(keys[half], one_head(q_ref[0, :, qs], head), mask, half, qb, blk)
        gp = dot_nn(values[half][: (qb + 1) * blk], one_head(g_ref[0, :, qs], head))
        g = g_ref[0, hs, qs].astype(F32) * o_ref[0, hs, qs].astype(F32)
        return s, gp, jnp.sum(g, axis=0, keepdims=True)

    def softmax(unit, held):
        s, gp, delta = held
        _, qs, _ = place(*unit)
        p = jnp.exp2(s - l_ref[0, 0, unit[1] : unit[1] + 1, qs])
        return p.astype(BF), (p * (gp - delta)).astype(BF)

    def finish(unit, pair):
        half, head, qb = unit
        p, ds = pair
        base, qs, hs = place(*unit)
        dv = dot_nt(g_ref[0, hs, qs], p)
        dk = dot_nt(q_ref[0, hs, qs], ds)
        turn[0, hs, qs] = dot_nn(k_ref[0, hs, base : base + (qb + 1) * blk], ds)
        first_half, second_half = slice(base, base + blk), slice(base + blk, base + 2 * blk)
        if qb == 0:
            turn[1, hs, first_half], turn[2, hs, first_half] = dk, dv
        else:
            turn[1, hs, first_half] += dk[:, :blk]
            turn[2, hs, first_half] += dv[:, :blk]
            turn[1, hs, second_half], turn[2, hs, second_half] = dk[:, blk:], dv[:, blk:]

    before = None
    for unit in (*units, None):
        held = products(unit) if unit else None
        if before:
            finish(before[0], softmax(*before))
        before = (unit, held)
    cos, sin = cos_ref[0], sin_ref[0]

    ones = jnp.ones((8, length), BF)
    for part, (out, scale) in enumerate(((gq_ref, HEAD**-0.5), (gk_ref, 1.0 / LOG2E), (gv_ref, 1.0))):
        for head in range(2):
            at = head * HEAD
            u = turn[part, at : at + hd]
            w = turn[part, at + hd : at + HEAD]
            if part < 2:
                u, w = (u * cos + w * sin) * scale, (w * cos - u * sin) * scale
            out[0, at : at + hd, :] = u.astype(BF)
            out[0, at + hd : at + HEAD, :] = w.astype(BF)
        sum_ref[0, part] = dot_nt(ones, out[0])


def attend_back_call(seg, qkv, o, g, lse, cos, sin, base, pairs, deps, us=15):
    nseq, _, _, length = qkv.shape
    blk = length // 4
    source = pl.BlockSpec((1, PAIR, length), lambda s, h: (s, base + h, 0))
    target = pl.BlockSpec((1, PAIR, length), lambda s, h: (s, h, 0))
    tab = pl.BlockSpec((1, HEAD // 2, length), lambda s, h: (s, 0, 0))
    turned = jax.ShapeDtypeStruct((nseq, pairs * PAIR, length), BF)
    return pl.pallas_call(
        attend_back_kernel,
        grid=(nseq, pairs),
        in_specs=[
            pl.BlockSpec((1, 8, 2 * blk), lambda s, h: (s, 0, 0)),
            *(spec(length) for spec in head_specs(base)), source, source,
            pl.BlockSpec((1, 1, 2, length), lambda s, h: (s, base + h, 0, 0)),
            tab, tab, *(ANY for _ in deps),
        ],
        out_specs=[
            target, target, target,
            pl.BlockSpec((1, 3, 8, PAIR), lambda s, h: (s, 0, 0, h)),
        ],
        out_shape=[turned, turned, turned, jax.ShapeDtypeStruct((nseq, 3, 8, pairs * PAIR), F32)],
        scratch_shapes=[pltpu.VMEM((4, blk, blk), F32), pltpu.VMEM((3, PAIR, length), F32)],
        compiler_params=params(62),
        cost_estimate=cost(us),
        name="attend_back",
    )(seg, qkv, qkv, qkv, o, g, lse, cos, sin, *deps)


def mlp_kernel(base, first, last, names, members, *refs):
    ref = dict(zip(names, refs))
    rows, width = ref["cot"].shape
    step = pl.program_id(0)
    final = pl.num_programs(0) - 1
    acc_u, acc_d, low = ref["acc_u"], ref["acc_d"], ref["low"]
    span = acc_u.shape[1]
    me, sems = ref["me"][0], ref["sems"]
    share = span // members
    small = ref["small"]

    def weights(names, start):
        for i, name in names:
            load_pieces(me, [ref[key] for key in ref if key[0] == name], ref[name], sems.at[i], start)

    named = list(enumerate(("wo", "wu", "wd")))[0 if first or last else 1 :]

    @pl.when(step == 0)
    def _():
        weights(named, True)
        acc_u[...] = jnp.zeros_like(acc_u)
        acc_d[...] = jnp.zeros_like(acc_d)
        ref["dbu"][...] = jnp.zeros_like(ref["dbu"])

    alpha = ref["mix"][4]
    cot = ref["cot"][...].astype(F32)
    g_out = cot * alpha
    low[...] = g_out.astype(BF)

    @pl.when(step == 0)
    def _():
        weights(named[:1], False)

    if first:
        hidden = ref["x"][...].astype(F32) + dot_tn(ref["a"][0], ref["wo"][...]) + vec(small, "bo")
        n, _ = norm_parts(hidden)
        ref["hid"][...] = hidden
        ref["act"][...] = (n * vec(small, "g2") + vec(small, "b2")).astype(BF)

    @pl.when(step == 0)
    def _():
        weights(named[1:], False)

    act2 = ref["act"]
    if first:
        total_up = ref["hid"][...] + vec(small, "bd")
        total_back = None
    else:
        total_up, total_back = ref["up_in"][...], ref["back_in"][...]
    chunk = width
    bu = vec(small, "bu", base, share)
    for at in range(0, span, chunk):
        cols = slice(at, at + chunk)
        wu, wd = ref["wu"][:, cols], ref["wd"][cols, :]
        pre = dot_nn(act2[...], wu) + bu[:, cols]
        g_act = dot_nt(low[...], wd)
        square = pre * pre
        h = 0.5 + 0.5 * jnp.tanh(pre * (GELU_A + GELU_B * square))
        act = (pre * h).astype(BF)
        slope = h + (pre * (h * (1.0 - h))) * (2.0 * GELU_A + 6.0 * GELU_B * square)
        g_pre = g_act * slope
        ref["dbu"][:, cols] += jnp.sum(g_pre, axis=0, keepdims=True)
        g_low = g_pre.astype(BF)
        total_up = total_up + dot_nn(act, wd)
        more = dot_nt(g_low, wu)
        total_back = more if total_back is None else total_back + more
        acc_d[cols, :] += dot_tn(act, low[...])
        acc_u[:, cols] += dot_tn(act2[...], g_low)
    ref["up"][...] = total_up
    if not last:
        ref["back"][...] = total_back
    else:
        e = total_back
        gain = vec(small, "g2")
        n, r = norm_parts(ref["hid"][...])
        eg = e * gain
        part = r * (
            eg - jnp.mean(eg, axis=-1, keepdims=True) - n * jnp.mean(eg * n, axis=-1, keepdims=True)
        )
        g_hidden = g_out + part
        ref["gh"][...] = g_hidden
        g_low = g_hidden.astype(BF)

        @pl.when(step == 0)
        def _():
            ref["sum"][...] = jnp.zeros_like(ref["sum"])
            ref["acc_o"][...] = jnp.zeros_like(ref["acc_o"])

        for i, term in enumerate((e * n, e, g_hidden, g_out, total_up * cot)):
            ref["sum"][i : i + 1, :] += jnp.sum(term, axis=0, keepdims=True)
        ref["acc_o"][...] += dot_nn(ref["a"][0], g_low)
        ref["ga"][0] = dot_nt(ref["wo"][...], g_low).astype(BF)

    @pl.when(step == final)
    def _():
        targets = [ref[name] for name in ("dw0", "dw1") if name in ref]
        sides, groups = targets[0].shape[1:3]
        at = 0
        for source in (acc_u, acc_d, ref["acc_o"]) if last else (acc_u, acc_d):
            own = source.shape[0] // members
            pack_all(targets, me, source, own, at)
            at += packed_rows(own, source.shape[1], sides, groups)


def mlp_call(base, share, first, last, values, form, members, deps):
    tokens, width = values["cot"].shape
    nseq, _, length = values["a"].shape
    span = share * members
    rows = length // 2
    row = pl.BlockSpec((rows, width), lambda i: (i, 0))
    col = pl.BlockSpec((1, width, rows), lambda i: (i // 2, 0, i % 2))
    f32row = jax.ShapeDtypeStruct((tokens, width), F32)
    ins = {
        "me": SMEM,
        "mix": SMEM,
        "cot": row,
        "small": whole(values["small"].shape),
    }
    parts = [(width // members, span), (span // members, width)]
    if last:
        parts.append((width // members, width))
    outs = {f"dw{i}": pair for i, pair in enumerate(packed_shapes(form, members, parts))}
    outs |= {
        "dbu": (whole((1, span)), jax.ShapeDtypeStruct((1, span), F32)),
        "up": (row, f32row),
    }
    scratch = {
        "acc_u": pltpu.VMEM((width, span), F32),
        "acc_d": pltpu.VMEM((span, width), F32),
        "low": pltpu.VMEM((rows, width), BF),
        "wu": pltpu.VMEM((width, span), BF),
        "wd": pltpu.VMEM((span, width), BF),
        "sems": pltpu.SemaphoreType.DMA((3, members)),
    }
    if first:
        ins |= {"x": row}
        outs |= {"hid": (row, f32row), "act": (row, jax.ShapeDtypeStruct((tokens, width), BF))}
    else:
        ins |= {"act": row, "up_in": row, "back_in": row}
    if last:
        ins |= {"hid": row}
        outs |= {
            "gh": (row, f32row),
            "ga": (col, jax.ShapeDtypeStruct(values["a"].shape, BF)),
            "sum": (whole((8, width)), jax.ShapeDtypeStruct((8, width), F32)),
        }
        scratch |= {"acc_o": pltpu.VMEM((width, width), F32)}
    else:
        outs |= {"back": (row, f32row)}
    if first or last:
        ins |= {"a": col}
        scratch |= {"wo": pltpu.VMEM((width, width), BF)}
    pieces = {(name, j): piece for name in ("wo", "wu", "wd") for j, piece in enumerate(values[name])}
    names = [*ins, *pieces, *(("dep", i) for i in range(len(deps))), *outs, *scratch]
    result = pl.pallas_call(
        lambda *refs: mlp_kernel(base, first, last, names, members, *refs),
        grid=(tokens // rows,),
        in_specs=[*ins.values(), *(ANY for _ in (*pieces, *deps))],
        out_specs=[spec for spec, _ in outs.values()],
        out_shape=[shape for _, shape in outs.values()],
        scratch_shapes=list(scratch.values()),
        compiler_params=params(62),
        cost_estimate=cost(45),
        name="mlp",
    )(*(values[name] for name in ins), *pieces.values(), *deps)
    return dict(zip(outs, result))


def qkv_grad_kernel(parts, deps, me_ref, act_ref, *refs):
    grads, targets, acc = refs[:parts], refs[parts + deps : -1], refs[-1]
    step = pl.program_id(0)
    last = pl.num_programs(0) - 1
    width = act_ref.shape[1]
    at = 0
    for g in grads:
        cols = slice(at, at + g.shape[1])
        at += g.shape[1]
        term = dot_tt(act_ref[...], g[0])
        acc[:, cols] = jnp.where(step == 0, term, acc[:, cols] + term)

    @pl.when(step == last)
    def _():
        split = len(targets)
        pack_all(targets, me_ref[0], acc, width // (targets[0].shape[0] * split), 0)


def turned_spec(v):
    return pl.BlockSpec((1, *v.shape[1:]), lambda s: (s, 0, 0))


def qkv_grad_call(me, grads, act, form, members, deps):
    tokens, width = act.shape
    nseq, _, length = grads[0].shape
    outs = packed_shapes(form, members, [(width // members, 3 * width)])
    return pl.pallas_call(
        lambda *refs: qkv_grad_kernel(len(grads), len(deps), *refs),
        grid=(nseq,),
        in_specs=[
            SMEM, pl.BlockSpec((length, width), lambda s: (s, 0)),
            *(turned_spec(g) for g in grads), *(ANY for _ in deps),
        ],
        out_specs=[spec for spec, _ in outs],
        out_shape=[shape for _, shape in outs],
        scratch_shapes=[pltpu.VMEM((width, 3 * width), F32)],
        compiler_params=params(62),
        cost_estimate=cost(13),
        name="qkv_grad",
    )(me, act, *grads, *deps)


def first_back_kernel(parts, deps, me_ref, shift_ref, x_ref, gh_ref, small_ref, *refs):
    smalls = refs[parts : parts + parts // 3 + 4]
    grads, pieces = refs[:parts], refs[parts + len(smalls) : -5 - deps]
    gx_ref, sum_ref, ring, w_ref, sems = refs[-5:]
    rows, width = x_ref.shape
    length = gx_ref.shape[0]
    seq, step = pl.program_id(0), pl.program_id(1)

    @pl.when((seq == 0) & (step == 0))
    def _():
        load_pieces(me_ref[0], pieces, w_ref, sems, True)
        sum_ref[...] = jnp.zeros_like(sum_ref)
        heads, (after, up0, up1, states) = smalls[:-4], smalls[-4:]
        for part in range(3):
            row = [sum(g[s, part, 0:1] for s in range(g.shape[0])) for g in heads]
            sum_ref[2 + part : 3 + part] = jnp.concatenate(row, axis=1)
        members = small_ref.shape[0]
        cuts = [v.shape[1] // members for v in (up0, up1)]
        segments = [
            v[:, m * cut : (m + 1) * cut] for m in range(members) for v, cut in zip((up0, up1), cuts)
        ]
        per = width // sum(cuts)
        for i in range(members // per):
            sum_ref[8 + i : 9 + i] = jnp.concatenate(segments[2 * per * i : 2 * per * (i + 1)], axis=1)
        for target, source, place, count in (
            (5, after, 2, 1), (6, after, 0, 2), (12, after, 3, 1), (13, states, 0, 4), (17, after, 4, 1)
        ):
            sum_ref[target : target + count] = source[place : place + count]
        load_pieces(me_ref[0], pieces, w_ref, sems, False)

    gain = vec(small_ref, "g1")
    e = dot_tt(jnp.concatenate([g[0] for g in grads], axis=0), w_ref[...])
    n, r = norm_parts(x_ref[...].astype(F32))
    eg = e * gain
    part = r * (
        eg - jnp.mean(eg, axis=-1, keepdims=True) - n * jnp.mean(eg * n, axis=-1, keepdims=True)
    )
    sum_ref[0:1] += jnp.sum(e * n, axis=0, keepdims=True)
    sum_ref[1:2] += jnp.sum(e, axis=0, keepdims=True)
    ring_put(ring, pl.multiple_of(step * rows, rows), gh_ref[...] + part)

    @pl.when(step == pl.num_programs(1) - 1)
    def _():
        gx_ref[...] = ring_get(ring, length - shift_ref[seq], length)


def first_back_call(me, shift, grads, x, gh, small, pieces, smalls, deps):
    tokens, width = x.shape
    nseq, _, length = grads[0].shape
    steps = 4
    rows = length // steps
    row = pl.BlockSpec((rows, width), lambda s, i: (s * steps + i, 0))
    return pl.pallas_call(
        lambda *refs: first_back_kernel(len(grads), len(deps), *refs),
        grid=(nseq, steps),
        in_specs=[
            SMEM, SMEM, row, row, whole(small.shape),
            *(pl.BlockSpec((1, g.shape[1], rows), lambda s, i: (s, 0, i)) for g in grads), *(whole(v.shape) for v in smalls),
            *(ANY for _ in (*pieces, *deps)),
        ],
        out_specs=[pl.BlockSpec((length, width), lambda s, i: (s, 0)), whole((24, width))],
        out_shape=[
            jax.ShapeDtypeStruct((tokens, width), F32),
            jax.ShapeDtypeStruct((24, width), F32),
        ],
        scratch_shapes=[
            ring_shape(length, width),
            pltpu.VMEM((width, 3 * width), BF),
            pltpu.SemaphoreType.DMA((len(pieces),)),
        ],
        compiler_params=params(62),
        cost_estimate=cost(20),
        name="first_back",
    )(me, shift, x, gh, small, *grads, *smalls, *pieces, *deps)


def states_kernel(mix_ref, e_ref, c_ref, part_ref, sum_ref):
    @pl.when(pl.program_id(0) == 0)
    def _():
        sum_ref[...] = jnp.zeros_like(sum_ref)

    cot = c_ref[...].astype(F32)
    total = None
    for j in range(e_ref.shape[0]):
        e = e_ref[j].astype(F32)
        term = mix_ref[j] * e
        total = term if total is None else total + term
        sum_ref[j : j + 1] += jnp.sum(e * cot, axis=0, keepdims=True)
    part_ref[...] = total


def states_call(mix, earlier, cot):
    states, tokens, width = earlier.shape
    rows = 256
    row = pl.BlockSpec((rows, width), lambda i: (i, 0))
    stack = pl.BlockSpec((states, rows, width), lambda i: (0, i, 0))
    return pl.pallas_call(
        states_kernel,
        grid=(tokens // rows,),
        in_specs=[SMEM, stack, row],
        out_specs=[row, whole((8, width))],
        out_shape=[
            jax.ShapeDtypeStruct((tokens, width), F32),
            jax.ShapeDtypeStruct((8, width), F32),
        ],
        compiler_params=params(62),
        cost_estimate=cost(11),
        name="states",
    )(mix, earlier, cot)


def spread_kernel(mix_ref, c_ref, *refs):
    out = refs[-1]
    cot = c_ref[...].astype(F32)
    for j in range(out.shape[0]):
        out[j] = mix_ref[j] * cot


def spread_call(states, mix, cot, deps):
    tokens, width = cot.shape
    rows = 256
    return pl.pallas_call(
        spread_kernel,
        grid=(tokens // rows,),
        in_specs=[SMEM, pl.BlockSpec((rows, width), lambda i: (i, 0)), *(ANY for _ in deps)],
        out_specs=pl.BlockSpec((states, rows, width), lambda i: (0, i, 0)),
        out_shape=jax.ShapeDtypeStruct((states, tokens, width), F32),
        compiler_params=params(62),
        cost_estimate=cost(20),
        name="spread",
    )(mix, cot, *deps)


def rows_kernel(*refs):
    out = refs[-1]
    out[...] = jnp.zeros_like(out)
    for i, ref in enumerate(refs[:-1]):
        out[i : i + 1, : ref.shape[0]] = ref[...].astype(F32).reshape(1, -1).astype(BF)


def rows_call(vectors, wide):
    return pl.pallas_call(
        rows_kernel,
        out_shape=jax.ShapeDtypeStruct((len(vectors), wide), BF),
        cost_estimate=cost(1),
        name="rows",
    )(*vectors)


def split_kernel(members, shares, wo_ref, wu_ref, wd_ref, *refs):
    outs = refs[-5:]
    outs[0][...] = wo_ref[...]
    deep = wu_ref.shape[1] // members
    base = 0
    for i, share in enumerate(shares):
        for m in range(members):
            outs[1 + i][:, m * share : (m + 1) * share] = wu_ref[:, m * deep + base : m * deep + base + share]
        outs[3 + i][...] = wd_ref[base : base + share]
        base += share


def split_call(members, shares, wo, wu, wd, deps):
    own = wu.shape[0]
    width = wd.shape[1]
    low = [(own, width), *((own, members * v) for v in shares), *((v, width) for v in shares)]
    full = pl.BlockSpec(memory_space=pltpu.VMEM)
    return pl.pallas_call(
        lambda *refs: split_kernel(members, shares, *refs),
        in_specs=[full, full, full, *(ANY for _ in deps)],
        out_specs=[full] * 5,
        out_shape=[jax.ShapeDtypeStruct(shape, BF) for shape in low],
        compiler_params=params(62),
        cost_estimate=cost(3),
        name="split",
    )(wo, wu, wd, *deps)


def mix_kernel(shift_ref, mix_ref, part_ref, b_ref, *refs):
    out_ref, ring = refs[-2:]
    length = b_ref.shape[0]
    ring_put(ring, 0, b_ref[...])
    rolled = ring_get(ring, length - shift_ref[pl.program_id(0)], length)
    out_ref[...] = (part_ref[...] + mix_ref[4] * rolled).astype(BF)


def mix_call(shift, mix, part, block_out, deps):
    tokens, width = part.shape
    nseq = shift.shape[0]
    length = tokens // nseq
    row = pl.BlockSpec((length, width), lambda s: (s, 0))
    return pl.pallas_call(
        mix_kernel,
        grid=(nseq,),
        in_specs=[SMEM, SMEM, row, row, *(ANY for _ in deps)],
        out_specs=row,
        out_shape=jax.ShapeDtypeStruct((tokens, width), BF),
        scratch_shapes=[ring_shape(length, width)],
        compiler_params=params(62),
        cost_estimate=cost(20),
        name="mix",
    )(shift, mix, part, block_out, *deps)


def swap(v, axis, bits):
    size = lax.axis_size(axis)
    return lax.ppermute(v, axis, [(i, i ^ bits) for i in range(size)])


def gate(arrays, deps):
    count = len(arrays)
    return pl.pallas_call(
        lambda *refs: None,
        in_specs=[ANY] * (count + len(deps)),
        out_specs=[ANY] * count,
        out_shape=[jax.ShapeDtypeStruct(v.shape, v.dtype) for v in arrays],
        input_output_aliases={i: i for i in range(count)},
        cost_estimate=cost(0.3),
        name="gate",
    )(*arrays, *deps)


def far_pieces(v):
    return [v, *(swap(v, "shard", 2 * k) for k in range(1, lax.axis_size("shard") // 2))]


def near_pieces(far, own=None):
    pieces = []
    for k, v in enumerate(far):
        pieces += [v, own if own is not None and k == 0 else swap(v, "shard", 1)]
    return pieces


def in_order(pieces, mine):
    stack = jnp.stack(pieces)
    return [lax.dynamic_index_in_dim(stack, j ^ mine, 0, keepdims=False) for j in range(len(pieces))]


def total_of(terms):
    total = terms[0].astype(F32)
    for term in terms[1:]:
        total = total + term.astype(F32)
    return total


def chain_start(pair):
    keep, send = pair
    return {"keep": keep, "near": swap(send, "shard", 1)}


def step_parts(kind, chain):
    if kind == "small":

        def body(idx, ins, outs):
            outs[0][...] = ins[0][...] + ins[1][...]

        return [(v, whole(v.shape)) for v in (chain["sum"], chain["got"])], [(*chain["sum"].shape, F32)], body
    keep, near = chain["keep"], chain["near"]
    chips, sides, groups, n, lanes = keep.shape
    half = (groups, n, lanes)

    def at(side):
        spec = pl.BlockSpec((1, 1, *half), lambda i, idx: (idx[0], side(idx), 0, 0, 0))
        deep = pl.BlockSpec((1, *half), lambda i, idx: (side(idx), 0, 0, 0))
        return [(keep, spec), (near, spec), *((far, deep) for far in chain["far"])]

    def total(refs, group):
        out = None
        for ref in refs:
            piece = ref[(0,) * (len(ref.shape) - 3) + (group,)].astype(F32)
            out = piece if out is None else out + piece
        return out

    if kind == "x":
        ins = []
        for k in range(1, chips):
            spec = pl.BlockSpec((1, sides, *half), lambda i, idx, k=k: (idx[0] ^ k, 0, 0, 0, 0))
            ins += [(keep, spec), (near, spec)]

        def body(idx, ins, outs):
            for k, out in enumerate(outs):
                out[...] = (ins[2 * k][0].astype(F32) + ins[2 * k + 1][0].astype(F32)).astype(BF)

        return ins, [(sides, *half)] * (chips - 1), body
    if kind == "y":

        def body(idx, ins, outs):
            for g in range(groups):
                outs[0][g] = total(ins, g).astype(BF)

        return at(lambda idx: 1 - idx[1]), [half], body
    if kind == "half":
        ins = [(v, whole(v.shape)) for v in (chain["done"], *chain["zg"])]

        def body(idx, ins, outs):
            for k, ref in enumerate(ins):
                outs[0][idx[2] ^ k] = ref[...]

        return ins, [half], body
    if kind == "z":

        def body(idx, ins, outs):
            for k in range(groups):
                outs[k][...] = total(ins, idx[2] ^ k).astype(outs[k].dtype)

        return [*at(lambda idx: idx[1]), (chain["yr"], whole(half))], [(n, lanes, F32), *[(n, lanes)] * (groups - 1)], body

    def body(idx, ins, outs):
        out = ins[0][...]
        for ref in ins[1:]:
            out = out + ref[...].astype(F32)
        outs[0][...] = out.astype(BF)

    return [(v, whole(v.shape)) for v in (chain["mine"], *chain["zr"])], [(n, lanes)], body


def step_call(idx, steps, deps, us=3):
    plans = [step_parts(kind, chain) for kind, chain in steps]
    ins = [pair for plan in plans for pair in plan[0]]
    outs = [shape for plan in plans for shape in plan[1]]
    types = [F32 if shape[-1] == F32 else BF for shape in outs]
    outs = [shape[:-1] if shape[-1] == F32 else shape for shape in outs]

    def kernel(idx_ref, *refs):
        at, out_at = 0, len(ins) + len(deps)
        for some, shapes, body in plans:
            body(idx_ref, refs[at : at + len(some)], refs[out_at : out_at + len(shapes)])
            at += len(some)
            out_at += len(shapes)

    results = pl.pallas_call(
        kernel,
        grid_spec=pltpu.PrefetchScalarGridSpec(
            num_scalar_prefetch=1,
            grid=(1,),
            in_specs=[*(spec for _, spec in ins), *(ANY for _ in deps)],
            out_specs=[whole(shape) for shape in outs],
        ),
        out_shape=[jax.ShapeDtypeStruct(shape, dtype) for shape, dtype in zip(outs, types)],
        compiler_params=params(62),
        cost_estimate=cost(us),
        name="_".join(["step", *(kind for kind, _ in steps)]),
    )(idx, *(v for v, _ in ins), *deps)
    at = 0
    others = range(1, lax.axis_size("rep") // 2)
    for (kind, chain), (_, shapes, _) in zip(steps, plans):
        sends = results[at : at + len(shapes)]
        at += len(shapes)
        if kind == "x":
            chain["far"] = [swap(v, "shard", 2 * (k + 1)) for k, v in enumerate(sends)]
        elif kind == "y":
            chain["yr"] = swap(sends[0], "rep", 1)
        elif kind == "z":
            chain["mine"] = sends[0]
            chain["zr"] = [swap(sends[k], "rep", 2 * k) for k in others]
        elif kind == "sum":
            chain["done"] = sends[0]
            chain["zg"] = [swap(sends[0], "rep", 2 * k) for k in others]
        elif kind == "half":
            chain["half"] = sends[0]
            chain["twin"] = swap(sends[0], "rep", 1)
        else:
            small_next(chain, sends[0])
    return results[0]


def small_next(chain, sums):
    chain["sum"] = sums
    count = chain["steps"] = chain.get("steps", -1) + 1
    bits = [("shard", 1 << b) for b in range(lax.axis_size("shard").bit_length() - 1)] + [("rep", 1)]
    if count < len(bits):
        chain["got"] = swap(sums, *bits[count])
    else:
        chain["got"] = [swap(sums, "rep", 2 * k) for k in range(1, lax.axis_size("rep") // 2)]


def small_end(chain, group):
    return total_of(in_order([chain["sum"], *chain["got"]], group))


def finish_call(idx, chains, plans, shapes, deps, us=4):
    ins = [v for chain in chains for v in (chain["half"], chain["twin"])]

    def kernel(idx_ref, *refs):
        outs = refs[len(ins) + len(deps) : len(ins) + len(deps) + len(shapes)]
        scratch = refs[-len(chains) :]
        for c, plan in enumerate(plans):
            both = scratch[c]
            both[idx_ref[1]] = refs[2 * c][...]
            both[1 - idx_ref[1]] = refs[2 * c + 1][...]
            sides, groups = both.shape[:2]
            at = 0
            for out, own, cols, place in plan:
                rows, wide = own // groups, cols // sides
                for j in range(wide // 128):
                    for side in range(sides):
                        for group in range(groups):
                            row, col = place(group * rows, side * wide + j * 128)
                            outs[out][row : row + rows, col : col + 128] = both[
                                side, group, at : at + rows, :
                            ].astype(F32)
                    at += rows

    return pl.pallas_call(
        kernel,
        in_specs=[SMEM, *(pl.BlockSpec(memory_space=pltpu.VMEM) for _ in ins), *(ANY for _ in deps)],
        out_specs=[pl.BlockSpec(memory_space=pltpu.VMEM) for _ in shapes],
        out_shape=[jax.ShapeDtypeStruct(shape, F32) for shape in shapes],
        scratch_shapes=[pltpu.VMEM((2, *chain["half"].shape), BF) for chain in chains],
        compiler_params=params(62),
        cost_estimate=cost(us),
        name="finish",
    )(idx, *ins, *deps)


def reduce_plain(packed):
    flat = packed.reshape(-1, 128)
    return lax.psum(lax.psum_scatter(flat, "shard", scatter_dimension=0, tiled=True), "rep")[None, None]


def reduce_small(v):
    for axis in ("shard", "rep"):
        bits = 1
        while bits < lax.axis_size(axis):
            v = v + swap(v, axis, bits)
            bits *= 2
    return v


def shards(
    inputs, earlier, segments, cotangent, mix_weights,
    ln1_gain, ln1_bias, qkv_weight, qkv_bias, out_weight, out_bias,
    ln2_gain, ln2_bias, up_weight, up_bias, down_weight, down_bias,
):
    nseq, length = segments.shape
    width = inputs.shape[1]
    blk = length // 2
    members, replicas = lax.axis_size("shard"), lax.axis_size("rep")
    me = lax.axis_index("shard").astype(jnp.int32)
    rep = lax.axis_index("rep").astype(jnp.int32)
    side = rep % 2
    me_ref = me[None]
    idx = jnp.stack([me // 2, side, rep // 2])
    own = width // members
    deep = down_weight.shape[0]
    ff = deep * members
    shares = [deep // 2, deep - deep // 2]
    fits = own % (8 * replicas) == 0 and all(v % (8 * replicas) == 0 and v % 128 == 0 for v in shares)
    form = (2, replicas // 2) if fits else (1, 1)

    wqkv = far_pieces(qkv_weight)
    wqkv_near = swap(qkv_weight, "shard", 1)
    vectors = [ln1_gain, ln1_bias, qkv_bias, out_bias, ln2_gain, ln2_bias, up_bias, down_bias]
    sizes = [v.shape[0] for v in vectors]
    wide = max(sizes)
    small = rows_call(vectors, wide)
    small = [small, *(swap(small, "shard", k) for k in range(1, members))]
    small = jnp.stack(in_order(small, me))

    part, sums3 = states_call(mix_weights, earlier, cotangent)
    inv = np.exp(np.arange(HEAD // 2) * (-math.log(10000.0) / (HEAD // 2)))
    angles = np.arange(length)[None, :] * inv[:, None]
    tables = jnp.asarray(np.stack([np.cos(angles), np.sin(angles)]), F32)
    shift, xr, cr, act, seg, cos, sin = roll_call(inputs, cotangent, segments, small, tables, [sums3])
    if any(v % 128 for v in (deep, *shares)):

        def shared(v):
            halves = jnp.split(v.reshape(v.shape[0], members, deep), [shares[0]], axis=-1)
            return [h.reshape(v.shape[0], -1) for h in halves]

        pieces = [out_weight, *shared(up_weight), down_weight[: shares[0]], down_weight[shares[0] :]]
    else:
        pieces = split_call(members, shares, out_weight, up_weight, down_weight, [act, *wqkv])
    wo, wo_near = far_pieces(pieces[0]), swap(pieces[0], "shard", 1)
    wd0, wd0_near = far_pieces(pieces[3]), swap(pieces[3], "shard", 1)
    wu0, wu0_near = far_pieces(pieces[1]), swap(pieces[1], "shard", 1)

    wqkv = near_pieces([qkv_weight, *gate(wqkv[1:], [act])], wqkv_near)
    qkv = qkv_call(me_ref, act, small, cos, sin, wqkv)
    o, lse = attend_call(seg, qkv)
    firsts = [(wo, wo_near), (wu0, wu0_near), (wd0, wd0_near)]
    count = len(wo) - 1
    far = gate([piece for pieces_of, _ in firsts for piece in pieces_of[1:]] + [pieces[2], pieces[4]], [lse])
    wo, wu0, wd0 = [
        near_pieces([pieces_of[0], *far[i * count : (i + 1) * count]], own)
        for i, (pieces_of, own) in enumerate(firsts)
    ]
    wu1, wd1 = [far_pieces(v) for v in far[-2:]]
    values = {"me": me_ref, "mix": mix_weights, "small": small, "x": xr, "cot": cr, "a": o, "wo": wo}
    got = mlp_call(0, shares[0], True, False, values | {"wu": wu0, "wd": wd0}, form, members, [])
    values |= {"up_in": got["up"], "back_in": got["back"], "hid": got["hid"], "act": got["act"]}
    far = gate([*wu1, *wd1], [got["dbu"]])
    wu1, wd1 = near_pieces(far[: count + 1]), near_pieces(far[count + 1 :])
    first, dbu = [got[name] for name in ("dw0", "dw1") if name in got], [got["dbu"]]
    spread = [earlier.shape[0], mix_weights, cotangent]
    if fits:
        early = chain_start(first)
        earlier_grad = spread_call(*spread, [first[0]])
        deps = [step_call(idx, [("x", early)], [earlier_grad])]
    else:
        earlier_grad, deps = spread_call(*spread, []), []
    got = mlp_call(
        shares[0], shares[1], False, True, values | {"wu": wu1, "wd": wd1}, form, members, deps
    )
    second = [got[name] for name in ("dw0", "dw1") if name in got]
    dbu.append(got["dbu"])
    block_out, gh, ga, sums2 = (got[name] for name in ("up", "gh", "ga", "sum"))

    groups = width // PAIR // 2
    back = [seg, qkv, o, ga, lse, cos, sin]

    def up_place(base, share):
        def place(row, col):
            return row, col // share * deep + base + col % share

        return place

    if fits:
        late = chain_start(second)
        t = step_call(idx, [("y", early)], [late["keep"]])
        gs = [attend_back_call(*back, 0, 2, [t])]
        t = step_call(idx, [("z", early), ("x", late)], [gs[0][0]])
        gs.append(attend_back_call(*back, 2, 2, [t]))
        t = step_call(idx, [("sum", early)], [gs[1][0]])
        for i in range(2, groups):
            gs.append(attend_back_call(*back, 2 * i, 2, [t, gs[-1][0]], 0.5))
        early["zg"] = gate(early["zg"], [gs[-1][0]])
        t = step_call(idx, [("y", late)], [gs[-1][0]])
        smalls = [*(g[3] for g in gs), sums2, *dbu, sums3]
        grads = [g[i] for i in range(3) for g in gs]
        pack = qkv_grad_call(me_ref, grads, act, form, members, [t])
        tail = chain_start(pack)
        t = step_call(idx, [("half", early), ("z", late)], [pack[0]], 20)
        t = step_call(idx, [("x", tail)], [t])
        output = mix_call(shift, mix_weights, part, block_out, [t])
        t = step_call(idx, [("sum", late)], [output])
        input_grad, sums = first_back_call(me_ref, shift, grads, xr, gh, small, wqkv, smalls, [t])
        early["twin"], *late["zg"] = gate([early["twin"], *late["zg"]], [sums])
        sums_chain = {}
        small_next(sums_chain, sums)
        t = step_call(idx, [("y", tail)], [sums, early["twin"]])
        t = step_call(idx, [("half", late), ("z", tail), ("small", sums_chain)], [])
        t = step_call(idx, [("sum", tail), ("small", sums_chain)], [])
        d_up, d_down, d_out = finish_call(
            idx,
            [early, late],
            [
                [
                    (0, own, shares[0] * members, up_place(0, shares[0])),
                    (1, shares[0], width, lambda row, col: (row, col)),
                ],
                [
                    (0, own, shares[1] * members, up_place(shares[0], shares[1])),
                    (1, shares[1], width, lambda row, col: (row + shares[0], col)),
                    (2, own, width, lambda row, col: (row, col)),
                ],
            ],
            [(own, ff), (deep, width), (own, width)],
            [t],
        )
        t = step_call(idx, [("half", tail)], [d_out])
        step_call(idx, [("small", sums_chain)], [t])
        (d_qkv,) = finish_call(
            idx, [tail], [[(0, own, 3 * width, lambda row, col: (row, col))]], [(own, 3 * width)], [], 0.01
        )
        sums_chain["got"] = gate(sums_chain["got"], [d_qkv])
        flat = small_end(sums_chain, rep // 2).reshape(-1)
    else:
        gs = [attend_back_call(*back, 2 * i, 2, []) for i in range(groups)]
        smalls = [*(g[3] for g in gs), sums2, *dbu, sums3]
        grads = [g[i] for i in range(3) for g in gs]
        pack = qkv_grad_call(me_ref, grads, act, form, members, [])
        output = mix_call(shift, mix_weights, part, block_out, [])
        input_grad, sums = first_back_call(me_ref, shift, grads, xr, gh, small, wqkv, smalls, [])
        ups, downs = [], []
        first, second, third = [reduce_plain(p[0]) for p in (first, second, pack)]
        for v, share in ((first, shares[0]), (second, shares[1])):
            at = packed_rows(own, share * members, *v.shape[:2])
            ups.append(unpack(v, 0, own, share * members).reshape(own, members, share))
            downs.append(unpack(v, at, share, width))
            at += packed_rows(share, width, *v.shape[:2])
        d_out = unpack(second, at, own, width).astype(F32)
        d_up = jnp.concatenate(ups, axis=2).reshape(own, -1).astype(F32)
        d_down = jnp.concatenate(downs, axis=0).astype(F32)
        d_qkv = unpack(third, 0, own, 3 * width).astype(F32)
        flat = reduce_small(sums).reshape(-1)

    parts, at = [], 0
    for size in sizes:
        parts.append(lax.dynamic_slice(flat, (at + me * size,), (size,)))
        at += size * members
    mix_grad = jnp.sum(flat[at : at + 5 * width].reshape(5, width), axis=1)
    return (
        output, input_grad, earlier_grad, mix_grad,
        parts[0], parts[1], d_qkv, parts[2], d_out, parts[3], parts[4], parts[5],
        d_up, parts[6], d_down, parts[7],
    )


def solution(mesh):
    rows, shard = P(("rep", "shard"), None), P("shard")
    mat, deep = P("shard", None), P(None, ("rep", "shard"), None)
    return jax.shard_map(
        shards,
        mesh=mesh,
        in_specs=(
            rows, deep, rows, rows, P(),
            shard, shard, mat, shard, mat, shard, shard, shard, mat, shard, mat, shard,
        ),
        out_specs=(
            rows, rows, deep, P(),
            shard, shard, mat, shard, mat, shard, shard, shard, mat, shard, mat, shard,
        ),
        check_vma=False,
    )
```
